128 devices in a mesh: ctx: 16 (over x, y), mp: 8 (over z, core).
Axes of the slice: x: 4, y: 4, z: 4, core: 2. Of those that a mesh axis runs over, the one named last changes fastest.
Arguments:
- tokens: bfloat16 [8192, 8192], P('ctx', 'mp'), may hold values from -12 to 12
- norm_gain: bfloat16 [8192], replicated, may hold values from 0.099609375 to 1.8984375
- router_weight: bfloat16 [8192], replicated, may hold values from -0.0625 to 0.0625
- query_weight: bfloat16 [8192, 4096], P('ctx', 'mp'), may hold values from -2 to 2
- key_weight: bfloat16 [8192, 1024], P('ctx', 'mp'), may hold values from -1 to 1
- value_weight: bfloat16 [8192, 1024], P('ctx', 'mp'), may hold values from -0.0625 to 0.0625
- out_weight: bfloat16 [4096, 8192], P('mp', 'ctx'), may hold values from -0.1875 to 0.1875
- mlp_gain: bfloat16 [8192], P('mp'), may hold values from 0.099609375 to 1.8984375
- gate_weight: bfloat16 [8192, 28672], P('mp', 'ctx'), may hold values from -0.0625 to 0.0625
- up_weight: bfloat16 [8192, 28672], P('mp', 'ctx'), may hold values from -0.0625 to 0.0625
- down_weight: bfloat16 [28672, 8192], P('ctx', 'mp'), may hold values from -0.0625 to 0.0625
- destination: int32 [8192], P('ctx'), may hold values from -1 to 1023, as said below
- kept_pos: int32 [1024], P('ctx'), may hold values from 0 to 8191, as said below
Outputs:
- layer_out: bfloat16 [8192, 8192], P('ctx', 'mp')
The draws below stay inside these ranges and needn't reach their ends.
Inputs may be any that keep to these rules, and one draw needn't show every extreme that they name: A token that skips the block has -1. The kept tokens, counted in sequence order as k = 0, 1, ..., 1023, have destination (k mod 16) * 64 + (k div 16): owner k mod 16, slot k div 16 of that owner. Each shard of 512 tokens keeps from 32 to 96 tokens, and in every draw some shard keeps exactly 96; so at most 6 kept tokens of one shard have one owner, and that most is reached in every draw. kept_pos[destination[t]] = t for every kept token t.
All inputs are finite; a program needn't handle non-finite values.
Results may differ from the reference program's by a relative error of at most 0.0055.
Values may be sent and summed in bfloat16 or wider, within the bound.
A program may use at most 128 MiB of HBM per device.

```python
import jax
import jax.numpy as jnp
from jax import lax

D = 8192
FF = 28672
HEADS = 32
KV_HEADS = 8
HEAD_DIM = 128
TOK_DEV = 512
TOKENS = 8192
KEPT_DEV = 64
KEPT = 1024


def kept_layout(key):
    shard_count = TOKENS // TOK_DEV
    pair_count = shard_count // 2
    spread_rows = KEPT_DEV // 2
    key_offset, key_forced, key_sign, key_order = jax.random.split(jax.random.fold_in(key, 41), 4)
    offsets = jax.random.randint(key_offset, (pair_count,), -spread_rows, spread_rows + 1)
    forced = jax.random.randint(key_forced, (), 0, pair_count)
    sign_value = 2 * jax.random.randint(key_sign, (), 0, 2) - 1
    offsets = jnp.where(jnp.arange(pair_count) == forced, spread_rows * sign_value, offsets)
    counts = jnp.concatenate([KEPT_DEV + offsets, (KEPT_DEV - offsets)[::-1]])
    orders = jax.vmap(lambda subkey: jax.random.permutation(subkey, TOK_DEV))(jax.random.split(key_order, shard_count))
    is_kept = (orders < counts[:, None]).reshape(-1)
    kept_rank = jnp.cumsum(is_kept.astype(jnp.int32)) - 1
    destination = jnp.where(is_kept, kept_rank % shard_count * KEPT_DEV + kept_rank // shard_count, -1).astype(jnp.int32)
    targets = jnp.where(is_kept, destination, KEPT).astype(jnp.int32)
    kept_pos = jnp.zeros((KEPT,), jnp.int32).at[targets].set(jnp.arange(TOKENS, dtype=jnp.int32), mode='drop')
    rank_slots = jnp.where(is_kept, kept_rank, KEPT).astype(jnp.int32)
    ranked = jnp.zeros((KEPT,), jnp.int32).at[rank_slots].set(jnp.arange(TOKENS, dtype=jnp.int32), mode='drop')
    return (destination, kept_pos, ranked)


def plant_sign(key):
    coins = jax.random.randint(jax.random.fold_in(key, 53), (D,), 0, 2)
    return (2 * coins - 1).astype(jnp.float32)


def plant_mask(width):
    within = jnp.arange(width, dtype=jnp.int32) % HEAD_DIM
    half_dim = HEAD_DIM // 2
    return (within % half_dim >= half_dim - 2).astype(jnp.float32)


def drawn_weight(key, salt, width, spread):
    base = jnp.clip(jax.random.normal(jax.random.fold_in(key, salt), (D, width), jnp.float32), -4.0, 4.0) * spread
    lift = jnp.sqrt(80.0) * HEAD_DIM ** 0.25 / D
    return (base + lift * plant_sign(key)[:, None] * plant_mask(width)[None, :]).astype(jnp.bfloat16)


def draw_destination(key, part):
    return kept_layout(key)[0]


def draw_kept_pos(key, part):
    return kept_layout(key)[1]


def draw_query_weight(key, part):
    return drawn_weight(key, 73, HEADS * HEAD_DIM, (D // 16) ** (-0.5))


def draw_key_weight(key, part):
    return drawn_weight(key, 79, KV_HEADS * HEAD_DIM, D ** (-0.5))


def draw_tokens(key, part):
    ranked = kept_layout(key)[2]
    noise_key = jax.random.fold_in(key, 61)
    ramp = jnp.arange(D, dtype=jnp.float32) / max(D - 1, 1)
    noise = jnp.clip(jax.random.normal(noise_key, (TOKENS, D), jnp.float32), -3.5, 3.5)
    column_scale = jnp.power(2.25, ramp)
    planted = jnp.arange(8, dtype=jnp.int32)
    planted_ranks = (planted + 1) * KEPT // 9
    strengths = 0.5 + 0.15 * (planted // 2).astype(jnp.float32)
    strength = jnp.zeros((TOKENS,), jnp.float32).at[ranked[planted_ranks]].set(strengths)
    lifted = strength[:, None] * plant_sign(key)[None, :] + jnp.sqrt(1.0 - strength * strength)[:, None] * noise
    return (lifted * column_scale[None, :]).astype(jnp.bfloat16)


def block_scale(rng, extent, pieces, least, top_value):
    level = 1.0
    for dim, blocks in pieces:
        heights = jax.random.uniform(jax.random.fold_in(jax.random.fold_in(rng, 6), dim), (blocks,), jnp.float32, least / len(pieces), top_value / len(pieces))
        level = level * jnp.repeat(jnp.exp(heights), extent[dim] // blocks).reshape((-1,) + (1,) * (len(extent) - 1 - dim))
    return level


def centred(own_key, shape, deviation, reach, cuts=(), held_as=jnp.bfloat16):
    level = block_scale(own_key, shape, cuts, -0.22, 0.18) if cuts else 1.0
    drawn = jax.random.normal(own_key, shape, jnp.float32) * deviation * level
    return jnp.minimum(jnp.maximum(drawn, -reach), reach).astype(held_as)


def setup_inputs(seed: int = 0) -> dict:
    streams_of = jax.random.split(jax.random.key(seed), 14)
    return {
        "tokens": draw_tokens(jax.random.fold_in(streams_of[13], 71), 0),
        "norm_gain": jnp.clip(1.0 + 0.18 * jax.random.normal(streams_of[1], (D,), jnp.float32), 0.099609375, 1.8984375).astype(jnp.bfloat16),
        "router_weight": centred(streams_of[2], (D,), D ** -0.5, 0.0625),
        "query_weight": draw_query_weight(jax.random.fold_in(streams_of[13], 71), 0),
        "key_weight": draw_key_weight(jax.random.fold_in(streams_of[13], 71), 0),
        "value_weight": centred(streams_of[5], (D, KV_HEADS * HEAD_DIM), D ** -0.5, 0.0625, ((0, 16), (1, 8))),
        "out_weight": centred(streams_of[6], (HEADS * HEAD_DIM, D), (HEADS * HEAD_DIM // 4) ** -0.5, 0.1875, ((0, 8), (1, 16))),
        "mlp_gain": jnp.clip(1.0 + 0.18 * jax.random.normal(streams_of[7], (D,), jnp.float32), 0.099609375, 1.8984375).astype(jnp.bfloat16),
        "gate_weight": centred(streams_of[8], (D, FF), D ** -0.5, 0.0625, ((0, 8), (1, 16))),
        "up_weight": centred(streams_of[9], (D, FF), D ** -0.5, 0.0625, ((0, 8), (1, 16))),
        "down_weight": centred(streams_of[10], (FF, D), (FF // 4) ** -0.5, 0.0625, ((0, 16), (1, 8))),
        "destination": draw_destination(jax.random.fold_in(streams_of[13], 71), 0),
        "kept_pos": draw_kept_pos(jax.random.fold_in(streams_of[13], 71), 0),
    }


def rotate(values, positions):
    half_dim = values.shape[-1] // 2
    exponent = jnp.arange(half_dim, dtype=jnp.float32) * (2.0 / values.shape[-1])
    frequency = 500000.0 ** (-exponent)
    angles = positions.astype(jnp.float32)[:, None] * frequency[None, :]
    cosine = jnp.cos(angles)[:, None, :]
    sine_part = jnp.sin(angles)[:, None, :]
    first_half = values[..., :half_dim]
    second_half = values[..., half_dim:]
    return jnp.concatenate([first_half * cosine - second_half * sine_part, second_half * cosine + first_half * sine_part], axis=-1)

def reference(tokens, norm_gain, router_weight, query_weight, key_weight, value_weight, out_weight, mlp_gain, gate_weight, up_weight, down_weight, destination, kept_pos):
    slot_count = kept_pos.shape[0]
    group_size = HEADS // KV_HEADS
    targets = jnp.where(destination >= 0, destination, slot_count).astype(jnp.int32)
    sources = jnp.zeros((slot_count,), jnp.int32).at[targets].set(jnp.arange(destination.shape[0], dtype=jnp.int32), mode='drop')
    gathered = tokens[sources]
    raw_rows = gathered.astype(jnp.float32)
    mean_square = lax.optimization_barrier(jnp.mean(raw_rows * raw_rows, axis=-1, keepdims=True))
    normed = (raw_rows * lax.rsqrt(mean_square + 1e-05) * norm_gain.astype(jnp.float32)).astype(jnp.bfloat16)
    router_score = jax.nn.sigmoid(jnp.dot(gathered, router_weight, preferred_element_type=jnp.float32))
    queries = jnp.dot(normed, query_weight, preferred_element_type=jnp.float32).reshape(slot_count, HEADS, HEAD_DIM)
    queries = rotate(queries, kept_pos).astype(jnp.bfloat16)
    keys_all = jnp.dot(normed, key_weight, preferred_element_type=jnp.float32).reshape(slot_count, KV_HEADS, HEAD_DIM)
    keys_all = rotate(keys_all, kept_pos).astype(jnp.bfloat16)
    values_all = jnp.dot(normed, value_weight, preferred_element_type=jnp.float32).reshape(slot_count, KV_HEADS, HEAD_DIM).astype(jnp.bfloat16)
    allowed = kept_pos[None, :] <= kept_pos[:, None]
    softmax_scale = HEAD_DIM ** (-0.5)

    def one_group(operands):
        group_queries, group_keys, group_values = operands
        scores = jnp.einsum('qgd,kd->gqk', group_queries.astype(jnp.float32), group_keys.astype(jnp.float32)) * softmax_scale
        scores = jnp.where(allowed[None], scores, -1e+30)
        row_peak = lax.optimization_barrier(jnp.max(scores, axis=-1, keepdims=True))
        weights = jnp.where(allowed[None], jnp.exp(scores - row_peak), 0.0)
        mixed = jnp.einsum('gqk,kd->qgd', weights, group_values.astype(jnp.float32))
        return mixed / lax.optimization_barrier(jnp.sum(weights, axis=-1)).transpose(1, 0)[..., None]
    grouped = queries.reshape(slot_count, KV_HEADS, group_size, HEAD_DIM).transpose(1, 0, 2, 3)
    attended = lax.map(one_group, (grouped, keys_all.transpose(1, 0, 2), values_all.transpose(1, 0, 2)))
    attended = attended.transpose(1, 0, 2, 3).reshape(slot_count, HEADS * HEAD_DIM).astype(jnp.bfloat16)
    head_delta = jnp.dot(attended, out_weight, preferred_element_type=jnp.float32)
    mixed_rows = raw_rows + head_delta
    second_square = lax.optimization_barrier(jnp.mean(mixed_rows * mixed_rows, axis=-1, keepdims=True))
    second_normed = (mixed_rows * lax.rsqrt(second_square + 1e-05) * mlp_gain.astype(jnp.float32)).astype(jnp.bfloat16)
    gate = jnp.dot(second_normed, gate_weight, preferred_element_type=jnp.float32)
    up_part = jnp.dot(second_normed, up_weight, preferred_element_type=jnp.float32)
    hidden = (jax.nn.silu(gate) * up_part).astype(jnp.bfloat16)
    mlp_delta = jnp.dot(hidden, down_weight, preferred_element_type=jnp.float32)
    update = (router_score[:, None] * (head_delta + mlp_delta)).astype(jnp.bfloat16)
    renewed = (raw_rows + update.astype(jnp.float32)).astype(jnp.bfloat16)
    return tokens.at[sources].set(renewed)
```

```python
import functools

import jax
import jax.numpy as jnp
from jax import lax
from jax.sharding import PartitionSpec as P

from jax.experimental import pallas as pl
from jax.experimental.pallas import tpu as pltpu

HEAD_DIM = 128
MESH = pl.DeviceIdType.MESH
EPS = 1e-05


def remote(source, target, sent, landed, device):
    return pltpu.make_async_remote_copy(
        src_ref=source,
        dst_ref=target,
        send_sem=sent,
        recv_sem=landed,
        device_id=device,
        device_id_type=MESH,
    )


def mlp_kernel(
    x_ref,
    inv_gain_ref,
    gate_ref,
    up_ref,
    down_ref,
    out_ref,
    own_x,
    sib_x,
    sib_gain,
    weight,
    down,
    part,
    sums,
    hidden,
    delta,
    deltas,
    load_sem,
    swap_send,
    swap_recv,
    x_send,
    x_recv,
    pass_send,
    pass_recv,
    sum_send,
    sum_recv,
    hid_send,
    hid_recv,
    hop_send,
    hop_recv,
    out_send,
    out_recv,
):
    rows, feats = x_ref.shape
    half = gate_ref.shape[1] // 2
    both = 2 * half
    group = 4 * rows
    c, m = lax.axis_index("ctx"), lax.axis_index("mp")
    x, y = c // 4, c % 4
    z, core = m // 2, m % 2
    sibling = (c, z * 2 + 1 - core)

    def peer(step):
        turn = step // 4
        shift = turn + (turn // 2) * (1 - 2 * (turn % 2))
        return lax.rem(x + 4 - shift, 4) * 4 + lax.rem(y + step % 4, 4)

    def z_peer(step):
        return lax.rem(z + step, 4)

    def group_of(turn):
        shift = turn + (turn // 2) * (1 - 2 * (turn % 2))
        return lax.rem(x + shift, 4)

    barrier = pltpu.get_barrier_semaphore()

    @pl.loop(1, 16)
    def _(k):
        pl.semaphore_signal(barrier, inc=1, device_id=(peer(k), m), device_id_type=MESH)

    for k in range(1, 4):
        pl.semaphore_signal(
            barrier, inc=1, device_id=(c, z_peer(k) * 2 + core), device_id_type=MESH
        )
    pl.semaphore_signal(barrier, inc=1, device_id=sibling, device_id_type=MESH)

    mine = pl.multiple_of(core * half, 128)
    others = pl.multiple_of((1 - core) * half, 128)
    loads = [
        pltpu.make_async_copy(
            gate_ref.at[:, pl.ds(mine, half)],
            weight.at[pl.ds(0, feats), pl.ds(0, half)],
            load_sem.at[0],
        ),
        pltpu.make_async_copy(
            up_ref.at[:, pl.ds(mine, half)],
            weight.at[pl.ds(0, feats), pl.ds(half, half)],
            load_sem.at[1],
        ),
        pltpu.make_async_copy(down_ref, down, load_sem.at[2]),
    ]
    for load in loads:
        load.start()
    my_rows = pl.ds(pl.multiple_of(c * rows, rows), rows)
    own_x[my_rows, :] = x_ref[...]
    pl.semaphore_wait(barrier, 19)

    def x_copy(who, device):
        place = pl.ds(pl.multiple_of(who * rows, rows), rows)
        return remote(own_x.at[place], own_x.at[place], x_send.at[who], x_recv.at[who], device)

    def x_out(k):
        return remote(
            own_x.at[my_rows], own_x.at[my_rows], x_send.at[k], x_recv.at[c], (peer(k), m)
        )

    def x_pass(who):
        place = pl.ds(pl.multiple_of(who * rows, rows), rows)
        return remote(
            own_x.at[place], sib_x.at[place], pass_send.at[who], pass_recv.at[who], sibling
        )

    @pl.loop(1, 4)
    def _(k):
        x_out(k).start()

    swaps = [
        remote(
            gate_ref.at[:, pl.ds(others, half)],
            weight.at[pl.ds(feats, feats), pl.ds(0, half)],
            swap_send.at[0],
            swap_recv.at[0],
            sibling,
        ),
        remote(
            up_ref.at[:, pl.ds(others, half)],
            weight.at[pl.ds(feats, feats), pl.ds(half, half)],
            swap_send.at[1],
            swap_recv.at[1],
            sibling,
        ),
        remote(inv_gain_ref, sib_gain, swap_send.at[2], swap_recv.at[2], sibling),
    ]
    x_pass(c).start()
    for swap in swaps:
        swap.start()

    @pl.loop(4, 16)
    def _(k):
        x_out(k).start()

    for load in loads:
        load.wait()
    for swap in swaps:
        swap.wait()

    def sum_out(turn, k):
        to = z_peer(k)
        return remote(
            part.at[turn, pl.ds(pl.multiple_of(to * rows, rows), rows)],
            sums.at[turn, z],
            sum_send.at[turn * 4 + k],
            sum_recv.at[turn * 4 + z],
            (c, to * 2 + core),
        )

    def sum_in(turn, k):
        at = z_peer(k)
        return remote(
            part.at[turn, pl.ds(0, rows)],
            sums.at[turn, at],
            sum_send.at[turn * 4 + k],
            sum_recv.at[turn * 4 + at],
            (c, at * 2 + core),
        )

    def hid_out(turn, k):
        return remote(
            hidden.at[turn, core, z],
            hidden.at[turn, core, z],
            hid_send.at[turn * 4 + k],
            hid_recv.at[turn * 4 + z],
            (c, z_peer(k) * 2 + core),
        )

    def hid_in(turn, k):
        at = z_peer(k)
        return remote(
            hidden.at[turn, core, at],
            hidden.at[turn, core, at],
            hid_send.at[turn * 4 + k],
            hid_recv.at[turn * 4 + at],
            (c, at * 2 + core),
        )

    def hid_pass(turn, at):
        return remote(
            hidden.at[turn, core, at],
            hidden.at[turn, core, at],
            hop_send.at[turn * 4 + at],
            hop_recv.at[turn * 4 + at],
            sibling,
        )

    def hid_passed(turn, at):
        return remote(
            hidden.at[turn, 1 - core, at],
            hidden.at[turn, 1 - core, at],
            hop_send.at[turn * 4 + at],
            hop_recv.at[turn * 4 + at],
            sibling,
        )

    def out_copy(who, slot):
        return remote(
            delta.at[pl.ds(pl.multiple_of(who * rows, rows), rows)],
            deltas.at[slot],
            out_send.at[who],
            out_recv.at[slot],
            (who, m),
        )

    def front(turn):
        g = group_of(turn)

        @pl.loop(0, 4)
        def _(k):
            who = g * 4 + lax.rem(y + 4 - k, 4)

            @pl.when(who != c)
            def _():
                x_copy(who, (who, m)).wait_recv()
                x_pass(who).start()

        @pl.loop(0, 4)
        def _(k):
            who = g * 4 + lax.rem(y + 4 - k, 4)
            x_pass(who).wait_recv()

        place = pl.ds(pl.multiple_of(g * group, group), group)
        mixed = own_x[place, :].astype(jnp.float32) * inv_gain_ref[0:1, :]
        square = jnp.sum(mixed * mixed, axis=1, keepdims=True)
        mixed = sib_x[place, :].astype(jnp.float32) * sib_gain[0:1, :]
        square = square + jnp.sum(mixed * mixed, axis=1, keepdims=True)
        square = jnp.broadcast_to(square, (group, 128))
        coarse = square.astype(jnp.bfloat16)
        fine = (square - coarse.astype(jnp.float32)).astype(jnp.bfloat16)
        lane = lax.broadcasted_iota(jnp.int32, (group, 128), 1)
        part[turn, :, pl.ds(both, 128)] = jnp.where(lane < 64, coarse, fine)

        @pl.loop(0, both // 256)
        def _(tile):
            cols = pl.ds(pl.multiple_of(tile * 256, 256), 256)
            total = jnp.dot(
                own_x[place, :], weight[pl.ds(0, feats), cols], preferred_element_type=jnp.float32
            )
            total += jnp.dot(
                sib_x[place, :],
                weight[pl.ds(feats, feats), cols],
                preferred_element_type=jnp.float32,
            )
            part[turn, :, cols] = total.astype(jnp.bfloat16)

        for k in (2, 1, 3):
            sum_out(turn, k).start()

    def middle(turn):
        total = part[turn, pl.ds(pl.multiple_of(z * rows, rows), rows), :].astype(jnp.float32)
        for k in range(1, 4):
            sum_in(turn, k).wait_recv()
            total += sums[turn, z_peer(k)].astype(jnp.float32)
        square = total[:, both : both + 1] + total[:, both + 64 : both + 65]
        scale = lax.rsqrt(square * (1.0 / (8 * feats)) + EPS)
        gate = total[:, :half] * scale
        up = total[:, half:both] * scale
        hidden[turn, core, z] = (gate / (1.0 + jnp.exp(-gate)) * up).astype(jnp.bfloat16)
        for k in (2, 1, 3):
            hid_out(turn, k).start()
        hid_pass(turn, z).start()

    def back(turn):
        for k in range(1, 4):
            hid_in(turn, k).wait_recv()
            hid_pass(turn, z_peer(k)).start()
        for k in range(4):
            hid_passed(turn, z_peer(k)).wait_recv()
        g = group_of(turn)
        place = pl.ds(pl.multiple_of(g * group, group), group)

        @pl.loop(0, feats // 256)
        def _(tile):
            cols = pl.ds(pl.multiple_of(tile * 256, 256), 256)
            total = jnp.dot(
                hidden[turn, 0].reshape(group, half),
                down[pl.ds(0, half), cols],
                preferred_element_type=jnp.float32,
            )
            total += jnp.dot(
                hidden[turn, 1].reshape(group, half),
                down[pl.ds(half, half), cols],
                preferred_element_type=jnp.float32,
            )
            delta[place, cols] = total.astype(jnp.bfloat16)

        @pl.loop(0, 4)
        def _(k):
            who = g * 4 + lax.rem(y + k, 4)

            @pl.when(who != c)
            def _():
                out_copy(who, c).start()

    @pl.loop(0, 6)
    def _(step):
        @pl.when(step < 4)
        def _():
            front(step)

        @pl.when((step >= 1) & (step < 5))
        def _():
            middle(step - 1)

        @pl.when(step >= 2)
        def _():
            back(step - 2)

    out_ref[...] = delta[my_rows, :].astype(jnp.float32)

    @pl.loop(1, 16)
    def _(k):
        who = peer(k)
        out_copy(who, who).wait_recv()
        out_ref[...] += deltas[who].astype(jnp.float32)

    @pl.loop(1, 16)
    def _(k):
        x_out(k).wait_send()
        out_copy(peer(k), c).wait_send()

    @pl.loop(0, 16)
    def _(who):
        x_pass(who).wait_send()

    @pl.loop(0, 4)
    def _(turn):
        for k in range(1, 4):
            sum_out(turn, k).wait_send()
            hid_out(turn, k).wait_send()
        for k in range(4):
            hid_pass(turn, z_peer(k)).wait_send()


def feed_forward(scaled, inv_gain, gate_weight, up_weight, down_weight):
    rows, feats = scaled.shape
    cols = gate_weight.shape[1]
    half = cols // 2
    dma = pltpu.SemaphoreType.DMA
    bf16 = jnp.bfloat16
    vmem, anywhere = pl.BlockSpec(memory_space=pltpu.VMEM), pl.BlockSpec(memory_space=pl.ANY)
    return pl.pallas_call(
        mlp_kernel,
        out_shape=jax.ShapeDtypeStruct((rows, feats), jnp.float32),
        in_specs=[vmem, vmem, anywhere, anywhere, anywhere],
        out_specs=vmem,
        scratch_shapes=[
            pltpu.VMEM((16 * rows, feats), bf16),
            pltpu.VMEM((16 * rows, feats), bf16),
            pltpu.VMEM((8, feats), jnp.float32),
            pltpu.VMEM((2 * feats, cols), bf16),
            pltpu.VMEM((cols, feats), bf16),
            pltpu.VMEM((4, 4 * rows, cols + 128), bf16),
            pltpu.VMEM((4, 4, rows, cols + 128), bf16),
            pltpu.VMEM((4, 2, 4, rows, half), bf16),
            pltpu.VMEM((16 * rows, feats), bf16),
            pltpu.VMEM((16, rows, feats), bf16),
            dma((3,)),
            dma((3,)),
            dma((3,)),
        ]
        + [dma((16,))] * 12,
        compiler_params=pltpu.CompilerParams(
            collective_id=3, has_side_effects=True, vmem_limit_bytes=56 * 2**20
        ),
        name="feed_forward",
    )(scaled, inv_gain, gate_weight, up_weight, down_weight)


def sent_to_all(shard, axis):
    count = lax.axis_size(axis)
    return lax.all_to_all(
        jnp.broadcast_to(shard[None], (count, *shard.shape)), axis, 0, 0, tiled=True
    )


def in_order(tiles, dim):
    tiles = jnp.moveaxis(tiles, 0, dim)
    dims = tiles.shape
    return tiles.reshape(*dims[:dim], dims[dim] * dims[dim + 1], *dims[dim + 2 :])


def collect(shard, axis, dim):
    tiles = sent_to_all(shard, axis)
    return in_order(tiles, dim)


def in_one_piece(arrays, axis, dim, along):
    both = jnp.concatenate(arrays, axis=along)
    result, at, done = (lax.all_gather(both, axis, axis=dim, tiled=True), 0, [])
    for a in arrays:
        done.append(lax.slice_in_dim(result, at, at + a.shape[along], axis=along))
        at += a.shape[along]
    return tuple(done)


def in_blocks(shard, dim, count):
    dims = shard.shape
    tiles = shard.reshape(*dims[:dim], count, dims[dim] // count, *dims[dim + 1 :])
    return jnp.moveaxis(tiles, dim, 0)


def sent_and_summed(shard, axis, dim):
    tiles = in_blocks(shard, dim, lax.axis_size(axis))
    arrived = lax.all_to_all(tiles, axis, split_axis=0, concat_axis=0, tiled=True)
    return arrived.astype(jnp.float32).sum(axis=0)


def taken_together(shard, axis):
    everything = sent_to_all(shard, axis)
    return jnp.sum(everything, axis=0)


def rotate(values, positions):
    half_dim = values.shape[-1] // 2
    exponent = jnp.arange(half_dim, dtype=jnp.float32) * (2.0 / values.shape[-1])
    frequency = 500000.0 ** (-exponent)
    angles = positions.astype(jnp.float32)[:, None] * frequency[None, :]
    cosine = jnp.cos(angles)[:, None, :]
    sine_part = jnp.sin(angles)[:, None, :]
    first_half = values[..., :half_dim]
    second_half = values[..., half_dim:]
    return jnp.concatenate(
        [
            first_half * cosine - second_half * sine_part,
            second_half * cosine + first_half * sine_part,
        ],
        axis=-1,
    )


def body(
    tokens,
    norm_gain,
    router_weight,
    query_weight,
    key_weight,
    value_weight,
    out_weight,
    mlp_gain,
    gate_weight,
    up_weight,
    down_weight,
    destination,
    kept_pos,
):
    ctx_count = lax.axis_size("ctx")
    mp_count = lax.axis_size("mp")
    my_index = lax.axis_index("ctx")
    tok_dev = tokens.shape[0]
    kept_dev = kept_pos.shape[0]
    feature_cols = tokens.shape[1]
    feature_total = feature_cols * mp_count
    capacity = (3 * kept_dev // 2 + ctx_count - 1) // ctx_count
    slots_all = ctx_count * capacity
    head_dim = HEAD_DIM
    query_cols = query_weight.shape[1]
    key_cols = key_weight.shape[1]
    kv_local = key_cols // head_dim
    q_local = query_cols // head_dim
    group_size = q_local // kv_local
    peer_ids = jnp.arange(ctx_count, dtype=jnp.int32)
    is_kept = destination >= 0
    owner_ids = destination // kept_dev
    slot_ids = destination % kept_dev
    kept_order = slot_ids * ctx_count + owner_ids
    first_order = jnp.min(jnp.where(is_kept, kept_order, ctx_count * kept_dev))
    first_slots = (first_order - peer_ids + ctx_count - 1) // ctx_count
    owner_match = owner_ids[:, None] == peer_ids[None, :]
    send_index = (
        owner_ids * capacity
        + slot_ids
        - jnp.sum(jnp.where(owner_match, first_slots[None, :], 0), axis=1)
    )
    send_index = jnp.where(is_kept, send_index, slots_all)
    token_ids = jnp.arange(tok_dev, dtype=jnp.int32)
    picked = jnp.full((slots_all,), tok_dev, jnp.int32).at[send_index].set(token_ids, mode="drop")
    outgoing = jnp.take(tokens, picked, axis=0, mode="fill", fill_value=0).reshape(
        ctx_count, capacity, feature_cols
    )
    incoming = lax.all_to_all(outgoing, "ctx", split_axis=0, concat_axis=0, tiled=True).reshape(
        slots_all, feature_cols
    )
    slot_range = jnp.arange(kept_dev, dtype=jnp.int32)
    source_ids = kept_pos // tok_dev
    source_match = source_ids[:, None] == peer_ids[None, :]
    first_from = jnp.min(jnp.where(source_match, slot_range[:, None], kept_dev), axis=0)
    recv_index = (
        source_ids * capacity
        + slot_range
        - jnp.sum(jnp.where(source_match, first_from[None, :], 0), axis=1)
    )
    local_rows = incoming[recv_index]
    full_rows = collect(local_rows, "mp", 1)
    raw_rows = full_rows.astype(jnp.float32)
    mean_square = jnp.mean(raw_rows * raw_rows, axis=-1, keepdims=True)
    normed = (raw_rows * lax.rsqrt(mean_square + 1e-05) * norm_gain.astype(jnp.float32)).astype(
        jnp.bfloat16
    )
    router_score = jax.nn.sigmoid(
        jnp.dot(full_rows, router_weight, preferred_element_type=jnp.float32)
    )
    pieces = in_one_piece((query_weight, key_weight, value_weight), "ctx", 0, 1)
    query_sum = jnp.dot(normed, pieces[0], preferred_element_type=jnp.float32)
    key_sum = jnp.dot(normed, pieces[1], preferred_element_type=jnp.float32)
    value_sum = jnp.dot(normed, pieces[2], preferred_element_type=jnp.float32)
    queries = rotate(query_sum.reshape(kept_dev, q_local, head_dim), kept_pos).astype(jnp.bfloat16)
    queries = queries.reshape(kept_dev, kv_local, group_size, head_dim)
    key_rows = (
        rotate(key_sum.reshape(kept_dev, kv_local, head_dim), kept_pos)
        .astype(jnp.bfloat16)
        .reshape(kept_dev, key_cols)
    )
    value_rows = value_sum.astype(jnp.bfloat16)
    query_order = slot_range * ctx_count + my_index
    softmax_scale = head_dim ** (-0.5)
    running_max = jnp.full((kept_dev, kv_local, group_size), -1e30, jnp.float32)
    key_piece, value_piece = in_one_piece((key_rows, value_rows), "ctx", 0, 1)
    piece_rows = key_piece.shape[0]
    key_piece = key_piece.reshape(piece_rows, kv_local, head_dim)
    value_piece = value_piece.reshape(piece_rows, kv_local, head_dim).astype(jnp.float32)
    row_ids = jnp.arange(piece_rows, dtype=jnp.int32)
    key_order = row_ids % kept_dev * ctx_count + row_ids // kept_dev
    allowed = (key_order[None, :] <= query_order[:, None])[:, None, None, :]
    scores = (
        jnp.einsum("qhgd,khd->qhgk", queries, key_piece, preferred_element_type=jnp.float32)
        * softmax_scale
    )
    scores = jnp.where(allowed, scores, -1e30)
    new_max = jnp.maximum(running_max, jnp.max(scores, axis=-1))
    weights = jnp.where(allowed, jnp.exp(scores - new_max[..., None]), 0.0)
    running_sum = jnp.sum(weights, axis=-1)
    weighted = jnp.einsum("qhgk,khd->qhgd", weights, value_piece)
    attended = (
        (weighted / running_sum[..., None]).reshape(kept_dev, query_cols).astype(jnp.bfloat16)
    )
    head_delta = jnp.dot(
        attended,
        lax.all_gather(out_weight, "ctx", axis=1, tiled=True),
        preferred_element_type=jnp.float32,
    )
    head_share = sent_and_summed(head_delta.astype(jnp.bfloat16), "mp", 1)
    mixed_share = local_rows.astype(jnp.float32) + head_share
    gain = mlp_gain.astype(jnp.float32)
    mlp_share = feed_forward(
        (mixed_share * gain).astype(jnp.bfloat16),
        jnp.broadcast_to(1.0 / gain, (8, feature_cols)),
        gate_weight,
        up_weight,
        down_weight,
    )
    update = (router_score[:, None] * (head_share + mlp_share)).astype(jnp.bfloat16)
    returning = (
        jnp.zeros((slots_all, feature_cols), jnp.bfloat16)
        .at[recv_index]
        .set(update)
        .reshape(ctx_count, capacity, feature_cols)
    )
    returned = lax.all_to_all(returning, "ctx", split_axis=0, concat_axis=0, tiled=True).reshape(
        slots_all, feature_cols
    )
    arriving = jnp.take(returned, send_index, axis=0, mode="fill", fill_value=0)
    return (tokens.astype(jnp.float32) + arriving.astype(jnp.float32)).astype(jnp.bfloat16)


def solution(mesh):
    in_specs = (
        P("ctx", "mp"),
        P(),
        P(),
        P("ctx", "mp"),
        P("ctx", "mp"),
        P("ctx", "mp"),
        P("mp", "ctx"),
        P("mp"),
        P("mp", "ctx"),
        P("mp", "ctx"),
        P("ctx", "mp"),
        P("ctx"),
        P("ctx"),
    )
    out_specs = P("ctx", "mp")
    return jax.shard_map(body, mesh=mesh, in_specs=in_specs, out_specs=out_specs, check_vma=False)
```

```python
import jax
import jax.numpy as jnp
from jax import lax
from jax.sharding import PartitionSpec as P

from jax.experimental import pallas as pl
from jax.experimental.pallas import tpu as pltpu

HEAD_DIM = 128
BOX = 16
MESH = pl.DeviceIdType.MESH
EPS = 1e-05


def remote(source, target, sent, landed, device):
    return pltpu.make_async_remote_copy(
        src_ref=source,
        dst_ref=target,
        send_sem=sent,
        recv_sem=landed,
        device_id=device,
        device_id_type=MESH,
    )


def mlp_kernel(
    x_ref,
    share_ref,
    score_ref,
    take_ref,
    send_ref,
    tokens_ref,
    inv_gain_ref,
    gate_ref,
    up_ref,
    down_ref,
    out_ref,
    own_x,
    sib_x,
    sib_gain,
    weight,
    down,
    part,
    sums,
    hidden,
    delta,
    deltas,
    total_ref,
    outbox,
    inbox,
    load_sem,
    swap_send,
    swap_recv,
    x_send,
    x_recv,
    pass_send,
    pass_recv,
    sum_send,
    sum_recv,
    hid_send,
    hid_recv,
    hop_send,
    hop_recv,
    out_send,
    out_recv,
    box_send,
    box_recv,
):
    rows, feats = x_ref.shape
    slots = outbox.shape[0]
    box = slots // 16
    half = gate_ref.shape[1] // 2
    both = 2 * half
    group = 4 * rows
    c, m = lax.axis_index("ctx"), lax.axis_index("mp")
    x, y = c // 4, c % 4
    z, core = m // 2, m % 2
    sibling = (c, z * 2 + 1 - core)

    def peer(step):
        turn = step // 4
        shift = turn + (turn // 2) * (1 - 2 * (turn % 2))
        return lax.rem(x + 4 - shift, 4) * 4 + lax.rem(y + step % 4, 4)

    def z_peer(step):
        return lax.rem(z + step, 4)

    def group_of(turn):
        shift = turn + (turn // 2) * (1 - 2 * (turn % 2))
        return lax.rem(x + shift, 4)

    barrier = pltpu.get_barrier_semaphore()

    @pl.loop(1, 16)
    def _(k):
        pl.semaphore_signal(barrier, inc=1, device_id=(peer(k), m), device_id_type=MESH)

    for k in range(1, 4):
        pl.semaphore_signal(
            barrier, inc=1, device_id=(c, z_peer(k) * 2 + core), device_id_type=MESH
        )
    pl.semaphore_signal(barrier, inc=1, device_id=sibling, device_id_type=MESH)

    mine = pl.multiple_of(core * half, 128)
    others = pl.multiple_of((1 - core) * half, 128)
    loads = [
        pltpu.make_async_copy(
            gate_ref.at[:, pl.ds(mine, half)],
            weight.at[pl.ds(0, feats), pl.ds(0, half)],
            load_sem.at[0],
        ),
        pltpu.make_async_copy(
            up_ref.at[:, pl.ds(mine, half)],
            weight.at[pl.ds(0, feats), pl.ds(half, half)],
            load_sem.at[1],
        ),
        pltpu.make_async_copy(down_ref, down, load_sem.at[2]),
    ]
    for load in loads:
        load.start()
    my_rows = pl.ds(pl.multiple_of(c * rows, rows), rows)
    own_x[my_rows, :] = x_ref[...]
    pl.semaphore_wait(barrier, 19)

    def x_copy(who, device):
        place = pl.ds(pl.multiple_of(who * rows, rows), rows)
        return remote(own_x.at[place], own_x.at[place], x_send.at[who], x_recv.at[who], device)

    def x_out(k):
        return remote(
            own_x.at[my_rows], own_x.at[my_rows], x_send.at[k], x_recv.at[c], (peer(k), m)
        )

    def x_pass(who):
        place = pl.ds(pl.multiple_of(who * rows, rows), rows)
        return remote(
            own_x.at[place], sib_x.at[place], pass_send.at[who], pass_recv.at[who], sibling
        )

    @pl.loop(1, 4)
    def _(k):
        x_out(k).start()

    swaps = [
        remote(
            gate_ref.at[:, pl.ds(others, half)],
            weight.at[pl.ds(feats, feats), pl.ds(0, half)],
            swap_send.at[0],
            swap_recv.at[0],
            sibling,
        ),
        remote(
            up_ref.at[:, pl.ds(others, half)],
            weight.at[pl.ds(feats, feats), pl.ds(half, half)],
            swap_send.at[1],
            swap_recv.at[1],
            sibling,
        ),
        remote(inv_gain_ref, sib_gain, swap_send.at[2], swap_recv.at[2], sibling),
    ]
    x_pass(c).start()
    for swap in swaps:
        swap.start()

    @pl.loop(4, 16)
    def _(k):
        x_out(k).start()

    for load in loads:
        load.wait()
    for swap in swaps:
        swap.wait()

    def sum_out(turn, k):
        to = z_peer(k)
        return remote(
            part.at[turn, pl.ds(pl.multiple_of(to * rows, rows), rows)],
            sums.at[turn, z],
            sum_send.at[turn * 4 + k],
            sum_recv.at[turn * 4 + z],
            (c, to * 2 + core),
        )

    def sum_in(turn, k):
        at = z_peer(k)
        return remote(
            part.at[turn, pl.ds(0, rows)],
            sums.at[turn, at],
            sum_send.at[turn * 4 + k],
            sum_recv.at[turn * 4 + at],
            (c, at * 2 + core),
        )

    def hid_out(turn, k):
        return remote(
            hidden.at[turn, core, z],
            hidden.at[turn, core, z],
            hid_send.at[turn * 4 + k],
            hid_recv.at[turn * 4 + z],
            (c, z_peer(k) * 2 + core),
        )

    def hid_in(turn, k):
        at = z_peer(k)
        return remote(
            hidden.at[turn, core, at],
            hidden.at[turn, core, at],
            hid_send.at[turn * 4 + k],
            hid_recv.at[turn * 4 + at],
            (c, at * 2 + core),
        )

    def hid_pass(turn, at):
        return remote(
            hidden.at[turn, core, at],
            hidden.at[turn, core, at],
            hop_send.at[turn * 4 + at],
            hop_recv.at[turn * 4 + at],
            sibling,
        )

    def hid_passed(turn, at):
        return remote(
            hidden.at[turn, 1 - core, at],
            hidden.at[turn, 1 - core, at],
            hop_send.at[turn * 4 + at],
            hop_recv.at[turn * 4 + at],
            sibling,
        )

    def out_copy(who, slot):
        return remote(
            delta.at[pl.ds(pl.multiple_of(who * rows, rows), rows)],
            deltas.at[slot],
            out_send.at[who],
            out_recv.at[slot],
            (who, m),
        )

    def front(turn):
        g = group_of(turn)

        @pl.loop(0, 4)
        def _(k):
            who = g * 4 + lax.rem(y + 4 - k, 4)

            @pl.when(who != c)
            def _():
                x_copy(who, (who, m)).wait_recv()
                x_pass(who).start()

        @pl.loop(0, 4)
        def _(k):
            who = g * 4 + lax.rem(y + 4 - k, 4)
            x_pass(who).wait_recv()

        place = pl.ds(pl.multiple_of(g * group, group), group)
        mixed = own_x[place, :].astype(jnp.float32) * inv_gain_ref[0:1, :]
        square = jnp.sum(mixed * mixed, axis=1, keepdims=True)
        mixed = sib_x[place, :].astype(jnp.float32) * sib_gain[0:1, :]
        square = square + jnp.sum(mixed * mixed, axis=1, keepdims=True)
        square = jnp.broadcast_to(square, (group, 128))
        coarse = square.astype(jnp.bfloat16)
        fine = (square - coarse.astype(jnp.float32)).astype(jnp.bfloat16)
        lane = lax.broadcasted_iota(jnp.int32, (group, 128), 1)
        part[turn, :, pl.ds(both, 128)] = jnp.where(lane < 64, coarse, fine)

        @pl.loop(0, both // 256)
        def _(tile):
            cols = pl.ds(pl.multiple_of(tile * 256, 256), 256)
            total = jnp.dot(
                own_x[place, :], weight[pl.ds(0, feats), cols], preferred_element_type=jnp.float32
            )
            total += jnp.dot(
                sib_x[place, :],
                weight[pl.ds(feats, feats), cols],
                preferred_element_type=jnp.float32,
            )
            part[turn, :, cols] = total.astype(jnp.bfloat16)

        for k in (2, 1, 3):
            sum_out(turn, k).start()

    def middle(turn):
        total = part[turn, pl.ds(pl.multiple_of(z * rows, rows), rows), :].astype(jnp.float32)
        for k in range(1, 4):
            sum_in(turn, k).wait_recv()
            total += sums[turn, z_peer(k)].astype(jnp.float32)
        square = total[:, both : both + 1] + total[:, both + 64 : both + 65]
        scale = lax.rsqrt(square * (1.0 / (8 * feats)) + EPS)
        gate = total[:, :half] * scale
        up = total[:, half:both] * scale
        hidden[turn, core, z] = (gate / (1.0 + jnp.exp(-gate)) * up).astype(jnp.bfloat16)
        for k in (2, 1, 3):
            hid_out(turn, k).start()
        hid_pass(turn, z).start()

    def back(turn):
        for k in range(1, 4):
            hid_in(turn, k).wait_recv()
            hid_pass(turn, z_peer(k)).start()
        for k in range(4):
            hid_passed(turn, z_peer(k)).wait_recv()
        g = group_of(turn)
        place = pl.ds(pl.multiple_of(g * group, group), group)

        @pl.loop(0, feats // 256)
        def _(tile):
            cols = pl.ds(pl.multiple_of(tile * 256, 256), 256)
            total = jnp.dot(
                hidden[turn, 0].reshape(group, half),
                down[pl.ds(0, half), cols],
                preferred_element_type=jnp.float32,
            )
            total += jnp.dot(
                hidden[turn, 1].reshape(group, half),
                down[pl.ds(half, half), cols],
                preferred_element_type=jnp.float32,
            )
            delta[place, cols] = total.astype(jnp.bfloat16)

        @pl.loop(0, 4)
        def _(k):
            who = g * 4 + lax.rem(y + k, 4)

            @pl.when(who != c)
            def _():
                out_copy(who, c).start()

    @pl.loop(0, 6)
    def _(step):
        @pl.when(step < 4)
        def _():
            front(step)

        @pl.when((step >= 1) & (step < 5))
        def _():
            middle(step - 1)

        @pl.when(step >= 2)
        def _():
            back(step - 2)

    total_ref[...] = share_ref[...] + delta[my_rows, :].astype(jnp.float32)

    @pl.loop(1, 16)
    def _(k):
        who = peer(k)
        out_copy(who, who).wait_recv()
        total_ref[...] += deltas[who].astype(jnp.float32)

    update = (score_ref[:, 0:1] * total_ref[...]).astype(jnp.bfloat16)
    slot_at = lax.broadcasted_iota(jnp.int32, (slots, rows), 0)
    give = jnp.where(slot_at == take_ref[0:1, :], 1.0, 0.0).astype(jnp.bfloat16)
    outbox[...] = jnp.dot(give, update, preferred_element_type=jnp.float32).astype(jnp.bfloat16)

    def box_of(who):
        return pl.ds(pl.multiple_of(who * box, box), box)

    def box_copy(who, slot):
        return remote(
            outbox.at[box_of(who)], inbox.at[box_of(slot)], box_send.at[who], box_recv.at[slot], (who, m)
        )

    @pl.loop(1, 16)
    def _(k):
        box_copy(peer(k), c).start()

    inbox[box_of(c), :] = outbox[box_of(c), :]
    slot_at = lax.broadcasted_iota(jnp.int32, (tokens_ref.shape[0], slots), 1)
    back_to = jnp.where(slot_at == send_ref[:, 0:1], 1.0, 0.0).astype(jnp.bfloat16)

    @pl.loop(1, 16)
    def _(k):
        box_copy(peer(k), peer(k)).wait_recv()

    @pl.loop(0, feats // 256)
    def _(tile):
        cols = pl.ds(pl.multiple_of(tile * 256, 256), 256)
        arrived = jnp.dot(back_to, inbox[:, cols], preferred_element_type=jnp.float32)
        out_ref[:, cols] = (tokens_ref[:, cols].astype(jnp.float32) + arrived).astype(jnp.bfloat16)

    @pl.loop(1, 16)
    def _(k):
        x_out(k).wait_send()
        out_copy(peer(k), c).wait_send()
        box_copy(peer(k), c).wait_send()

    @pl.loop(0, 16)
    def _(who):
        x_pass(who).wait_send()

    @pl.loop(0, 4)
    def _(turn):
        for k in range(1, 4):
            sum_out(turn, k).wait_send()
            hid_out(turn, k).wait_send()
        for k in range(4):
            hid_pass(turn, z_peer(k)).wait_send()


def feed_forward(scaled, share, score, take, send, tokens, inv_gain, gate_weight, up_weight, down_weight):
    rows, feats = scaled.shape
    cols = gate_weight.shape[1]
    half = cols // 2
    dma = pltpu.SemaphoreType.DMA
    bf16 = jnp.bfloat16
    vmem, anywhere = pl.BlockSpec(memory_space=pltpu.VMEM), pl.BlockSpec(memory_space=pl.ANY)
    return pl.pallas_call(
        mlp_kernel,
        out_shape=jax.ShapeDtypeStruct(tokens.shape, bf16),
        in_specs=[vmem] * 7 + [anywhere, anywhere, anywhere],
        out_specs=vmem,
        scratch_shapes=[
            pltpu.VMEM((16 * rows, feats), bf16),
            pltpu.VMEM((16 * rows, feats), bf16),
            pltpu.VMEM((8, feats), jnp.float32),
            pltpu.VMEM((2 * feats, cols), bf16),
            pltpu.VMEM((cols, feats), bf16),
            pltpu.VMEM((4, 4 * rows, cols + 128), bf16),
            pltpu.VMEM((4, 4, rows, cols + 128), bf16),
            pltpu.VMEM((4, 2, 4, rows, half), bf16),
            pltpu.VMEM((16 * rows, feats), bf16),
            pltpu.VMEM((16, rows, feats), bf16),
            pltpu.VMEM((rows, feats), jnp.float32),
            pltpu.VMEM((16 * BOX, feats), bf16),
            pltpu.VMEM((16 * BOX, feats), bf16),
            dma((3,)),
            dma((3,)),
            dma((3,)),
        ]
        + [dma((16,))] * 14,
        compiler_params=pltpu.CompilerParams(
            collective_id=3, has_side_effects=True, vmem_limit_bytes=56 * 2**20
        ),
        name="feed_forward",
    )(scaled, share, score, take, send, tokens, inv_gain, gate_weight, up_weight, down_weight)


def attend_kernel(
    tokens_ref,
    send_ref,
    take_ref,
    gain_ref,
    router_ref,
    query_ref,
    key_ref,
    value_ref,
    out_weight_ref,
    cosine_ref,
    sine_ref,
    mlp_gain_ref,
    share_ref,
    scaled_ref,
    score_ref,
    outbox,
    inbox,
    full,
    normed,
    blocks,
    weight,
    out_weight,
    part,
    parts,
    key_value,
    attended,
    delta,
    deltas,
    load_sem,
    box_send,
    box_recv,
    row_send,
    row_recv,
    hop_send,
    hop_recv,
    norm_send,
    norm_recv,
    part_send,
    part_recv,
    kv_send,
    kv_recv,
    att_send,
    att_recv,
    out_send,
    out_recv,
):
    rows, feats = share_ref.shape
    width = blocks.shape[1]
    slots = outbox.shape[0]
    box = slots // 16
    group = 4 * rows
    q_cols, kv_cols = query_ref.shape[1], key_ref.shape[1]
    heads = q_cols // HEAD_DIM
    c, m = lax.axis_index("ctx"), lax.axis_index("mp")
    x, y = c // 4, c % 4
    home = c // 2
    z, core = m // 2, m % 2
    sibling = (c, z * 2 + 1 - core)

    def peer(step):
        turn = step // 4
        shift = turn + (turn // 2) * (1 - 2 * (turn % 2))
        return lax.rem(x + 4 - shift, 4) * 4 + lax.rem(y + step % 4, 4)

    def group_of(turn):
        shift = turn + (turn // 2) * (1 - 2 * (turn % 2))
        return lax.rem(x + shift, 4)

    def rows_of(who, count=1):
        return pl.ds(pl.multiple_of(who * (rows * count), rows), rows * count)

    is_home = m == home
    barrier = pltpu.get_barrier_semaphore()

    @pl.loop(0, 16)
    def _(k):
        @pl.when(k > 0)
        def _():
            pl.semaphore_signal(barrier, inc=1, device_id=(peer(k), m), device_id_type=MESH)

        @pl.when(jnp.logical_not(is_home & (k // 8 == c % 2) & (k % 8 == m)))
        def _():
            pl.semaphore_signal(
                barrier, inc=1, device_id=(2 * m + k // 8, k % 8), device_id_type=MESH
            )

    for k in range(1, 4):
        pl.semaphore_signal(
            barrier,
            inc=1,
            device_id=(c, lax.rem(z + k, 4) * 2 + core),
            device_id_type=MESH,
        )
    pl.semaphore_signal(barrier, inc=1, device_id=sibling, device_id_type=MESH)

    loads = [
        pltpu.make_async_copy(query_ref, weight.at[:, pl.ds(0, q_cols)], load_sem.at[0]),
        pltpu.make_async_copy(key_ref, weight.at[:, pl.ds(q_cols, kv_cols)], load_sem.at[1]),
        pltpu.make_async_copy(
            value_ref, weight.at[:, pl.ds(q_cols + kv_cols, kv_cols)], load_sem.at[2]
        ),
        pltpu.make_async_copy(out_weight_ref, out_weight, load_sem.at[3]),
    ]
    for load in loads:
        load.start()

    slot_at = lax.broadcasted_iota(jnp.int32, (slots, tokens_ref.shape[0]), 0)
    pick = jnp.where(slot_at == send_ref[0:1, :], 1.0, 0.0).astype(jnp.bfloat16)

    @pl.loop(0, feats // 256)
    def _(tile):
        cols = pl.ds(pl.multiple_of(tile * 256, 256), 256)
        outbox[:, cols] = jnp.dot(
            pick, tokens_ref[:, cols], preferred_element_type=jnp.float32
        ).astype(jnp.bfloat16)

    def box_of(who):
        return pl.ds(pl.multiple_of(who * box, box), box)

    inbox[box_of(c), :] = outbox[box_of(c), :]
    pl.semaphore_wait(barrier, jnp.where(is_home, 34, 35))

    def box_copy(who, slot):
        return remote(
            outbox.at[box_of(who)], inbox.at[box_of(slot)], box_send.at[who], box_recv.at[slot], (who, m)
        )

    @pl.loop(1, 16)
    def _(k):
        box_copy(peer(k), c).start()

    @pl.loop(1, 16)
    def _(k):
        box_copy(peer(k), peer(k)).wait_recv()

    slot_at = lax.broadcasted_iota(jnp.int32, (rows, slots), 1)
    take = jnp.where(slot_at == take_ref[:, 0:1], 1.0, 0.0).astype(jnp.bfloat16)
    full[m] = jnp.dot(take, inbox[...], preferred_element_type=jnp.float32).astype(jnp.bfloat16)

    def row_copy(k, who):
        return remote(
            full.at[who],
            full.at[who],
            row_send.at[k],
            row_recv.at[who],
            (c, lax.rem(z + k, 4) * 2 + core),
        )

    def hop(who):
        return remote(full.at[who], full.at[who], hop_send.at[who], hop_recv.at[who], sibling)

    def z_block(k):
        return lax.rem(z + k, 4) * 2 + core

    def z_sibling(k):
        return lax.rem(z + k, 4) * 2 + 1 - core

    for k in (2, 1, 3):
        row_copy(k, m).start()
    hop(m).start()
    for k in (1, 3, 2):
        row_copy(k, z_block(k)).wait_recv()
        hop(z_block(k)).start()
    for k in (0, 1, 3, 2):
        hop(z_sibling(k)).wait_recv()

    square, route = 0.0, 0.0
    for at in range(8):
        wide = full[at].astype(jnp.float32)
        square += jnp.sum(wide * wide, axis=1, keepdims=True)
        route += jnp.sum(wide * router_ref[at : at + 1, :], axis=1, keepdims=True)
    scale = lax.rsqrt(square * (1.0 / (8 * feats)) + EPS)
    score_ref[...] = jnp.broadcast_to(1.0 / (1.0 + jnp.exp(-route)), score_ref.shape)
    for at in range(8):
        wide = full[at].astype(jnp.float32) * scale * gain_ref[at : at + 1, :]
        wide = wide.astype(jnp.bfloat16)
        normed[2 * at] = wide[:, :width]
        normed[2 * at + 1] = wide[:, width:]

    def norm_copy(who, slot):
        return remote(
            normed.at[who], blocks.at[rows_of(slot)], norm_send.at[who], norm_recv.at[slot], (who, m)
        )

    @pl.loop(1, 16)
    def _(k):
        norm_copy(peer(k), c).start()

    blocks[rows_of(c), :] = normed[c]
    for load in loads:
        load.wait()

    def part_copy(who, slot):
        return remote(
            part.at[rows_of(who)], parts.at[slot], part_send.at[who], part_recv.at[slot], (who, m)
        )

    @pl.loop(0, 4)
    def _(turn):
        g = group_of(turn)

        @pl.loop(0, 4)
        def _(k):
            who = g * 4 + k

            @pl.when(who != c)
            def _():
                norm_copy(who, who).wait_recv()

        here = rows_of(g, 4)
        part[here, :] = jnp.dot(
            blocks[here, :], weight[...], preferred_element_type=jnp.float32
        ).astype(jnp.bfloat16)

        @pl.loop(0, 4)
        def _(k):
            who = g * 4 + lax.rem(y + k, 4)

            @pl.when(who != c)
            def _():
                part_copy(who, c).start()

    for at in range(0, weight.shape[1], HEAD_DIM):
        total_at = part[rows_of(c), at : at + HEAD_DIM]
        share_ref[:, at : at + HEAD_DIM] = total_at.astype(jnp.float32)

    @pl.loop(1, 16)
    def _(k):
        who = peer(k)
        part_copy(who, who).wait_recv()
        share_ref[:, 0 : weight.shape[1]] += parts[who].astype(jnp.float32)

    def turned(at):
        head = share_ref[:, at : at + HEAD_DIM]
        swapped = pltpu.roll(head, HEAD_DIM // 2, 1)
        return (head * cosine_ref[...] + swapped * sine_ref[...]).astype(jnp.bfloat16)

    mine = rows_of(c)
    key_value[mine, 0:HEAD_DIM] = turned(q_cols)
    at = q_cols + kv_cols
    key_value[mine, HEAD_DIM : 2 * HEAD_DIM] = share_ref[:, at : at + HEAD_DIM].astype(jnp.bfloat16)

    def kv_copy(k, who):
        return remote(
            key_value.at[rows_of(who)],
            key_value.at[rows_of(who)],
            kv_send.at[k],
            kv_recv.at[who],
            (peer(k), m),
        )

    @pl.loop(1, 16)
    def _(k):
        kv_copy(k, c).start()

    queries = jnp.concatenate([turned(h * HEAD_DIM) for h in range(heads)], axis=0)

    @pl.loop(1, 16)
    def _(k):
        kv_copy(k, peer(k)).wait_recv()

    keys = 16 * rows
    scores = lax.dot_general(
        queries,
        key_value[:, 0:HEAD_DIM],
        (((1,), (1,)), ((), ())),
        preferred_element_type=jnp.float32,
    ) * (HEAD_DIM ** (-0.5))
    query_at = lax.broadcasted_iota(jnp.int32, (heads * rows, keys), 0) % rows * 16 + c
    key_at = lax.broadcasted_iota(jnp.int32, (heads * rows, keys), 1)
    allowed = key_at % rows * 16 + key_at // rows <= query_at
    scores = jnp.where(allowed, scores, -1e30)
    weights = jnp.exp(scores - jnp.max(scores, axis=1, keepdims=True))
    weights = jnp.where(allowed, weights, 0.0)
    total = jnp.sum(weights, axis=1, keepdims=True)
    mixed = (
        jnp.dot(
            weights.astype(jnp.bfloat16),
            key_value[:, HEAD_DIM : 2 * HEAD_DIM],
            preferred_element_type=jnp.float32,
        )
        / total
    ).astype(jnp.bfloat16)
    for h in range(heads):
        attended[mine, h * HEAD_DIM : (h + 1) * HEAD_DIM] = mixed[h * rows : (h + 1) * rows]

    def att_copy(k, who):
        return remote(
            attended.at[rows_of(who)],
            attended.at[rows_of(who)],
            att_send.at[k],
            att_recv.at[who],
            (peer(k), m),
        )

    @pl.loop(1, 16)
    def _(k):
        att_copy(k, c).start()

    my_slot = (c % 2) * 8 + m

    def out_copy(who):
        return remote(
            delta.at[rows_of(who)],
            deltas.at[my_slot],
            out_send.at[who],
            out_recv.at[my_slot],
            (who, home),
        )

    def out_in(slot):
        return remote(
            delta.at[pl.ds(0, rows)],
            deltas.at[slot],
            out_send.at[slot],
            out_recv.at[slot],
            (2 * m + slot // 8, slot % 8),
        )

    @pl.loop(0, 4)
    def _(turn):
        g = group_of(turn)

        @pl.loop(0, 4)
        def _(k):
            who = g * 4 + lax.rem(y + 4 - k, 4)

            @pl.when(who != c)
            def _():
                step = turn * 4 + k
                att_copy(step, who).wait_recv()

        here = rows_of(g, 4)
        delta[here, :] = jnp.dot(
            attended[here, :], out_weight[...], preferred_element_type=jnp.float32
        ).astype(jnp.bfloat16)

        @pl.loop(0, 4)
        def _(k):
            who = g * 4 + lax.rem(y + k, 4)

            @pl.when(jnp.logical_not(is_home & (who == c)))
            def _():
                out_copy(who).start()

    @pl.when(is_home)
    def _():
        deltas[my_slot] = delta[mine, :]

    share_ref[...] = jnp.zeros_like(share_ref)

    for side in range(2):

        @pl.loop(0, 8)
        def _(k):
            slot = side * 8 + lax.rem(k + m, 8)

            @pl.when(jnp.logical_not(is_home & (slot == my_slot)))
            def _():
                out_in(slot).wait_recv()

            share_ref[:, side * width : (side + 1) * width] += deltas[slot].astype(jnp.float32)

    mixed = full[m].astype(jnp.float32) + share_ref[...]
    scaled_ref[...] = (mixed * mlp_gain_ref[0:1, :]).astype(jnp.bfloat16)

    for k in range(1, 4):
        row_copy(k, m).wait_send()
    for k in range(4):
        hop(z_block(k)).wait_send()

    @pl.loop(0, 16)
    def _(k):
        @pl.when(jnp.logical_not(is_home & (k == c)))
        def _():
            out_copy(k).wait_send()

        @pl.when(k != c)
        def _():
            box_copy(k, c).wait_send()
            norm_copy(k, c).wait_send()
            part_copy(k, c).wait_send()

        @pl.when(k > 0)
        def _():
            kv_copy(k, c).wait_send()
            att_copy(k, c).wait_send()


def attend(tokens, send, take, gain, router, query, key, value, out_weight, cosine, sine, mlp_gain):
    count, slots = take.shape[0], 16 * BOX
    feats = tokens.shape[1]
    width = query.shape[0]
    cols = query.shape[1] + key.shape[1] + value.shape[1]
    out_cols = out_weight.shape[1]
    dma = pltpu.SemaphoreType.DMA
    bf16 = jnp.bfloat16
    vmem, anywhere = pl.BlockSpec(memory_space=pltpu.VMEM), pl.BlockSpec(memory_space=pl.ANY)
    return pl.pallas_call(
        attend_kernel,
        out_shape=(
            jax.ShapeDtypeStruct((count, feats), jnp.float32),
            jax.ShapeDtypeStruct((count, feats), bf16),
            jax.ShapeDtypeStruct((count, 128), jnp.float32),
        ),
        in_specs=[vmem] * 5 + [anywhere] * 4 + [vmem] * 3,
        out_specs=(vmem, vmem, vmem),
        scratch_shapes=[
            pltpu.VMEM((slots, feats), bf16),
            pltpu.VMEM((slots, feats), bf16),
            pltpu.VMEM((8, count, feats), bf16),
            pltpu.VMEM((16, count, width), bf16),
            pltpu.VMEM((16 * count, width), bf16),
            pltpu.VMEM((width, cols), bf16),
            pltpu.VMEM(out_weight.shape, bf16),
            pltpu.VMEM((16 * count, cols), bf16),
            pltpu.VMEM((16, count, cols), bf16),
            pltpu.VMEM((16 * count, 2 * HEAD_DIM), bf16),
            pltpu.VMEM((16 * count, query.shape[1]), bf16),
            pltpu.VMEM((16 * count, out_cols), bf16),
            pltpu.VMEM((16, count, out_cols), bf16),
            dma((4,)),
        ]
        + [dma((16,))] * 16,
        compiler_params=pltpu.CompilerParams(
            collective_id=2, has_side_effects=True, vmem_limit_bytes=48 * 2**20
        ),
        name="attend",
    )(tokens, send, take, gain, router, query, key, value, out_weight, cosine, sine, mlp_gain)


def body(
    tokens,
    norm_gain,
    router_weight,
    query_weight,
    key_weight,
    value_weight,
    out_weight,
    mlp_gain,
    gate_weight,
    up_weight,
    down_weight,
    destination,
    kept_pos,
):
    ctx_count = lax.axis_size("ctx")
    tok_dev = tokens.shape[0]
    kept_dev = kept_pos.shape[0]
    feature_cols = tokens.shape[1]
    capacity = BOX
    slots_all = ctx_count * capacity
    peer_ids = jnp.arange(ctx_count, dtype=jnp.int32)
    is_kept = destination >= 0
    owner_ids = destination // kept_dev
    slot_ids = destination % kept_dev
    kept_order = slot_ids * ctx_count + owner_ids
    first_order = jnp.min(jnp.where(is_kept, kept_order, ctx_count * kept_dev))
    first_slots = (first_order - peer_ids + ctx_count - 1) // ctx_count
    owner_match = owner_ids[:, None] == peer_ids[None, :]
    send_index = (
        owner_ids * capacity
        + slot_ids
        - jnp.sum(jnp.where(owner_match, first_slots[None, :], 0), axis=1)
    )
    send_index = jnp.where(is_kept, send_index, slots_all)
    slot_range = jnp.arange(kept_dev, dtype=jnp.int32)
    source_ids = kept_pos // tok_dev
    source_match = source_ids[:, None] == peer_ids[None, :]
    first_from = jnp.min(jnp.where(source_match, slot_range[:, None], kept_dev), axis=0)
    recv_index = (
        source_ids * capacity
        + slot_range
        - jnp.sum(jnp.where(source_match, first_from[None, :], 0), axis=1)
    )
    half_dim = HEAD_DIM // 2
    exponent = jnp.arange(half_dim, dtype=jnp.float32) * (2.0 / HEAD_DIM)
    angles = kept_pos.astype(jnp.float32)[:, None] * (500000.0 ** (-exponent))[None, :]
    cosine, sine = jnp.cos(angles), jnp.sin(angles)
    later_gain = mlp_gain.astype(jnp.float32)
    head_share, scaled, score = attend(
        tokens,
        jnp.broadcast_to(send_index, (8, tok_dev)),
        jnp.broadcast_to(recv_index[:, None], (kept_dev, 128)),
        norm_gain.astype(jnp.float32).reshape(8, feature_cols),
        router_weight.astype(jnp.float32).reshape(8, feature_cols),
        query_weight,
        key_weight,
        value_weight,
        out_weight,
        jnp.concatenate([cosine, cosine], axis=1),
        jnp.concatenate([-sine, sine], axis=1),
        jnp.broadcast_to(later_gain, (8, feature_cols)),
    )
    return feed_forward(
        scaled,
        head_share,
        score,
        jnp.broadcast_to(recv_index, (8, kept_dev)),
        jnp.broadcast_to(send_index[:, None], (tok_dev, 128)),
        tokens,
        jnp.broadcast_to(1.0 / later_gain, (8, feature_cols)),
        gate_weight,
        up_weight,
        down_weight,
    )


def solution(mesh):
    in_specs = (
        P("ctx", "mp"),
        P(),
        P(),
        P("ctx", "mp"),
        P("ctx", "mp"),
        P("ctx", "mp"),
        P("mp", "ctx"),
        P("mp"),
        P("mp", "ctx"),
        P("mp", "ctx"),
        P("ctx", "mp"),
        P("ctx"),
        P("ctx"),
    )
    out_specs = P("ctx", "mp")
    return jax.shard_map(body, mesh=mesh, in_specs=in_specs, out_specs=out_specs, check_vma=False)
```

```python
import jax
import jax.numpy as jnp
from jax import lax
from jax.sharding import PartitionSpec as P

from jax.experimental import pallas as pl
from jax.experimental.pallas import tpu as pltpu

HEAD_DIM = 128
BOX = 16
MESH = pl.DeviceIdType.MESH
OFFSETS = (
    (0, 0), (0, 1), (1, 0), (0, 3), (3, 0), (1, 1), (3, 3), (1, 3),
    (3, 1), (0, 2), (2, 0), (1, 2), (2, 1), (3, 2), (2, 3), (2, 2),
)
EPS = 1e-05


def ahead(c, k):
    dx, dy = OFFSETS[k]
    return lax.rem(c // 4 + dx, 4) * 4 + lax.rem(c % 4 + dy, 4)


def behind(c, k):
    dx, dy = OFFSETS[k]
    return lax.rem(c // 4 + 4 - dx, 4) * 4 + lax.rem(c % 4 + 4 - dy, 4)


def remote(source, target, sent, landed, device):
    return pltpu.make_async_remote_copy(
        src_ref=source,
        dst_ref=target,
        send_sem=sent,
        recv_sem=landed,
        device_id=device,
        device_id_type=MESH,
    )


def mlp_kernel(
    x_ref,
    share_ref,
    score_ref,
    take_ref,
    send_ref,
    tokens_ref,
    inv_gain_ref,
    gate_ref,
    up_ref,
    gate_half_ref,
    up_half_ref,
    down_ref,
    out_ref,
    own_x,
    sib_x,
    sib_gain,
    weight,
    down,
    part,
    relayed,
    joined,
    sums,
    hidden,
    delta,
    deltas,
    total_ref,
    outbox,
    inbox,
    load_sem,
    swap_send,
    swap_recv,
    x_send,
    x_recv,
    pass_send,
    pass_recv,
    far_send,
    far_recv,
    sum_send,
    sum_recv,
    join_send,
    join_recv,
    hid_send,
    hid_recv,
    lap_send,
    lap_recv,
    hop_send,
    hop_recv,
    out_send,
    out_recv,
    box_send,
    box_recv,
):
    rows, feats = x_ref.shape
    slots = outbox.shape[0]
    box = slots // 16
    half = gate_ref.shape[1] // 2
    both = 2 * half
    group = 4 * rows
    c, m = lax.axis_index("ctx"), lax.axis_index("mp")
    x, y = c // 4, c % 4
    z, core = m // 2, m % 2
    sibling = (c, z * 2 + 1 - core)

    def z_peer(step):
        return lax.rem(z + step, 4)

    barrier = pltpu.get_barrier_semaphore()

    for k in range(1, 16):
        pl.semaphore_signal(barrier, inc=1, device_id=(ahead(c, k), m), device_id_type=MESH)

    for k in (1, 3):
        pl.semaphore_signal(
            barrier, inc=1, device_id=(c, z_peer(k) * 2 + core), device_id_type=MESH
        )
    pl.semaphore_signal(barrier, inc=1, device_id=sibling, device_id_type=MESH)

    mine = pl.multiple_of(core * half, 128)
    loads = [
        pltpu.make_async_copy(
            gate_ref.at[:, pl.ds(mine, half)],
            weight.at[pl.ds(0, feats), pl.ds(0, half)],
            load_sem.at[0],
        ),
        pltpu.make_async_copy(
            up_ref.at[:, pl.ds(mine, half)],
            weight.at[pl.ds(0, feats), pl.ds(half, half)],
            load_sem.at[1],
        ),
        pltpu.make_async_copy(
            gate_half_ref, weight.at[pl.ds(feats, feats), pl.ds(0, half)], load_sem.at[2]
        ),
        pltpu.make_async_copy(
            up_half_ref, weight.at[pl.ds(feats, feats), pl.ds(half, half)], load_sem.at[3]
        ),
        pltpu.make_async_copy(down_ref, down, load_sem.at[4]),
    ]
    for load in loads:
        load.start()
    own_x[0:rows, :] = x_ref[...]
    pl.semaphore_wait(barrier, 18)

    def x_copy(k):
        place = pl.ds(k * rows, rows)
        return remote(x_ref, own_x.at[place], x_send.at[k], x_recv.at[k], (behind(c, k), m))

    def x_in(slot):
        place = pl.ds(pl.multiple_of(slot * rows, rows), rows)
        return remote(x_ref, own_x.at[place], x_send.at[slot], x_recv.at[slot], sibling)

    def x_pass(who):
        place = pl.ds(pl.multiple_of(who * rows, rows), rows)
        return remote(
            own_x.at[place], sib_x.at[place], pass_send.at[who], pass_recv.at[who], sibling
        )

    for k in range(1, 4):
        x_copy(k).start()
    gain_swap = remote(inv_gain_ref, sib_gain, swap_send.at[0], swap_recv.at[0], sibling)
    x_pass(0).start()
    gain_swap.start()

    short = rows // 2

    def near(way):
        return z_peer(1 + 2 * way)

    def chip(way):
        return (c, near(way) * 2 + core)

    def piece(turn, to, side):
        return part.at[turn, pl.ds(pl.multiple_of(to * rows + side * short, short), short)]

    def far_copy(turn, way):
        at = turn * 2 + way
        return remote(
            piece(turn, z_peer(2), way),
            relayed.at[turn, way],
            far_send.at[at],
            far_recv.at[at],
            chip(way),
        )

    def sum_copy(turn, way):
        at = turn * 2 + way
        return remote(
            piece(turn, near(way), 1 - way),
            sums.at[turn, way, pl.ds((1 - way) * short, short)],
            sum_send.at[at],
            sum_recv.at[at],
            chip(way),
        )

    def join_copy(turn, way):
        at = turn * 2 + way
        return remote(
            joined.at[turn, way],
            sums.at[turn, way, pl.ds(way * short, short)],
            join_send.at[at],
            join_recv.at[at],
            chip(way),
        )

    def hid_copy(turn, way, slot):
        at = turn * 2 + way
        return remote(
            hidden.at[turn, core, slot],
            hidden.at[turn, core, slot],
            hid_send.at[at],
            hid_recv.at[at],
            chip(way),
        )

    def lap_copy(turn, way, slot):
        at = turn * 2 + way
        there = hidden.at[turn, core, slot, pl.ds(way * short, short)]
        return remote(there, there, lap_send.at[at], lap_recv.at[at], chip(way))

    def hid_pass(turn, at):
        return remote(
            hidden.at[turn, core, at],
            hidden.at[turn, core, at],
            hop_send.at[turn * 4 + at],
            hop_recv.at[turn * 4 + at],
            sibling,
        )

    def hid_passed(turn, at):
        return remote(
            hidden.at[turn, 1 - core, at],
            hidden.at[turn, 1 - core, at],
            hop_send.at[turn * 4 + at],
            hop_recv.at[turn * 4 + at],
            sibling,
        )

    def out_copy(slot, who):
        return remote(
            delta.at[pl.ds(pl.multiple_of(slot * rows, rows), rows)],
            deltas.at[slot],
            out_send.at[slot],
            out_recv.at[slot],
            (who, m),
        )

    def out_in(slot):
        return remote(
            delta.at[pl.ds(0, rows)], deltas.at[slot], out_send.at[slot], out_recv.at[slot], sibling
        )

    def front(turn):
        @pl.loop(0, 4)
        def _(k):
            slot = turn * 4 + k

            @pl.when(slot > 0)
            def _():
                x_in(slot).wait_recv()
                x_pass(slot).start()

        for t in range(3):

            @pl.when(turn == t)
            def _():
                for k in range(4 * t + 4, 4 * t + 8):
                    x_copy(k).start()

        @pl.when(turn == 0)
        def _():
            for load in loads:
                load.wait()
            gain_swap.wait()

        @pl.loop(0, 4)
        def _(k):
            x_pass(turn * 4 + k).wait_recv()

        place = pl.ds(pl.multiple_of(turn * group, group), group)
        mixed = own_x[place, :].astype(jnp.float32) * inv_gain_ref[0:1, :]
        square = jnp.sum(mixed * mixed, axis=1, keepdims=True)
        mixed = sib_x[place, :].astype(jnp.float32) * sib_gain[0:1, :]
        square = square + jnp.sum(mixed * mixed, axis=1, keepdims=True)
        square = jnp.broadcast_to(square, (group, 128))
        coarse = square.astype(jnp.bfloat16)
        fine = (square - coarse.astype(jnp.float32)).astype(jnp.bfloat16)
        lane = lax.broadcasted_iota(jnp.int32, (group, 128), 1)
        part[turn, :, pl.ds(both, 128)] = jnp.where(lane < 64, coarse, fine)

        @pl.loop(0, both // 256)
        def _(tile):
            cols = pl.ds(pl.multiple_of(tile * 256, 256), 256)
            total = jnp.dot(
                own_x[place, :], weight[pl.ds(0, feats), cols], preferred_element_type=jnp.float32
            )
            total += jnp.dot(
                sib_x[place, :],
                weight[pl.ds(feats, feats), cols],
                preferred_element_type=jnp.float32,
            )
            part[turn, :, cols] = total.astype(jnp.bfloat16)

        for way in range(2):
            far_copy(turn, way).start()
        for way in range(2):
            sum_copy(turn, way).start()

    def relay(turn):
        for way in range(2):
            far_copy(turn, way).wait_recv()
            joined[turn, way] = (
                piece(turn, near(way), way)[...].astype(jnp.float32)
                + relayed[turn, way].astype(jnp.float32)
            ).astype(jnp.bfloat16)
            join_copy(turn, way).start()

    def middle(turn):
        total = part[turn, pl.ds(pl.multiple_of(z * rows, rows), rows), :].astype(jnp.float32)
        for way in range(2):
            sum_copy(turn, way).wait_recv()
            join_copy(turn, way).wait_recv()
            total += sums[turn, way].astype(jnp.float32)
        square = total[:, both : both + 1] + total[:, both + 64 : both + 65]
        scale = lax.rsqrt(square * (1.0 / (8 * feats)) + EPS)
        gate = total[:, :half] * scale
        up = total[:, half:both] * scale
        hidden[turn, core, z] = (gate / (1.0 + jnp.exp(-gate)) * up).astype(jnp.bfloat16)
        for way in range(2):
            hid_copy(turn, way, z).start()
        hid_pass(turn, z).start()

    def lap(turn):
        for way in range(2):
            slot = near(1 - way)
            hid_copy(turn, way, slot).wait_recv()
            lap_copy(turn, way, slot).start()
            hid_pass(turn, slot).start()

    def back(turn):
        for way in range(2):
            lap_copy(turn, way, z_peer(2)).wait_recv()
        hid_pass(turn, z_peer(2)).start()
        for k in range(4):
            hid_passed(turn, z_peer(k)).wait_recv()
        place = pl.ds(pl.multiple_of(turn * group, group), group)

        @pl.loop(0, feats // 256)
        def _(tile):
            cols = pl.ds(pl.multiple_of(tile * 256, 256), 256)
            total = jnp.dot(
                hidden[turn, 0].reshape(group, half),
                down[pl.ds(0, half), cols],
                preferred_element_type=jnp.float32,
            )
            total += jnp.dot(
                hidden[turn, 1].reshape(group, half),
                down[pl.ds(half, half), cols],
                preferred_element_type=jnp.float32,
            )
            delta[place, cols] = total.astype(jnp.bfloat16)

        for k in range(4):
            dx, dy = 0, 0
            for t in range(4):
                dx = jnp.where(turn == t, OFFSETS[4 * t + k][0], dx)
                dy = jnp.where(turn == t, OFFSETS[4 * t + k][1], dy)
            who = lax.rem(x + dx, 4) * 4 + lax.rem(y + dy, 4)
            if k > 0:
                out_copy(turn * 4 + k, who).start()
            else:

                @pl.when(turn > 0)
                def _():
                    out_copy(turn * 4, who).start()

    @pl.loop(0, 8)
    def _(step):
        for late, stage in enumerate((front, relay, middle, lap, back)):

            @pl.when((step >= late) & (step < late + 4))
            def _():
                stage(step - late)

    total_ref[...] = share_ref[...] + delta[0:rows, :].astype(jnp.float32)

    @pl.loop(1, 16)
    def _(k):
        out_in(k).wait_recv()
        total_ref[...] += deltas[k].astype(jnp.float32)

    update = (score_ref[:, 0:1] * total_ref[...]).astype(jnp.bfloat16)
    slot_at = lax.broadcasted_iota(jnp.int32, (slots, rows), 0)
    give = jnp.where(slot_at == take_ref[0:1, :], 1.0, 0.0).astype(jnp.bfloat16)
    outbox[...] = jnp.dot(give, update, preferred_element_type=jnp.float32).astype(jnp.bfloat16)

    def box_of(who):
        return pl.ds(pl.multiple_of(who * box, box), box)

    def box_copy(k):
        who = ahead(c, k)
        return remote(
            outbox.at[box_of(who)], inbox.at[box_of(c)], box_send.at[k], box_recv.at[c], (who, m)
        )

    def box_in(who):
        return remote(
            outbox.at[box_of(who)], inbox.at[box_of(who)], box_send.at[0], box_recv.at[who], sibling
        )

    for k in range(1, 16):
        box_copy(k).start()

    inbox[box_of(c), :] = outbox[box_of(c), :]
    slot_at = lax.broadcasted_iota(jnp.int32, (tokens_ref.shape[0], slots), 1)
    back_to = jnp.where(slot_at == send_ref[:, 0:1], 1.0, 0.0).astype(jnp.bfloat16)

    for k in range(1, 16):
        box_in(ahead(c, k)).wait_recv()

    @pl.loop(0, feats // 256)
    def _(tile):
        cols = pl.ds(pl.multiple_of(tile * 256, 256), 256)
        arrived = jnp.dot(back_to, inbox[:, cols], preferred_element_type=jnp.float32)
        out_ref[:, cols] = (tokens_ref[:, cols].astype(jnp.float32) + arrived).astype(jnp.bfloat16)

    for k in range(1, 16):
        x_copy(k).wait_send()
        out_in(k).wait_send()
        box_copy(k).wait_send()

    @pl.loop(0, 16)
    def _(who):
        x_pass(who).wait_send()

    @pl.loop(0, 4)
    def _(turn):
        for way in range(2):
            far_copy(turn, way).wait_send()
            sum_copy(turn, way).wait_send()
            join_copy(turn, way).wait_send()
            hid_copy(turn, way, z).wait_send()
            lap_copy(turn, way, near(1 - way)).wait_send()
        for k in range(4):
            hid_pass(turn, z_peer(k)).wait_send()


def feed_forward(scaled, share, score, take, send, tokens, inv_gain, gate_weight, up_weight, gate_half, up_half, down_weight):
    rows, feats = scaled.shape
    cols = gate_weight.shape[1]
    half = cols // 2
    dma = pltpu.SemaphoreType.DMA
    bf16 = jnp.bfloat16
    vmem, anywhere = pl.BlockSpec(memory_space=pltpu.VMEM), pl.BlockSpec(memory_space=pl.ANY)
    return pl.pallas_call(
        mlp_kernel,
        out_shape=jax.ShapeDtypeStruct(tokens.shape, bf16),
        in_specs=[vmem] * 7 + [anywhere] * 5,
        out_specs=vmem,
        scratch_shapes=[
            pltpu.VMEM((16 * rows, feats), bf16),
            pltpu.VMEM((16 * rows, feats), bf16),
            pltpu.VMEM((8, feats), jnp.float32),
            pltpu.VMEM((2 * feats, cols), bf16),
            pltpu.VMEM((cols, feats), bf16),
            pltpu.VMEM((4, 4 * rows, cols + 128), bf16),
            pltpu.VMEM((4, 2, rows // 2, cols + 128), bf16),
            pltpu.VMEM((4, 2, rows // 2, cols + 128), bf16),
            pltpu.VMEM((4, 2, rows, cols + 128), bf16),
            pltpu.VMEM((4, 2, 4, rows, half), bf16),
            pltpu.VMEM((16 * rows, feats), bf16),
            pltpu.VMEM((16, rows, feats), bf16),
            pltpu.VMEM((rows, feats), jnp.float32),
            pltpu.VMEM((16 * BOX, feats), bf16),
            pltpu.VMEM((16 * BOX, feats), bf16),
            dma((5,)),
            dma((1,)),
            dma((1,)),
        ]
        + [dma((16,))] * 20,
        compiler_params=pltpu.CompilerParams(
            collective_id=3, has_side_effects=True, vmem_limit_bytes=56 * 2**20
        ),
        name="feed_forward",
    )(scaled, share, score, take, send, tokens, inv_gain, gate_weight, up_weight, gate_half, up_half, down_weight)


def attend_kernel(
    tokens_ref,
    send_ref,
    take_ref,
    gain_ref,
    router_ref,
    query_ref,
    key_ref,
    value_ref,
    out_weight_ref,
    gate_ref,
    up_ref,
    cosine_ref,
    sine_ref,
    mlp_gain_ref,
    share_ref,
    scaled_ref,
    score_ref,
    gate_half_ref,
    up_half_ref,
    outbox,
    inbox,
    full,
    normed,
    blocks,
    weight,
    out_weight,
    part,
    parts,
    key_value,
    attended,
    delta,
    deltas,
    load_sem,
    swap_send,
    swap_recv,
    box_send,
    box_recv,
    row_send,
    row_recv,
    hop_send,
    hop_recv,
    norm_send,
    norm_recv,
    part_send,
    part_recv,
    kv_send,
    kv_recv,
    att_send,
    att_recv,
    out_send,
    out_recv,
):
    rows, feats = share_ref.shape
    width = blocks.shape[1]
    slots = outbox.shape[0]
    box = slots // 16
    group = 4 * rows
    q_cols, kv_cols = query_ref.shape[1], key_ref.shape[1]
    heads = q_cols // HEAD_DIM
    c, m = lax.axis_index("ctx"), lax.axis_index("mp")
    x, y = c // 4, c % 4
    home = c // 2
    z, core = m // 2, m % 2
    sibling = (c, z * 2 + 1 - core)

    def rows_of(who, count=1):
        return pl.ds(pl.multiple_of(who * (rows * count), rows), rows * count)

    is_home = m == home
    barrier = pltpu.get_barrier_semaphore()

    @pl.loop(0, 16)
    def _(k):
        @pl.when(jnp.logical_not(is_home & (k // 8 == c % 2) & (k % 8 == m)))
        def _():
            pl.semaphore_signal(
                barrier, inc=1, device_id=(2 * m + k // 8, k % 8), device_id_type=MESH
            )

    for k in range(1, 16):
        pl.semaphore_signal(barrier, inc=1, device_id=(ahead(c, k), m), device_id_type=MESH)
    for k in range(1, 4):
        pl.semaphore_signal(
            barrier,
            inc=1,
            device_id=(c, lax.rem(z + k, 4) * 2 + core),
            device_id_type=MESH,
        )
    pl.semaphore_signal(barrier, inc=1, device_id=sibling, device_id_type=MESH)

    loads = [
        pltpu.make_async_copy(query_ref, weight.at[:, pl.ds(0, q_cols)], load_sem.at[0]),
        pltpu.make_async_copy(key_ref, weight.at[:, pl.ds(q_cols, kv_cols)], load_sem.at[1]),
        pltpu.make_async_copy(
            value_ref, weight.at[:, pl.ds(q_cols + kv_cols, kv_cols)], load_sem.at[2]
        ),
        pltpu.make_async_copy(out_weight_ref, out_weight, load_sem.at[3]),
    ]
    for load in loads:
        load.start()

    slot_at = lax.broadcasted_iota(jnp.int32, (slots, tokens_ref.shape[0]), 0)
    pick = jnp.where(slot_at == send_ref[0:1, :], 1.0, 0.0).astype(jnp.bfloat16)

    @pl.loop(0, feats // 256)
    def _(tile):
        cols = pl.ds(pl.multiple_of(tile * 256, 256), 256)
        outbox[:, cols] = jnp.dot(
            pick, tokens_ref[:, cols], preferred_element_type=jnp.float32
        ).astype(jnp.bfloat16)

    def box_of(who):
        return pl.ds(pl.multiple_of(who * box, box), box)

    inbox[box_of(c), :] = outbox[box_of(c), :]
    pl.semaphore_wait(barrier, jnp.where(is_home, 34, 35))

    def box_copy(k):
        who = ahead(c, k)
        return remote(
            outbox.at[box_of(who)], inbox.at[box_of(c)], box_send.at[k], box_recv.at[c], (who, m)
        )

    def box_in(who):
        return remote(
            outbox.at[box_of(who)], inbox.at[box_of(who)], box_send.at[0], box_recv.at[who], sibling
        )

    for k in range(1, 16):
        box_copy(k).start()
    for k in range(1, 16):
        box_in(ahead(c, k)).wait_recv()

    slot_at = lax.broadcasted_iota(jnp.int32, (rows, slots), 1)
    take = jnp.where(slot_at == take_ref[:, 0:1], 1.0, 0.0).astype(jnp.bfloat16)
    full[m] = jnp.dot(take, inbox[...], preferred_element_type=jnp.float32).astype(jnp.bfloat16)

    def row_copy(k, who):
        return remote(
            full.at[who],
            full.at[who],
            row_send.at[k],
            row_recv.at[who],
            (c, lax.rem(z + k, 4) * 2 + core),
        )

    def hop(who):
        return remote(full.at[who], full.at[who], hop_send.at[who], hop_recv.at[who], sibling)

    def z_block(k):
        return lax.rem(z + k, 4) * 2 + core

    def z_sibling(k):
        return lax.rem(z + k, 4) * 2 + 1 - core

    for k in (2, 1, 3):
        row_copy(k, m).start()
    hop(m).start()
    for k in (1, 3, 2):
        row_copy(k, z_block(k)).wait_recv()
        hop(z_block(k)).start()
    for k in (0, 1, 3, 2):
        hop(z_sibling(k)).wait_recv()

    square, route = 0.0, 0.0
    for at in range(8):
        wide = full[at].astype(jnp.float32)
        square += jnp.sum(wide * wide, axis=1, keepdims=True)
        route += jnp.sum(wide * router_ref[at : at + 1, :], axis=1, keepdims=True)
    scale = lax.rsqrt(square * (1.0 / (8 * feats)) + EPS)
    score_ref[...] = jnp.broadcast_to(1.0 / (1.0 + jnp.exp(-route)), score_ref.shape)
    for at in range(8):
        wide = full[at].astype(jnp.float32) * scale * gain_ref[at : at + 1, :]
        wide = wide.astype(jnp.bfloat16)
        normed[2 * at] = wide[:, :width]
        normed[2 * at + 1] = wide[:, width:]

    def norm_copy(k):
        who = behind(c, k)
        return remote(
            normed.at[who], blocks.at[rows_of(k)], norm_send.at[k], norm_recv.at[k], (who, m)
        )

    def norm_in(slot):
        return remote(
            normed.at[0], blocks.at[rows_of(slot)], norm_send.at[slot], norm_recv.at[slot], sibling
        )

    for k in range(1, 16):
        norm_copy(k).start()
    blocks[0:rows, :] = normed[c]
    half = gate_half_ref.shape[1]
    others = pl.ds(pl.multiple_of((1 - core) * half, 128), half)
    swaps = [
        remote(gate_ref.at[:, others], gate_half_ref, swap_send.at[0], swap_recv.at[0], sibling),
        remote(up_ref.at[:, others], up_half_ref, swap_send.at[1], swap_recv.at[1], sibling),
    ]
    for swap in swaps:
        swap.start()
    for load in loads:
        load.wait()

    def part_copy(k):
        return remote(
            part.at[rows_of(k)], parts.at[k], part_send.at[k], part_recv.at[k], (ahead(c, k), m)
        )

    for turn in range(4):
        for k in range(max(4 * turn, 1), 4 * turn + 4):
            norm_in(k).wait_recv()
        here = rows_of(turn, 4)
        part[here, :] = jnp.dot(
            blocks[here, :], weight[...], preferred_element_type=jnp.float32
        ).astype(jnp.bfloat16)
        for k in range(max(4 * turn, 1), 4 * turn + 4):
            part_copy(k).start()

    for at in range(0, weight.shape[1], HEAD_DIM):
        total_at = part[0:rows, at : at + HEAD_DIM]
        share_ref[:, at : at + HEAD_DIM] = total_at.astype(jnp.float32)

    @pl.loop(1, 16)
    def _(k):
        remote(
            part.at[0:rows], parts.at[k], part_send.at[k], part_recv.at[k], sibling
        ).wait_recv()
        share_ref[:, 0 : weight.shape[1]] += parts[k].astype(jnp.float32)

    def turned(at):
        head = share_ref[:, at : at + HEAD_DIM]
        swapped = pltpu.roll(head, HEAD_DIM // 2, 1)
        return (head * cosine_ref[...] + swapped * sine_ref[...]).astype(jnp.bfloat16)

    mine = rows_of(c)
    key_value[mine, 0:HEAD_DIM] = turned(q_cols)
    at = q_cols + kv_cols
    key_value[mine, HEAD_DIM : 2 * HEAD_DIM] = share_ref[:, at : at + HEAD_DIM].astype(jnp.bfloat16)

    def kv_copy(k, who, device):
        return remote(
            key_value.at[rows_of(who)],
            key_value.at[rows_of(who)],
            kv_send.at[k],
            kv_recv.at[who],
            device,
        )

    for k in range(1, 16):
        kv_copy(k, c, (behind(c, k), m)).start()

    queries = jnp.concatenate([turned(h * HEAD_DIM) for h in range(heads)], axis=0)

    for k in range(1, 16):
        kv_copy(k, ahead(c, k), sibling).wait_recv()

    keys = 16 * rows
    scores = lax.dot_general(
        queries,
        key_value[:, 0:HEAD_DIM],
        (((1,), (1,)), ((), ())),
        preferred_element_type=jnp.float32,
    ) * (HEAD_DIM ** (-0.5))
    query_at = lax.broadcasted_iota(jnp.int32, (heads * rows, keys), 0) % rows * 16 + c
    key_at = lax.broadcasted_iota(jnp.int32, (heads * rows, keys), 1)
    allowed = key_at % rows * 16 + key_at // rows <= query_at
    scores = jnp.where(allowed, scores, -1e30)
    weights = jnp.exp(scores - jnp.max(scores, axis=1, keepdims=True))
    weights = jnp.where(allowed, weights, 0.0)
    total = jnp.sum(weights, axis=1, keepdims=True)
    mixed = (
        jnp.dot(
            weights.astype(jnp.bfloat16),
            key_value[:, HEAD_DIM : 2 * HEAD_DIM],
            preferred_element_type=jnp.float32,
        )
        / total
    ).astype(jnp.bfloat16)
    for h in range(heads):
        attended[0:rows, h * HEAD_DIM : (h + 1) * HEAD_DIM] = mixed[h * rows : (h + 1) * rows]

    def att_copy(k):
        return remote(
            attended.at[0:rows],
            attended.at[rows_of(k)],
            att_send.at[k],
            att_recv.at[k],
            (behind(c, k), m),
        )

    for k in range(1, 16):
        att_copy(k).start()

    my_slot = (c % 2) * 8 + m

    def out_copy(k, who):
        return remote(
            delta.at[rows_of(k)],
            deltas.at[my_slot],
            out_send.at[k],
            out_recv.at[my_slot],
            (who, home),
        )

    def out_in(slot):
        return remote(
            delta.at[pl.ds(0, rows)],
            deltas.at[slot],
            out_send.at[slot],
            out_recv.at[slot],
            (2 * m + slot // 8, slot % 8),
        )

    for turn in range(4):
        for k in range(max(4 * turn, 1), 4 * turn + 4):
            att_copy(k).wait_recv()
        here = rows_of(turn, 4)
        delta[here, :] = jnp.dot(
            attended[here, :], out_weight[...], preferred_element_type=jnp.float32
        ).astype(jnp.bfloat16)
        for k in range(4 * turn, 4 * turn + 4):
            if k > 0:
                out_copy(k, ahead(c, k)).start()
            else:

                @pl.when(jnp.logical_not(is_home))
                def _():
                    out_copy(0, c).start()

    @pl.when(is_home)
    def _():
        deltas[my_slot] = delta[0:rows, :]

    share_ref[...] = jnp.zeros_like(share_ref)

    for side in range(2):

        @pl.loop(0, 8)
        def _(k):
            slot = side * 8 + lax.rem(k + m, 8)

            @pl.when(jnp.logical_not(is_home & (slot == my_slot)))
            def _():
                out_in(slot).wait_recv()

            share_ref[:, side * width : (side + 1) * width] += deltas[slot].astype(jnp.float32)

    mixed = full[m].astype(jnp.float32) + share_ref[...]
    scaled_ref[...] = (mixed * mlp_gain_ref[0:1, :]).astype(jnp.bfloat16)

    for k in range(1, 4):
        row_copy(k, m).wait_send()
    for k in range(4):
        hop(z_block(k)).wait_send()

    for swap in swaps:
        swap.wait()

    @pl.when(jnp.logical_not(is_home))
    def _():
        out_copy(0, c).wait_send()

    for k in range(1, 16):
        out_copy(k, ahead(c, k)).wait_send()
        box_copy(k).wait_send()
        norm_copy(k).wait_send()
        part_copy(k).wait_send()
        kv_copy(k, c, sibling).wait_send()
        att_copy(k).wait_send()


def attend(
    tokens, send, take, gain, router, query, key, value, out_weight, gate, up, cosine, sine, mlp_gain
):
    count, slots = take.shape[0], 16 * BOX
    feats = tokens.shape[1]
    width = query.shape[0]
    cols = query.shape[1] + key.shape[1] + value.shape[1]
    out_cols = out_weight.shape[1]
    dma = pltpu.SemaphoreType.DMA
    bf16 = jnp.bfloat16
    vmem, anywhere = pl.BlockSpec(memory_space=pltpu.VMEM), pl.BlockSpec(memory_space=pl.ANY)
    return pl.pallas_call(
        attend_kernel,
        out_shape=(
            jax.ShapeDtypeStruct((count, feats), jnp.float32),
            jax.ShapeDtypeStruct((count, feats), bf16),
            jax.ShapeDtypeStruct((count, 128), jnp.float32),
            jax.ShapeDtypeStruct((gate.shape[0], gate.shape[1] // 2), bf16),
            jax.ShapeDtypeStruct((up.shape[0], up.shape[1] // 2), bf16),
        ),
        in_specs=[vmem] * 5 + [anywhere] * 6 + [vmem] * 3,
        out_specs=(vmem, vmem, vmem, anywhere, anywhere),
        scratch_shapes=[
            pltpu.VMEM((slots, feats), bf16),
            pltpu.VMEM((slots, feats), bf16),
            pltpu.VMEM((8, count, feats), bf16),
            pltpu.VMEM((16, count, width), bf16),
            pltpu.VMEM((16 * count, width), bf16),
            pltpu.VMEM((width, cols), bf16),
            pltpu.VMEM(out_weight.shape, bf16),
            pltpu.VMEM((16 * count, cols), bf16),
            pltpu.VMEM((16, count, cols), bf16),
            pltpu.VMEM((16 * count, 2 * HEAD_DIM), bf16),
            pltpu.VMEM((16 * count, query.shape[1]), bf16),
            pltpu.VMEM((16 * count, out_cols), bf16),
            pltpu.VMEM((16, count, out_cols), bf16),
            dma((4,)),
            dma((2,)),
            dma((2,)),
        ]
        + [dma((16,))] * 16,
        compiler_params=pltpu.CompilerParams(
            collective_id=2, has_side_effects=True, vmem_limit_bytes=48 * 2**20
        ),
        name="attend",
    )(tokens, send, take, gain, router, query, key, value, out_weight, gate, up, cosine, sine, mlp_gain)


def body(
    tokens,
    norm_gain,
    router_weight,
    query_weight,
    key_weight,
    value_weight,
    out_weight,
    mlp_gain,
    gate_weight,
    up_weight,
    down_weight,
    destination,
    kept_pos,
):
    ctx_count = lax.axis_size("ctx")
    tok_dev = tokens.shape[0]
    kept_dev = kept_pos.shape[0]
    feature_cols = tokens.shape[1]
    capacity = BOX
    slots_all = ctx_count * capacity
    peer_ids = jnp.arange(ctx_count, dtype=jnp.int32)
    is_kept = destination >= 0
    owner_ids = destination // kept_dev
    slot_ids = destination % kept_dev
    kept_order = slot_ids * ctx_count + owner_ids
    first_order = jnp.min(jnp.where(is_kept, kept_order, ctx_count * kept_dev))
    first_slots = (first_order - peer_ids + ctx_count - 1) // ctx_count
    owner_match = owner_ids[:, None] == peer_ids[None, :]
    send_index = (
        owner_ids * capacity
        + slot_ids
        - jnp.sum(jnp.where(owner_match, first_slots[None, :], 0), axis=1)
    )
    send_index = jnp.where(is_kept, send_index, slots_all)
    slot_range = jnp.arange(kept_dev, dtype=jnp.int32)
    source_ids = kept_pos // tok_dev
    source_match = source_ids[:, None] == peer_ids[None, :]
    first_from = jnp.min(jnp.where(source_match, slot_range[:, None], kept_dev), axis=0)
    recv_index = (
        source_ids * capacity
        + slot_range
        - jnp.sum(jnp.where(source_match, first_from[None, :], 0), axis=1)
    )
    half_dim = HEAD_DIM // 2
    exponent = jnp.arange(half_dim, dtype=jnp.float32) * (2.0 / HEAD_DIM)
    angles = kept_pos.astype(jnp.float32)[:, None] * (500000.0 ** (-exponent))[None, :]
    cosine, sine = jnp.cos(angles), jnp.sin(angles)
    later_gain = mlp_gain.astype(jnp.float32)
    head_share, scaled, score, gate_half, up_half = attend(
        tokens,
        jnp.broadcast_to(send_index, (8, tok_dev)),
        jnp.broadcast_to(recv_index[:, None], (kept_dev, 128)),
        norm_gain.astype(jnp.float32).reshape(8, feature_cols),
        router_weight.astype(jnp.float32).reshape(8, feature_cols),
        query_weight,
        key_weight,
        value_weight,
        out_weight,
        gate_weight,
        up_weight,
        jnp.concatenate([cosine, cosine], axis=1),
        jnp.concatenate([-sine, sine], axis=1),
        jnp.broadcast_to(later_gain, (8, feature_cols)),
    )
    return feed_forward(
        scaled,
        head_share,
        score,
        jnp.broadcast_to(recv_index, (8, kept_dev)),
        jnp.broadcast_to(send_index[:, None], (tok_dev, 128)),
        tokens,
        jnp.broadcast_to(1.0 / later_gain, (8, feature_cols)),
        gate_weight,
        up_weight,
        gate_half,
        up_half,
        down_weight,
    )


def solution(mesh):
    in_specs = (
        P("ctx", "mp"),
        P(),
        P(),
        P("ctx", "mp"),
        P("ctx", "mp"),
        P("ctx", "mp"),
        P("mp", "ctx"),
        P("mp"),
        P("mp", "ctx"),
        P("mp", "ctx"),
        P("ctx", "mp"),
        P("ctx"),
        P("ctx"),
    )
    out_specs = P("ctx", "mp")
    return jax.shard_map(body, mesh=mesh, in_specs=in_specs, out_specs=out_specs, check_vma=False)
```

```python
import jax
import jax.numpy as jnp
from jax import lax
from jax.sharding import PartitionSpec as P

from jax.experimental import pallas as pl
from jax.experimental.pallas import tpu as pltpu

HEAD_DIM = 128
BOX = 16
MESH = pl.DeviceIdType.MESH
OFFSETS = (
    (0, 0), (0, 1), (1, 0), (0, 3), (3, 0), (1, 1), (3, 3), (1, 3),
    (3, 1), (0, 2), (2, 0), (1, 2), (2, 1), (3, 2), (2, 3), (2, 2),
)
EPS = 1e-05


def ahead(c, k):
    dx, dy = OFFSETS[k]
    return lax.rem(c // 4 + dx, 4) * 4 + lax.rem(c % 4 + dy, 4)


def behind(c, k):
    dx, dy = OFFSETS[k]
    return lax.rem(c // 4 + 4 - dx, 4) * 4 + lax.rem(c % 4 + 4 - dy, 4)


def remote(source, target, sent, landed, device):
    return pltpu.make_async_remote_copy(
        src_ref=source,
        dst_ref=target,
        send_sem=sent,
        recv_sem=landed,
        device_id=device,
        device_id_type=MESH,
    )


def mlp_kernel(
    x_ref,
    share_ref,
    score_ref,
    take_ref,
    send_ref,
    tokens_ref,
    inv_gain_ref,
    gate_ref,
    up_ref,
    gate_half_ref,
    up_half_ref,
    down_ref,
    out_ref,
    own_x,
    sib_x,
    sib_gain,
    weight,
    down,
    part,
    relayed,
    joined,
    sums,
    hidden,
    delta,
    deltas,
    total_ref,
    outbox,
    inbox,
    load_sem,
    swap_send,
    swap_recv,
    x_send,
    x_recv,
    pass_send,
    pass_recv,
    far_send,
    far_recv,
    sum_send,
    sum_recv,
    join_send,
    join_recv,
    hid_send,
    hid_recv,
    lap_send,
    lap_recv,
    hop_send,
    hop_recv,
    out_send,
    out_recv,
    box_send,
    box_recv,
):
    rows, feats = x_ref.shape
    slots = outbox.shape[0]
    box = slots // 16
    half = gate_ref.shape[1] // 2
    both = 2 * half
    group = 4 * rows
    c, m = lax.axis_index("ctx"), lax.axis_index("mp")
    x, y = c // 4, c % 4
    z, core = m // 2, m % 2
    sibling = (c, z * 2 + 1 - core)

    def z_peer(step):
        return lax.rem(z + step, 4)

    barrier = pltpu.get_barrier_semaphore()

    for k in range(1, 16):
        pl.semaphore_signal(barrier, inc=1, device_id=(ahead(c, k), m), device_id_type=MESH)

    for k in (1, 3):
        pl.semaphore_signal(
            barrier, inc=1, device_id=(c, z_peer(k) * 2 + core), device_id_type=MESH
        )
    pl.semaphore_signal(barrier, inc=1, device_id=sibling, device_id_type=MESH)

    mine = pl.multiple_of(core * half, 128)
    loads = [
        pltpu.make_async_copy(
            gate_ref.at[:, pl.ds(mine, half)],
            weight.at[pl.ds(0, feats), pl.ds(0, half)],
            load_sem.at[0],
        ),
        pltpu.make_async_copy(
            up_ref.at[:, pl.ds(mine, half)],
            weight.at[pl.ds(0, feats), pl.ds(half, half)],
            load_sem.at[1],
        ),
        pltpu.make_async_copy(
            gate_half_ref, weight.at[pl.ds(feats, feats), pl.ds(0, half)], load_sem.at[2]
        ),
        pltpu.make_async_copy(
            up_half_ref, weight.at[pl.ds(feats, feats), pl.ds(half, half)], load_sem.at[3]
        ),
        pltpu.make_async_copy(down_ref, down, load_sem.at[4]),
    ]
    for load in loads:
        load.start()
    own_x[0:rows, :] = x_ref[...]
    pl.semaphore_wait(barrier, 18)

    def x_copy(k):
        place = pl.ds(k * rows, rows)
        return remote(x_ref, own_x.at[place], x_send.at[k], x_recv.at[k], (behind(c, k), m))

    def x_in(slot):
        place = pl.ds(pl.multiple_of(slot * rows, rows), rows)
        return remote(x_ref, own_x.at[place], x_send.at[slot], x_recv.at[slot], sibling)

    def x_pass(who):
        place = pl.ds(pl.multiple_of(who * rows, rows), rows)
        return remote(
            own_x.at[place], sib_x.at[place], pass_send.at[who], pass_recv.at[who], sibling
        )

    for k in range(1, 4):
        x_copy(k).start()
    gain_swap = remote(inv_gain_ref, sib_gain, swap_send.at[0], swap_recv.at[0], sibling)
    x_pass(0).start()
    gain_swap.start()

    short = rows // 2

    def near(way):
        return z_peer(1 + 2 * way)

    def chip(way):
        return (c, near(way) * 2 + core)

    def piece(turn, to, side):
        return part.at[turn, pl.ds(pl.multiple_of(to * rows + side * short, short), short)]

    def far_copy(turn, way):
        at = turn * 2 + way
        return remote(
            piece(turn, z_peer(2), way),
            relayed.at[turn, way],
            far_send.at[at],
            far_recv.at[at],
            chip(way),
        )

    def sum_copy(turn, way):
        at = turn * 2 + way
        return remote(
            piece(turn, near(way), 1 - way),
            sums.at[turn, way, pl.ds((1 - way) * short, short)],
            sum_send.at[at],
            sum_recv.at[at],
            chip(way),
        )

    def join_copy(turn, way):
        at = turn * 2 + way
        return remote(
            joined.at[turn, way],
            sums.at[turn, way, pl.ds(way * short, short)],
            join_send.at[at],
            join_recv.at[at],
            chip(way),
        )

    def hid_copy(turn, way, slot):
        at = turn * 2 + way
        return remote(
            hidden.at[turn, core, slot],
            hidden.at[turn, core, slot],
            hid_send.at[at],
            hid_recv.at[at],
            chip(way),
        )

    def lap_copy(turn, way, slot):
        at = turn * 2 + way
        there = hidden.at[turn, core, slot, pl.ds(way * short, short)]
        return remote(there, there, lap_send.at[at], lap_recv.at[at], chip(way))

    def hid_pass(turn, at):
        return remote(
            hidden.at[turn, core, at],
            hidden.at[turn, core, at],
            hop_send.at[turn * 4 + at],
            hop_recv.at[turn * 4 + at],
            sibling,
        )

    def hid_passed(turn, at):
        return remote(
            hidden.at[turn, 1 - core, at],
            hidden.at[turn, 1 - core, at],
            hop_send.at[turn * 4 + at],
            hop_recv.at[turn * 4 + at],
            sibling,
        )

    def out_copy(slot, who):
        return remote(
            delta.at[pl.ds(pl.multiple_of(slot * rows, rows), rows)],
            deltas.at[slot],
            out_send.at[slot],
            out_recv.at[slot],
            (who, m),
        )

    def out_in(slot):
        return remote(
            delta.at[pl.ds(0, rows)], deltas.at[slot], out_send.at[slot], out_recv.at[slot], sibling
        )

    def front(turn):
        @pl.loop(0, 4)
        def _(k):
            slot = turn * 4 + k

            @pl.when(slot > 0)
            def _():
                x_in(slot).wait_recv()
                x_pass(slot).start()

        for t in range(3):

            @pl.when(turn == t)
            def _():
                for k in range(4 * t + 4, 4 * t + 8):
                    x_copy(k).start()

        @pl.when(turn == 0)
        def _():
            for load in loads:
                load.wait()
            gain_swap.wait()

        @pl.loop(0, 4)
        def _(k):
            x_pass(turn * 4 + k).wait_recv()

        place = pl.ds(pl.multiple_of(turn * group, group), group)
        mixed = own_x[place, :].astype(jnp.float32) * inv_gain_ref[0:1, :]
        square = jnp.sum(mixed * mixed, axis=1, keepdims=True)
        mixed = sib_x[place, :].astype(jnp.float32) * sib_gain[0:1, :]
        square = square + jnp.sum(mixed * mixed, axis=1, keepdims=True)
        square = jnp.broadcast_to(square, (group, 128))
        coarse = square.astype(jnp.bfloat16)
        fine = (square - coarse.astype(jnp.float32)).astype(jnp.bfloat16)
        lane = lax.broadcasted_iota(jnp.int32, (group, 128), 1)
        part[turn, :, pl.ds(both, 128)] = jnp.where(lane < 64, coarse, fine)

        @pl.loop(0, both // 256)
        def _(tile):
            cols = pl.ds(pl.multiple_of(tile * 256, 256), 256)
            total = jnp.dot(
                own_x[place, :], weight[pl.ds(0, feats), cols], preferred_element_type=jnp.float32
            )
            total += jnp.dot(
                sib_x[place, :],
                weight[pl.ds(feats, feats), cols],
                preferred_element_type=jnp.float32,
            )
            part[turn, :, cols] = total.astype(jnp.bfloat16)

        for way in range(2):
            far_copy(turn, way).start()
        for way in range(2):
            sum_copy(turn, way).start()

    def relay(turn):
        for way in range(2):
            far_copy(turn, way).wait_recv()
            joined[turn, way] = (
                piece(turn, near(way), way)[...].astype(jnp.float32)
                + relayed[turn, way].astype(jnp.float32)
            ).astype(jnp.bfloat16)
            join_copy(turn, way).start()

    def middle(turn):
        total = part[turn, pl.ds(pl.multiple_of(z * rows, rows), rows), :].astype(jnp.float32)
        for way in range(2):
            sum_copy(turn, way).wait_recv()
            join_copy(turn, way).wait_recv()
            total += sums[turn, way].astype(jnp.float32)
        square = total[:, both : both + 1] + total[:, both + 64 : both + 65]
        scale = lax.rsqrt(square * (1.0 / (8 * feats)) + EPS)
        gate = total[:, :half] * scale
        up = total[:, half:both] * scale
        hidden[turn, core, z] = (gate / (1.0 + jnp.exp(-gate)) * up).astype(jnp.bfloat16)
        for way in range(2):
            hid_copy(turn, way, z).start()
        hid_pass(turn, z).start()

    def lap(turn):
        for way in range(2):
            slot = near(1 - way)
            hid_copy(turn, way, slot).wait_recv()
            lap_copy(turn, way, slot).start()
            hid_pass(turn, slot).start()

    def back(turn):
        for way in range(2):
            lap_copy(turn, way, z_peer(2)).wait_recv()
        hid_pass(turn, z_peer(2)).start()
        for k in range(4):
            hid_passed(turn, z_peer(k)).wait_recv()
        place = pl.ds(pl.multiple_of(turn * group, group), group)

        @pl.loop(0, feats // 256)
        def _(tile):
            cols = pl.ds(pl.multiple_of(tile * 256, 256), 256)
            total = jnp.dot(
                hidden[turn, 0].reshape(group, half),
                down[pl.ds(0, half), cols],
                preferred_element_type=jnp.float32,
            )
            total += jnp.dot(
                hidden[turn, 1].reshape(group, half),
                down[pl.ds(half, half), cols],
                preferred_element_type=jnp.float32,
            )
            delta[place, cols] = total.astype(jnp.bfloat16)

        for k in range(4):
            dx, dy = 0, 0
            for t in range(4):
                dx = jnp.where(turn == t, OFFSETS[4 * t + k][0], dx)
                dy = jnp.where(turn == t, OFFSETS[4 * t + k][1], dy)
            who = lax.rem(x + dx, 4) * 4 + lax.rem(y + dy, 4)
            if k > 0:
                out_copy(turn * 4 + k, who).start()
            else:

                @pl.when(turn > 0)
                def _():
                    out_copy(turn * 4, who).start()

    @pl.loop(0, 8)
    def _(step):
        for late, stage in enumerate((front, relay, middle, lap, back)):

            @pl.when((step >= late) & (step < late + 4))
            def _():
                stage(step - late)

    total_ref[...] = share_ref[...] + delta[0:rows, :].astype(jnp.float32)

    @pl.loop(1, 16)
    def _(k):
        out_in(k).wait_recv()
        total_ref[...] += deltas[k].astype(jnp.float32)

    update = (score_ref[:, 0:1] * total_ref[...]).astype(jnp.bfloat16)
    slot_at = lax.broadcasted_iota(jnp.int32, (slots, rows), 0)
    give = jnp.where(slot_at == take_ref[0:1, :], 1.0, 0.0).astype(jnp.bfloat16)
    outbox[...] = jnp.dot(give, update, preferred_element_type=jnp.float32).astype(jnp.bfloat16)

    def box_of(who):
        return pl.ds(pl.multiple_of(who * box, box), box)

    def box_copy(k):
        who = ahead(c, k)
        return remote(
            outbox.at[box_of(who)], inbox.at[box_of(c)], box_send.at[k], box_recv.at[c], (who, m)
        )

    def box_in(who):
        return remote(
            outbox.at[box_of(who)], inbox.at[box_of(who)], box_send.at[0], box_recv.at[who], sibling
        )

    for k in range(1, 16):
        box_copy(k).start()

    inbox[box_of(c), :] = outbox[box_of(c), :]
    slot_at = lax.broadcasted_iota(jnp.int32, (tokens_ref.shape[0], slots), 1)
    back_to = jnp.where(slot_at == send_ref[:, 0:1], 1.0, 0.0).astype(jnp.bfloat16)

    for k in range(1, 16):
        box_in(ahead(c, k)).wait_recv()

    @pl.loop(0, feats // 256)
    def _(tile):
        cols = pl.ds(pl.multiple_of(tile * 256, 256), 256)
        arrived = jnp.dot(back_to, inbox[:, cols], preferred_element_type=jnp.float32)
        out_ref[:, cols] = (tokens_ref[:, cols].astype(jnp.float32) + arrived).astype(jnp.bfloat16)

    for k in range(1, 16):
        x_copy(k).wait_send()
        out_in(k).wait_send()
        box_copy(k).wait_send()

    @pl.loop(0, 16)
    def _(who):
        x_pass(who).wait_send()

    @pl.loop(0, 4)
    def _(turn):
        for way in range(2):
            far_copy(turn, way).wait_send()
            sum_copy(turn, way).wait_send()
            join_copy(turn, way).wait_send()
            hid_copy(turn, way, z).wait_send()
            lap_copy(turn, way, near(1 - way)).wait_send()
        for k in range(4):
            hid_pass(turn, z_peer(k)).wait_send()


def feed_forward(scaled, share, score, take, send, tokens, inv_gain, gate_weight, up_weight, gate_half, up_half, down_weight):
    rows, feats = scaled.shape
    cols = gate_weight.shape[1]
    half = cols // 2
    dma = pltpu.SemaphoreType.DMA
    bf16 = jnp.bfloat16
    vmem, anywhere = pl.BlockSpec(memory_space=pltpu.VMEM), pl.BlockSpec(memory_space=pl.ANY)
    return pl.pallas_call(
        mlp_kernel,
        out_shape=jax.ShapeDtypeStruct(tokens.shape, bf16),
        in_specs=[vmem] * 7 + [anywhere] * 5,
        out_specs=vmem,
        scratch_shapes=[
            pltpu.VMEM((16 * rows, feats), bf16),
            pltpu.VMEM((16 * rows, feats), bf16),
            pltpu.VMEM((8, feats), jnp.float32),
            pltpu.VMEM((2 * feats, cols), bf16),
            pltpu.VMEM((cols, feats), bf16),
            pltpu.VMEM((4, 4 * rows, cols + 128), bf16),
            pltpu.VMEM((4, 2, rows // 2, cols + 128), bf16),
            pltpu.VMEM((4, 2, rows // 2, cols + 128), bf16),
            pltpu.VMEM((4, 2, rows, cols + 128), bf16),
            pltpu.VMEM((4, 2, 4, rows, half), bf16),
            pltpu.VMEM((16 * rows, feats), bf16),
            pltpu.VMEM((16, rows, feats), bf16),
            pltpu.VMEM((rows, feats), jnp.float32),
            pltpu.VMEM((16 * BOX, feats), bf16),
            pltpu.VMEM((16 * BOX, feats), bf16),
            dma((5,)),
            dma((1,)),
            dma((1,)),
        ]
        + [dma((16,))] * 20,
        compiler_params=pltpu.CompilerParams(
            collective_id=3, has_side_effects=True, vmem_limit_bytes=56 * 2**20
        ),
        name="feed_forward",
    )(scaled, share, score, take, send, tokens, inv_gain, gate_weight, up_weight, gate_half, up_half, down_weight)


def attend_kernel(
    tokens_ref,
    send_ref,
    take_ref,
    gain_ref,
    router_ref,
    query_ref,
    key_ref,
    value_ref,
    out_weight_ref,
    gate_ref,
    up_ref,
    cosine_ref,
    sine_ref,
    mlp_gain_ref,
    share_ref,
    scaled_ref,
    score_ref,
    gate_half_ref,
    up_half_ref,
    outbox,
    inbox,
    full,
    normed,
    blocks,
    weight,
    out_weight,
    part,
    parts,
    key_value,
    attended,
    delta,
    deltas,
    load_sem,
    swap_send,
    swap_recv,
    box_send,
    box_recv,
    row_send,
    row_recv,
    hop_send,
    hop_recv,
    norm_send,
    norm_recv,
    wide_send,
    wide_recv,
    part_send,
    part_recv,
    kv_send,
    kv_recv,
    att_send,
    att_recv,
    out_send,
    out_recv,
):
    rows, feats = share_ref.shape
    width = query_ref.shape[0]
    slots = outbox.shape[0]
    box = slots // 16
    group = 4 * rows
    cols = weight.shape[1]
    q_cols, kv_cols = query_ref.shape[1], key_ref.shape[1]
    heads = q_cols // HEAD_DIM
    c, m = lax.axis_index("ctx"), lax.axis_index("mp")
    x, y = c // 4, c % 4
    z, core = m // 2, m % 2
    sibling = (c, z * 2 + 1 - core)

    def rows_of(who, count=1):
        return pl.ds(pl.multiple_of(who * (rows * count), rows), rows * count)

    is_home = x == z
    barrier = pltpu.get_barrier_semaphore()

    def x_peer(k):
        return (lax.rem(x + k, 4) * 4 + y, m)

    def y_peer(k):
        return (x * 4 + lax.rem(y + k, 4), m)

    @pl.loop(0, 8)
    def _(k):
        @pl.when(jnp.logical_not(is_home & (k == m)))
        def _():
            pl.semaphore_signal(barrier, inc=1, device_id=(z * 4 + y, k), device_id_type=MESH)

    for k in range(1, 16):
        pl.semaphore_signal(barrier, inc=1, device_id=(ahead(c, k), m), device_id_type=MESH)
    for k in range(1, 4):
        pl.semaphore_signal(
            barrier,
            inc=1,
            device_id=(c, lax.rem(z + k, 4) * 2 + core),
            device_id_type=MESH,
        )
    pl.semaphore_signal(barrier, inc=1, device_id=sibling, device_id_type=MESH)

    band = pl.ds(pl.multiple_of(y * width, width), width)
    loads = [
        pltpu.make_async_copy(query_ref, weight.at[band, pl.ds(0, q_cols)], load_sem.at[0]),
        pltpu.make_async_copy(key_ref, weight.at[band, pl.ds(q_cols, kv_cols)], load_sem.at[1]),
        pltpu.make_async_copy(
            value_ref, weight.at[band, pl.ds(q_cols + kv_cols, kv_cols)], load_sem.at[2]
        ),
        pltpu.make_async_copy(out_weight_ref, out_weight.at[y], load_sem.at[3]),
    ]
    for load in loads:
        load.start()

    slot_at = lax.broadcasted_iota(jnp.int32, (slots, tokens_ref.shape[0]), 0)
    pick = jnp.where(slot_at == send_ref[0:1, :], 1.0, 0.0).astype(jnp.bfloat16)

    @pl.loop(0, feats // 256)
    def _(tile):
        cols = pl.ds(pl.multiple_of(tile * 256, 256), 256)
        outbox[:, cols] = jnp.dot(
            pick, tokens_ref[:, cols], preferred_element_type=jnp.float32
        ).astype(jnp.bfloat16)

    def box_of(who):
        return pl.ds(pl.multiple_of(who * box, box), box)

    inbox[box_of(c), :] = outbox[box_of(c), :]
    pl.semaphore_wait(barrier, jnp.where(is_home, 26, 27))

    def box_copy(k):
        who = ahead(c, k)
        return remote(
            outbox.at[box_of(who)], inbox.at[box_of(c)], box_send.at[k], box_recv.at[c], (who, m)
        )

    def box_in(who):
        return remote(
            outbox.at[box_of(who)], inbox.at[box_of(who)], box_send.at[0], box_recv.at[who], sibling
        )

    def weight_copy(k):
        return remote(
            weight.at[band], weight.at[band], wide_send.at[k], wide_recv.at[k], y_peer(k)
        )

    def out_weight_copy(k):
        return remote(
            out_weight.at[y],
            out_weight.at[y],
            wide_send.at[4 + k],
            wide_recv.at[4 + k],
            y_peer(k),
        )

    def weight_lap(k):
        whose = lax.rem(y + 4 - k, 4)
        start = whose * width + (k // 2) * (width // 2)
        there = weight.at[pl.ds(pl.multiple_of(start, width // 2), width // 2)]
        return remote(there, there, wide_send.at[k - 1], wide_recv.at[k - 1], y_peer(k))

    def out_weight_lap(k):
        whose = lax.rem(y + 4 - k, 4)
        there = out_weight.at[whose, pl.ds((k // 2) * (width // 2), width // 2)]
        return remote(there, there, wide_send.at[k + 3], wide_recv.at[k + 3], y_peer(k))

    for k in range(1, 16):
        box_copy(k).start()
    for load in loads:
        load.wait()
    for k in (1, 3):
        weight_copy(k).start()
    for k in range(1, 16):
        box_in(ahead(c, k)).wait_recv()

    slot_at = lax.broadcasted_iota(jnp.int32, (rows, slots), 1)
    take = jnp.where(slot_at == take_ref[:, 0:1], 1.0, 0.0).astype(jnp.bfloat16)
    full[m] = jnp.dot(take, inbox[...], preferred_element_type=jnp.float32).astype(jnp.bfloat16)

    def row_copy(k, who):
        return remote(
            full.at[who],
            full.at[who],
            row_send.at[k],
            row_recv.at[who],
            (c, lax.rem(z + k, 4) * 2 + core),
        )

    def hop(who):
        return remote(full.at[who], full.at[who], hop_send.at[who], hop_recv.at[who], sibling)

    def z_block(k):
        return lax.rem(z + k, 4) * 2 + core

    def z_sibling(k):
        return lax.rem(z + k, 4) * 2 + 1 - core

    for k in (2, 1, 3):
        row_copy(k, m).start()
    hop(m).start()
    for k in (1, 3, 2):
        row_copy(k, z_block(k)).wait_recv()
        hop(z_block(k)).start()
    for k in (0, 1, 3, 2):
        hop(z_sibling(k)).wait_recv()

    for k in (1, 3):
        weight_copy(k).wait_recv()
        weight_lap(k).start()
    square, route = 0.0, 0.0
    for at in range(8):
        wide = full[at].astype(jnp.float32)
        square += jnp.sum(wide * wide, axis=1, keepdims=True)
        route += jnp.sum(wide * router_ref[at : at + 1, :], axis=1, keepdims=True)
    scale = lax.rsqrt(square * (1.0 / (8 * feats)) + EPS)
    score_ref[...] = jnp.broadcast_to(1.0 / (1.0 + jnp.exp(-route)), score_ref.shape)
    for at in range(8):
        wide = full[at].astype(jnp.float32) * scale * gain_ref[at : at + 1, :]
        wide = wide.astype(jnp.bfloat16)
        normed[at] = wide

    def norm_copy(k):
        to = lax.rem(x + 4 - k, 4)
        return remote(
            normed.at[pl.ds(2 * to, 2)],
            blocks.at[:, k],
            norm_send.at[k],
            norm_recv.at[k],
            (to * 4 + y, m),
        )

    for k in (1, 3, 2):
        norm_copy(k).start()
    blocks[0, 0] = normed[2 * x]
    blocks[1, 0] = normed[2 * x + 1]
    half = gate_half_ref.shape[1]
    others = pl.ds(pl.multiple_of((1 - core) * half, 128), half)
    swaps = [
        remote(gate_ref.at[:, others], gate_half_ref, swap_send.at[0], swap_recv.at[0], sibling),
        remote(up_ref.at[:, others], up_half_ref, swap_send.at[1], swap_recv.at[1], sibling),
    ]
    for swap in swaps:
        swap.start()

    def part_copy(k):
        return remote(part.at[rows_of(k)], parts.at[k], part_send.at[k], part_recv.at[k], x_peer(k))

    for k in (1, 3, 2):
        norm_copy(k).wait_recv()
    for k in (1, 3):
        weight_lap(k).wait_recv()
    for k in (1, 3):
        out_weight_copy(k).start()

    @pl.loop(0, cols // 256)
    def _(tile):
        at = pl.ds(pl.multiple_of(tile * 256, 256), 256)
        total = jnp.dot(
            blocks[0].reshape(group, feats),
            weight[pl.ds(0, feats), at],
            preferred_element_type=jnp.float32,
        )
        total += jnp.dot(
            blocks[1].reshape(group, feats),
            weight[pl.ds(feats, feats), at],
            preferred_element_type=jnp.float32,
        )
        part[:, at] = total.astype(jnp.bfloat16)
        share_ref[:, at] = total[0:rows]

    for k in (1, 3, 2):
        part_copy(k).start()
    for k in (1, 3, 2):
        part_copy(k).wait_recv()
        share_ref[:, 0:cols] += parts[k].astype(jnp.float32)

    def turned(at):
        head = share_ref[:, at : at + HEAD_DIM]
        swapped = pltpu.roll(head, HEAD_DIM // 2, 1)
        return (head * cosine_ref[...] + swapped * sine_ref[...]).astype(jnp.bfloat16)

    mine = rows_of(c)
    key_value[mine, 0:HEAD_DIM] = turned(q_cols)
    at = q_cols + kv_cols
    key_value[mine, HEAD_DIM : 2 * HEAD_DIM] = share_ref[:, at : at + HEAD_DIM].astype(jnp.bfloat16)

    def kv_copy(k, who, device):
        return remote(
            key_value.at[rows_of(who)],
            key_value.at[rows_of(who)],
            kv_send.at[k],
            kv_recv.at[who],
            device,
        )

    for k in range(1, 16):
        kv_copy(k, c, (behind(c, k), m)).start()

    queries = jnp.concatenate([turned(h * HEAD_DIM) for h in range(heads)], axis=0)

    for k in range(1, 16):
        kv_copy(k, ahead(c, k), sibling).wait_recv()
    for k in (1, 3):
        out_weight_copy(k).wait_recv()
        out_weight_lap(k).start()

    keys = 16 * rows
    scores = lax.dot_general(
        queries,
        key_value[:, 0:HEAD_DIM],
        (((1,), (1,)), ((), ())),
        preferred_element_type=jnp.float32,
    ) * (HEAD_DIM ** (-0.5))
    query_at = lax.broadcasted_iota(jnp.int32, (heads * rows, keys), 0) % rows * 16 + c
    key_at = lax.broadcasted_iota(jnp.int32, (heads * rows, keys), 1)
    allowed = key_at % rows * 16 + key_at // rows <= query_at
    scores = jnp.where(allowed, scores, -1e30)
    weights = jnp.exp(scores - jnp.max(scores, axis=1, keepdims=True))
    weights = jnp.where(allowed, weights, 0.0)
    total = jnp.sum(weights, axis=1, keepdims=True)
    mixed = (
        jnp.dot(
            weights.astype(jnp.bfloat16),
            key_value[:, HEAD_DIM : 2 * HEAD_DIM],
            preferred_element_type=jnp.float32,
        )
        / total
    ).astype(jnp.bfloat16)
    for h in range(heads):
        attended[0:rows, h * HEAD_DIM : (h + 1) * HEAD_DIM] = mixed[h * rows : (h + 1) * rows]

    def att_copy(k):
        to = lax.rem(x + 4 - k, 4)
        return remote(
            attended.at[0:rows],
            attended.at[rows_of(k)],
            att_send.at[k],
            att_recv.at[k],
            (to * 4 + y, m),
        )

    for k in (1, 3, 2):
        att_copy(k).start()

    def out_copy(k, side):
        return remote(
            delta.at[side, rows_of(k)],
            deltas.at[m],
            out_send.at[2 * k + side],
            out_recv.at[m],
            (lax.rem(x + k, 4) * 4 + y, 2 * x + side),
        )

    def out_in(slot):
        return remote(
            delta.at[0, pl.ds(0, rows)],
            deltas.at[slot],
            out_send.at[slot],
            out_recv.at[slot],
            sibling,
        )

    for k in (1, 3):
        out_weight_lap(k).wait_recv()
    for k in (1, 3, 2):
        att_copy(k).wait_recv()
    for side in range(2):
        for at in range(2):
            delta[side, :, at * width : (at + 1) * width] = jnp.dot(
                attended[...], out_weight[2 * side + at], preferred_element_type=jnp.float32
            ).astype(jnp.bfloat16)
        for k in (2, 1, 3):
            out_copy(k, side).start()

        @pl.when(jnp.logical_not(is_home & (side == core)))
        def _():
            out_copy(0, side).start()

    @pl.when(is_home)
    def _():
        deltas[m] = delta[core, 0:rows, :]

    share_ref[...] = jnp.zeros_like(share_ref)

    @pl.loop(0, 8)
    def _(k):
        slot = lax.rem(k + m, 8)

        @pl.when(jnp.logical_not(is_home & (slot == m)))
        def _():
            out_in(slot).wait_recv()

        share_ref[...] += deltas[slot].astype(jnp.float32)

    mixed = full[m].astype(jnp.float32) + share_ref[...]
    scaled_ref[...] = (mixed * mlp_gain_ref[0:1, :]).astype(jnp.bfloat16)

    for k in range(1, 4):
        row_copy(k, m).wait_send()
    for k in range(4):
        hop(z_block(k)).wait_send()

    for swap in swaps:
        swap.wait()

    for k in (1, 3):
        weight_copy(k).wait_send()
        weight_lap(k).wait_send()
        out_weight_copy(k).wait_send()
        out_weight_lap(k).wait_send()
    for side in range(2):
        for k in range(1, 4):
            out_copy(k, side).wait_send()

        @pl.when(jnp.logical_not(is_home & (side == core)))
        def _():
            out_copy(0, side).wait_send()

    for k in range(1, 4):
        norm_copy(k).wait_send()
        part_copy(k).wait_send()
        att_copy(k).wait_send()
    for k in range(1, 16):
        box_copy(k).wait_send()
        kv_copy(k, c, sibling).wait_send()


def attend(
    tokens, send, take, gain, router, query, key, value, out_weight, gate, up, cosine, sine, mlp_gain
):
    count, slots = take.shape[0], 16 * BOX
    feats = tokens.shape[1]
    width = query.shape[0]
    cols = query.shape[1] + key.shape[1] + value.shape[1]
    dma = pltpu.SemaphoreType.DMA
    bf16 = jnp.bfloat16
    vmem, anywhere = pl.BlockSpec(memory_space=pltpu.VMEM), pl.BlockSpec(memory_space=pl.ANY)
    return pl.pallas_call(
        attend_kernel,
        out_shape=(
            jax.ShapeDtypeStruct((count, feats), jnp.float32),
            jax.ShapeDtypeStruct((count, feats), bf16),
            jax.ShapeDtypeStruct((count, 128), jnp.float32),
            jax.ShapeDtypeStruct((gate.shape[0], gate.shape[1] // 2), bf16),
            jax.ShapeDtypeStruct((up.shape[0], up.shape[1] // 2), bf16),
        ),
        in_specs=[vmem] * 5 + [anywhere] * 6 + [vmem] * 3,
        out_specs=(vmem, vmem, vmem, anywhere, anywhere),
        scratch_shapes=[
            pltpu.VMEM((slots, feats), bf16),
            pltpu.VMEM((slots, feats), bf16),
            pltpu.VMEM((8, count, feats), bf16),
            pltpu.VMEM((8, count, feats), bf16),
            pltpu.VMEM((2, 4, count, feats), bf16),
            pltpu.VMEM((4 * width, cols), bf16),
            pltpu.VMEM((4, *out_weight.shape), bf16),
            pltpu.VMEM((4 * count, cols), bf16),
            pltpu.VMEM((4, count, cols), bf16),
            pltpu.VMEM((16 * count, 2 * HEAD_DIM), bf16),
            pltpu.VMEM((4 * count, query.shape[1]), bf16),
            pltpu.VMEM((2, 4 * count, feats), bf16),
            pltpu.VMEM((8, count, feats), bf16),
            dma((4,)),
            dma((2,)),
            dma((2,)),
        ]
        + [dma((16,))] * 18,
        compiler_params=pltpu.CompilerParams(
            collective_id=2, has_side_effects=True, vmem_limit_bytes=48 * 2**20
        ),
        name="attend",
    )(tokens, send, take, gain, router, query, key, value, out_weight, gate, up, cosine, sine, mlp_gain)


def body(
    tokens,
    norm_gain,
    router_weight,
    query_weight,
    key_weight,
    value_weight,
    out_weight,
    mlp_gain,
    gate_weight,
    up_weight,
    down_weight,
    destination,
    kept_pos,
):
    ctx_count = lax.axis_size("ctx")
    tok_dev = tokens.shape[0]
    kept_dev = kept_pos.shape[0]
    feature_cols = tokens.shape[1]
    capacity = BOX
    slots_all = ctx_count * capacity
    peer_ids = jnp.arange(ctx_count, dtype=jnp.int32)
    is_kept = destination >= 0
    owner_ids = destination // kept_dev
    slot_ids = destination % kept_dev
    kept_order = slot_ids * ctx_count + owner_ids
    first_order = jnp.min(jnp.where(is_kept, kept_order, ctx_count * kept_dev))
    first_slots = (first_order - peer_ids + ctx_count - 1) // ctx_count
    owner_match = owner_ids[:, None] == peer_ids[None, :]
    send_index = (
        owner_ids * capacity
        + slot_ids
        - jnp.sum(jnp.where(owner_match, first_slots[None, :], 0), axis=1)
    )
    send_index = jnp.where(is_kept, send_index, slots_all)
    slot_range = jnp.arange(kept_dev, dtype=jnp.int32)
    source_ids = kept_pos // tok_dev
    source_match = source_ids[:, None] == peer_ids[None, :]
    first_from = jnp.min(jnp.where(source_match, slot_range[:, None], kept_dev), axis=0)
    recv_index = (
        source_ids * capacity
        + slot_range
        - jnp.sum(jnp.where(source_match, first_from[None, :], 0), axis=1)
    )
    half_dim = HEAD_DIM // 2
    exponent = jnp.arange(half_dim, dtype=jnp.float32) * (2.0 / HEAD_DIM)
    angles = kept_pos.astype(jnp.float32)[:, None] * (500000.0 ** (-exponent))[None, :]
    cosine, sine = jnp.cos(angles), jnp.sin(angles)
    later_gain = mlp_gain.astype(jnp.float32)
    head_share, scaled, score, gate_half, up_half = attend(
        tokens,
        jnp.broadcast_to(send_index, (8, tok_dev)),
        jnp.broadcast_to(recv_index[:, None], (kept_dev, 128)),
        norm_gain.astype(jnp.float32).reshape(8, feature_cols),
        router_weight.astype(jnp.float32).reshape(8, feature_cols),
        query_weight,
        key_weight,
        value_weight,
        out_weight,
        gate_weight,
        up_weight,
        jnp.concatenate([cosine, cosine], axis=1),
        jnp.concatenate([-sine, sine], axis=1),
        jnp.broadcast_to(later_gain, (8, feature_cols)),
    )
    return feed_forward(
        scaled,
        head_share,
        score,
        jnp.broadcast_to(recv_index, (8, kept_dev)),
        jnp.broadcast_to(send_index[:, None], (tok_dev, 128)),
        tokens,
        jnp.broadcast_to(1.0 / later_gain, (8, feature_cols)),
        gate_weight,
        up_weight,
        gate_half,
        up_half,
        down_weight,
    )


def solution(mesh):
    in_specs = (
        P("ctx", "mp"),
        P(),
        P(),
        P("ctx", "mp"),
        P("ctx", "mp"),
        P("ctx", "mp"),
        P("mp", "ctx"),
        P("mp"),
        P("mp", "ctx"),
        P("mp", "ctx"),
        P("ctx", "mp"),
        P("ctx"),
        P("ctx"),
    )
    out_specs = P("ctx", "mp")
    return jax.shard_map(body, mesh=mesh, in_specs=in_specs, out_specs=out_specs, check_vma=False)
```

```python
import jax
import jax.numpy as jnp
from jax import lax
from jax.sharding import PartitionSpec as P

from jax.experimental import pallas as pl
from jax.experimental.pallas import tpu as pltpu

HEAD_DIM = 128
BOX = 16
VMEM_BYTES = 60 * 2**20
MESH = pl.DeviceIdType.MESH
OFFSETS = (
    (0, 0), (0, 1), (1, 0), (0, 3), (3, 0), (1, 1), (3, 3), (1, 3),
    (3, 1), (0, 2), (2, 0), (1, 2), (2, 1), (3, 2), (2, 3), (2, 2),
)
EPS = 1e-05


def ahead(c, k):
    dx, dy = OFFSETS[k]
    return lax.rem(c // 4 + dx, 4) * 4 + lax.rem(c % 4 + dy, 4)


def behind(c, k):
    dx, dy = OFFSETS[k]
    return lax.rem(c // 4 + 4 - dx, 4) * 4 + lax.rem(c % 4 + 4 - dy, 4)


def send_slots(destination, kept):
    owner, slot = destination // kept, destination % kept
    going = destination >= 0
    order = jnp.where(going, slot * 16 + owner, 16 * kept)
    first = (jnp.min(order) - owner + 15) // 16
    return jnp.where(going, owner * BOX + slot - first, 16 * BOX)


def take_slots(row, column, shard, axis):
    kept = row.shape[1]
    same = column // shard == row // shard
    at = lax.broadcasted_iota(jnp.int32, (kept, kept), axis)
    first = jnp.min(jnp.where(same, at, kept), axis=axis, keepdims=True)
    mine = row if axis == 0 else column
    return mine // shard * BOX + lax.broadcasted_iota(jnp.int32, mine.shape, 1 - axis) - first


def remote(source, target, sent, landed, device):
    return pltpu.make_async_remote_copy(
        src_ref=source,
        dst_ref=target,
        send_sem=sent,
        recv_sem=landed,
        device_id=device,
        device_id_type=MESH,
    )


def mlp_kernel(
    x_ref,
    share_ref,
    score_ref,
    kept_row_ref,
    kept_column_ref,
    destination_ref,
    gains_ref,
    gate_ref,
    up_ref,
    gate_half_ref,
    up_half_ref,
    down_ref,
    out_ref,
    own_x,
    sib_x,
    own_gain,
    sib_gain,
    weight,
    down,
    part,
    relayed,
    joined,
    sums,
    hidden,
    delta,
    deltas,
    total_ref,
    outbox,
    inbox,
    load_sem,
    swap_send,
    swap_recv,
    x_send,
    x_recv,
    pass_send,
    pass_recv,
    far_send,
    far_recv,
    sum_send,
    sum_recv,
    join_send,
    join_recv,
    hid_send,
    hid_recv,
    lap_send,
    lap_recv,
    hop_send,
    hop_recv,
    out_send,
    out_recv,
    box_send,
    box_recv,
):
    rows, feats = x_ref.shape
    slots = outbox.shape[0]
    box = slots // 16
    half = gate_ref.shape[1] // 2
    both = 2 * half
    group = 4 * rows
    c, m = lax.axis_index("ctx"), lax.axis_index("mp")
    x, y = c // 4, c % 4
    z, core = m // 2, m % 2
    sibling = (c, z * 2 + 1 - core)

    def z_peer(step):
        return lax.rem(z + step, 4)

    barrier = pltpu.get_barrier_semaphore()

    for k in range(1, 16):
        pl.semaphore_signal(barrier, inc=1, device_id=(ahead(c, k), m), device_id_type=MESH)

    for k in (1, 3):
        pl.semaphore_signal(
            barrier, inc=1, device_id=(c, z_peer(k) * 2 + core), device_id_type=MESH
        )
    pl.semaphore_signal(barrier, inc=1, device_id=sibling, device_id_type=MESH)

    mine = pl.multiple_of(core * half, 128)
    loads = [
        pltpu.make_async_copy(
            gate_ref.at[:, pl.ds(mine, half)],
            weight.at[pl.ds(0, feats), pl.ds(0, half)],
            load_sem.at[0],
        ),
        pltpu.make_async_copy(
            up_ref.at[:, pl.ds(mine, half)],
            weight.at[pl.ds(0, feats), pl.ds(half, half)],
            load_sem.at[1],
        ),
        pltpu.make_async_copy(
            gate_half_ref, weight.at[pl.ds(feats, feats), pl.ds(0, half)], load_sem.at[2]
        ),
        pltpu.make_async_copy(
            up_half_ref, weight.at[pl.ds(feats, feats), pl.ds(half, half)], load_sem.at[3]
        ),
        pltpu.make_async_copy(down_ref, down, load_sem.at[4]),
    ]
    for load in loads:
        load.start()
    own_x[0:rows, :] = x_ref[...]
    own_gain[...] = 1.0 / gains_ref[16:24, :]
    pl.semaphore_wait(barrier, 18)

    def x_copy(k):
        place = pl.ds(k * rows, rows)
        return remote(x_ref, own_x.at[place], x_send.at[k], x_recv.at[k], (behind(c, k), m))

    def x_in(slot):
        place = pl.ds(pl.multiple_of(slot * rows, rows), rows)
        return remote(x_ref, own_x.at[place], x_send.at[slot], x_recv.at[slot], sibling)

    def x_pass(who):
        place = pl.ds(pl.multiple_of(who * rows, rows), rows)
        return remote(
            own_x.at[place], sib_x.at[place], pass_send.at[who], pass_recv.at[who], sibling
        )

    for k in range(1, 4):
        x_copy(k).start()
    gain_swap = remote(own_gain, sib_gain, swap_send.at[0], swap_recv.at[0], sibling)
    x_pass(0).start()
    gain_swap.start()

    short = rows // 2

    def near(way):
        return z_peer(1 + 2 * way)

    def chip(way):
        return (c, near(way) * 2 + core)

    def piece(turn, to, side):
        return part.at[turn, pl.ds(pl.multiple_of(to * rows + side * short, short), short)]

    def far_copy(turn, way):
        at = turn * 2 + way
        return remote(
            piece(turn, z_peer(2), way),
            relayed.at[turn, way],
            far_send.at[at],
            far_recv.at[at],
            chip(way),
        )

    def sum_copy(turn, way):
        at = turn * 2 + way
        return remote(
            piece(turn, near(way), 1 - way),
            sums.at[turn, way, pl.ds((1 - way) * short, short)],
            sum_send.at[at],
            sum_recv.at[at],
            chip(way),
        )

    def join_copy(turn, way):
        at = turn * 2 + way
        return remote(
            joined.at[turn, way],
            sums.at[turn, way, pl.ds(way * short, short)],
            join_send.at[at],
            join_recv.at[at],
            chip(way),
        )

    def hid_copy(turn, way, slot):
        at = turn * 2 + way
        return remote(
            hidden.at[turn, core, slot],
            hidden.at[turn, core, slot],
            hid_send.at[at],
            hid_recv.at[at],
            chip(way),
        )

    def lap_copy(turn, way, slot):
        at = turn * 2 + way
        there = hidden.at[turn, core, slot, pl.ds(way * short, short)]
        return remote(there, there, lap_send.at[at], lap_recv.at[at], chip(way))

    def hid_pass(turn, at):
        return remote(
            hidden.at[turn, core, at],
            hidden.at[turn, core, at],
            hop_send.at[turn * 4 + at],
            hop_recv.at[turn * 4 + at],
            sibling,
        )

    def hid_passed(turn, at):
        return remote(
            hidden.at[turn, 1 - core, at],
            hidden.at[turn, 1 - core, at],
            hop_send.at[turn * 4 + at],
            hop_recv.at[turn * 4 + at],
            sibling,
        )

    def out_copy(slot, who):
        return remote(
            delta.at[pl.ds(pl.multiple_of(slot * rows, rows), rows)],
            deltas.at[slot],
            out_send.at[slot],
            out_recv.at[slot],
            (who, m),
        )

    def out_in(slot):
        return remote(
            delta.at[pl.ds(0, rows)], deltas.at[slot], out_send.at[slot], out_recv.at[slot], sibling
        )

    def front(turn):
        @pl.loop(0, 4)
        def _(k):
            slot = turn * 4 + k

            @pl.when(slot > 0)
            def _():
                x_in(slot).wait_recv()
                x_pass(slot).start()

        for t in range(3):

            @pl.when(turn == t)
            def _():
                for k in range(4 * t + 4, 4 * t + 8):
                    x_copy(k).start()

        @pl.when(turn == 0)
        def _():
            for load in loads:
                load.wait()
            gain_swap.wait()

        @pl.loop(0, 4)
        def _(k):
            x_pass(turn * 4 + k).wait_recv()

        place = pl.ds(pl.multiple_of(turn * group, group), group)
        mixed = own_x[place, :].astype(jnp.float32) * own_gain[0:1, :]
        square = jnp.sum(mixed * mixed, axis=1, keepdims=True)
        mixed = sib_x[place, :].astype(jnp.float32) * sib_gain[0:1, :]
        square = square + jnp.sum(mixed * mixed, axis=1, keepdims=True)
        square = jnp.broadcast_to(square, (group, 128))
        coarse = square.astype(jnp.bfloat16)
        fine = (square - coarse.astype(jnp.float32)).astype(jnp.bfloat16)
        lane = lax.broadcasted_iota(jnp.int32, (group, 128), 1)
        part[turn, :, pl.ds(both, 128)] = jnp.where(lane < 64, coarse, fine)

        @pl.loop(0, both // 256)
        def _(tile):
            cols = pl.ds(pl.multiple_of(tile * 256, 256), 256)
            total = jnp.dot(
                own_x[place, :], weight[pl.ds(0, feats), cols], preferred_element_type=jnp.float32
            )
            total += jnp.dot(
                sib_x[place, :],
                weight[pl.ds(feats, feats), cols],
                preferred_element_type=jnp.float32,
            )
            part[turn, :, cols] = total.astype(jnp.bfloat16)

        for way in range(2):
            far_copy(turn, way).start()
        for way in range(2):
            sum_copy(turn, way).start()

    def relay(turn):
        for way in range(2):
            far_copy(turn, way).wait_recv()
            joined[turn, way] = (
                piece(turn, near(way), way)[...].astype(jnp.float32)
                + relayed[turn, way].astype(jnp.float32)
            ).astype(jnp.bfloat16)
            join_copy(turn, way).start()

    def middle(turn):
        total = part[turn, pl.ds(pl.multiple_of(z * rows, rows), rows), :].astype(jnp.float32)
        for way in range(2):
            sum_copy(turn, way).wait_recv()
            join_copy(turn, way).wait_recv()
            total += sums[turn, way].astype(jnp.float32)
        square = total[:, both : both + 1] + total[:, both + 64 : both + 65]
        scale = lax.rsqrt(square * (1.0 / (8 * feats)) + EPS)
        gate = total[:, :half] * scale
        up = total[:, half:both] * scale
        hidden[turn, core, z] = (gate / (1.0 + jnp.exp(-gate)) * up).astype(jnp.bfloat16)
        for way in range(2):
            hid_copy(turn, way, z).start()
        hid_pass(turn, z).start()

    def lap(turn):
        for way in range(2):
            slot = near(1 - way)
            hid_copy(turn, way, slot).wait_recv()
            lap_copy(turn, way, slot).start()
            hid_pass(turn, slot).start()

    def back(turn):
        for way in range(2):
            lap_copy(turn, way, z_peer(2)).wait_recv()
        hid_pass(turn, z_peer(2)).start()
        for k in range(4):
            hid_passed(turn, z_peer(k)).wait_recv()
        place = pl.ds(pl.multiple_of(turn * group, group), group)

        @pl.loop(0, feats // 256)
        def _(tile):
            cols = pl.ds(pl.multiple_of(tile * 256, 256), 256)
            total = jnp.dot(
                hidden[turn, 0].reshape(group, half),
                down[pl.ds(0, half), cols],
                preferred_element_type=jnp.float32,
            )
            total += jnp.dot(
                hidden[turn, 1].reshape(group, half),
                down[pl.ds(half, half), cols],
                preferred_element_type=jnp.float32,
            )
            delta[place, cols] = total.astype(jnp.bfloat16)

        for k in range(4):
            dx, dy = 0, 0
            for t in range(4):
                dx = jnp.where(turn == t, OFFSETS[4 * t + k][0], dx)
                dy = jnp.where(turn == t, OFFSETS[4 * t + k][1], dy)
            who = lax.rem(x + dx, 4) * 4 + lax.rem(y + dy, 4)
            if k > 0:
                out_copy(turn * 4 + k, who).start()
            else:

                @pl.when(turn > 0)
                def _():
                    out_copy(turn * 4, who).start()

    @pl.loop(0, 8)
    def _(step):
        for late, stage in enumerate((front, relay, middle, lap, back)):

            @pl.when((step >= late) & (step < late + 4))
            def _():
                stage(step - late)

    total_ref[...] = share_ref[...] + delta[0:rows, :].astype(jnp.float32)

    @pl.loop(1, 16)
    def _(k):
        out_in(k).wait_recv()
        total_ref[...] += deltas[k].astype(jnp.float32)

    update = (score_ref[:, 0:1] * total_ref[...]).astype(jnp.bfloat16)
    slot_at = lax.broadcasted_iota(jnp.int32, (slots, rows), 0)
    shard = destination_ref.shape[1]
    taken = take_slots(kept_row_ref[0:1, :], kept_column_ref[:, 0:1], shard, 0)
    give = jnp.where(slot_at == taken, 1.0, 0.0).astype(jnp.bfloat16)
    outbox[...] = jnp.dot(give, update, preferred_element_type=jnp.float32).astype(jnp.bfloat16)

    def box_of(who):
        return pl.ds(pl.multiple_of(who * box, box), box)

    def box_copy(k):
        who = ahead(c, k)
        return remote(
            outbox.at[box_of(who)], inbox.at[box_of(c)], box_send.at[k], box_recv.at[c], (who, m)
        )

    def box_in(who):
        return remote(
            outbox.at[box_of(who)], inbox.at[box_of(who)], box_send.at[0], box_recv.at[who], sibling
        )

    for k in range(1, 16):
        box_copy(k).start()

    inbox[box_of(c), :] = outbox[box_of(c), :]
    slot_at = lax.broadcasted_iota(jnp.int32, (slots, shard), 0)
    sent = send_slots(destination_ref[0:1, :], rows)
    back_to = jnp.where(slot_at == sent, 1.0, 0.0).T.astype(jnp.bfloat16)

    for k in range(1, 16):
        box_in(ahead(c, k)).wait_recv()

    @pl.loop(0, feats // 256)
    def _(tile):
        cols = pl.ds(pl.multiple_of(tile * 256, 256), 256)
        out_ref[:, cols] = jnp.dot(
            back_to, inbox[:, cols], preferred_element_type=jnp.float32
        ).astype(jnp.bfloat16)

    for k in range(1, 16):
        x_copy(k).wait_send()
        out_in(k).wait_send()
        box_copy(k).wait_send()

    @pl.loop(0, 16)
    def _(who):
        x_pass(who).wait_send()

    @pl.loop(0, 4)
    def _(turn):
        for way in range(2):
            far_copy(turn, way).wait_send()
            sum_copy(turn, way).wait_send()
            join_copy(turn, way).wait_send()
            hid_copy(turn, way, z).wait_send()
            lap_copy(turn, way, near(1 - way)).wait_send()
        for k in range(4):
            hid_pass(turn, z_peer(k)).wait_send()


def feed_forward(
    scaled,
    share,
    score,
    kept_row,
    kept_column,
    destination,
    gains,
    gate_weight,
    up_weight,
    gate_half,
    up_half,
    down_weight,
):
    rows, feats = scaled.shape
    cols = gate_weight.shape[1]
    half = cols // 2
    dma = pltpu.SemaphoreType.DMA
    bf16 = jnp.bfloat16
    vmem, anywhere = pl.BlockSpec(memory_space=pltpu.VMEM), pl.BlockSpec(memory_space=pl.ANY)
    return pl.pallas_call(
        mlp_kernel,
        out_shape=jax.ShapeDtypeStruct((destination.shape[1], feats), bf16),
        in_specs=[vmem] * 7 + [anywhere] * 5,
        out_specs=vmem,
        scratch_shapes=[
            pltpu.VMEM((16 * rows, feats), bf16),
            pltpu.VMEM((16 * rows, feats), bf16),
            pltpu.VMEM((8, feats), jnp.float32),
            pltpu.VMEM((8, feats), jnp.float32),
            pltpu.VMEM((2 * feats, cols), bf16),
            pltpu.VMEM((cols, feats), bf16),
            pltpu.VMEM((4, 4 * rows, cols + 128), bf16),
            pltpu.VMEM((4, 2, rows // 2, cols + 128), bf16),
            pltpu.VMEM((4, 2, rows // 2, cols + 128), bf16),
            pltpu.VMEM((4, 2, rows, cols + 128), bf16),
            pltpu.VMEM((4, 2, 4, rows, half), bf16),
            pltpu.VMEM((16 * rows, feats), bf16),
            pltpu.VMEM((16, rows, feats), bf16),
            pltpu.VMEM((rows, feats), jnp.float32),
            pltpu.VMEM((16 * BOX, feats), bf16),
            pltpu.VMEM((16 * BOX, feats), bf16),
            dma((5,)),
            dma((1,)),
            dma((1,)),
        ]
        + [dma((16,))] * 20,
        compiler_params=pltpu.CompilerParams(
            collective_id=3, has_side_effects=True, vmem_limit_bytes=VMEM_BYTES
        ),
        name="feed_forward",
    )(
        scaled,
        share,
        score,
        kept_row,
        kept_column,
        destination,
        gains,
        gate_weight,
        up_weight,
        gate_half,
        up_half,
        down_weight,
    )


def attend_kernel(
    tokens_ref,
    destination_ref,
    kept_row_ref,
    kept_column_ref,
    gains_ref,
    query_ref,
    key_ref,
    value_ref,
    out_weight_ref,
    gate_ref,
    up_ref,
    cosine_ref,
    sine_ref,
    share_ref,
    scaled_ref,
    score_ref,
    gate_half_ref,
    up_half_ref,
    outbox,
    inbox,
    full,
    normed,
    blocks,
    weight,
    out_weight,
    part,
    parts,
    key_value,
    attended,
    delta,
    deltas,
    load_sem,
    swap_send,
    swap_recv,
    box_send,
    box_recv,
    row_send,
    row_recv,
    hop_send,
    hop_recv,
    norm_send,
    norm_recv,
    wide_send,
    wide_recv,
    part_send,
    part_recv,
    kv_send,
    kv_recv,
    att_send,
    att_recv,
    out_send,
    out_recv,
):
    rows, feats = share_ref.shape
    width = query_ref.shape[0]
    slots = outbox.shape[0]
    box = slots // 16
    group = 4 * rows
    cols = weight.shape[1]
    q_cols, kv_cols = query_ref.shape[1], key_ref.shape[1]
    heads = q_cols // HEAD_DIM
    c, m = lax.axis_index("ctx"), lax.axis_index("mp")
    x, y = c // 4, c % 4
    z, core = m // 2, m % 2
    sibling = (c, z * 2 + 1 - core)

    def rows_of(who, count=1):
        return pl.ds(pl.multiple_of(who * (rows * count), rows), rows * count)

    is_home = x == z
    barrier = pltpu.get_barrier_semaphore()

    def x_peer(k):
        return (lax.rem(x + k, 4) * 4 + y, m)

    def y_peer(k):
        return (x * 4 + lax.rem(y + k, 4), m)

    @pl.loop(0, 8)
    def _(k):
        @pl.when(jnp.logical_not(is_home & (k == m)))
        def _():
            pl.semaphore_signal(barrier, inc=1, device_id=(z * 4 + y, k), device_id_type=MESH)

    for k in range(1, 16):
        pl.semaphore_signal(barrier, inc=1, device_id=(ahead(c, k), m), device_id_type=MESH)
    for k in range(1, 4):
        pl.semaphore_signal(
            barrier,
            inc=1,
            device_id=(c, lax.rem(z + k, 4) * 2 + core),
            device_id_type=MESH,
        )
    pl.semaphore_signal(barrier, inc=1, device_id=sibling, device_id_type=MESH)

    band = pl.ds(pl.multiple_of(y * width, width), width)
    loads = [
        pltpu.make_async_copy(query_ref, weight.at[band, pl.ds(0, q_cols)], load_sem.at[0]),
        pltpu.make_async_copy(key_ref, weight.at[band, pl.ds(q_cols, kv_cols)], load_sem.at[1]),
        pltpu.make_async_copy(
            value_ref, weight.at[band, pl.ds(q_cols + kv_cols, kv_cols)], load_sem.at[2]
        ),
        pltpu.make_async_copy(out_weight_ref, out_weight.at[y], load_sem.at[3]),
    ]
    for load in loads:
        load.start()

    slot_at = lax.broadcasted_iota(jnp.int32, (slots, tokens_ref.shape[0]), 0)
    sent = send_slots(destination_ref[0:1, :], rows)
    pick = jnp.where(slot_at == sent, 1.0, 0.0).astype(jnp.bfloat16)

    @pl.loop(0, feats // 256)
    def _(tile):
        cols = pl.ds(pl.multiple_of(tile * 256, 256), 256)
        outbox[:, cols] = jnp.dot(
            pick, tokens_ref[:, cols], preferred_element_type=jnp.float32
        ).astype(jnp.bfloat16)

    def box_of(who):
        return pl.ds(pl.multiple_of(who * box, box), box)

    inbox[box_of(c), :] = outbox[box_of(c), :]
    pl.semaphore_wait(barrier, jnp.where(is_home, 26, 27))

    def box_copy(k):
        who = ahead(c, k)
        return remote(
            outbox.at[box_of(who)], inbox.at[box_of(c)], box_send.at[k], box_recv.at[c], (who, m)
        )

    def box_in(who):
        return remote(
            outbox.at[box_of(who)], inbox.at[box_of(who)], box_send.at[0], box_recv.at[who], sibling
        )

    def weight_copy(k):
        return remote(
            weight.at[band], weight.at[band], wide_send.at[k], wide_recv.at[k], y_peer(k)
        )

    def out_weight_copy(k):
        return remote(
            out_weight.at[y],
            out_weight.at[y],
            wide_send.at[4 + k],
            wide_recv.at[4 + k],
            y_peer(k),
        )

    def weight_lap(k):
        whose = lax.rem(y + 4 - k, 4)
        start = whose * width + (k // 2) * (width // 2)
        there = weight.at[pl.ds(pl.multiple_of(start, width // 2), width // 2)]
        return remote(there, there, wide_send.at[k - 1], wide_recv.at[k - 1], y_peer(k))

    def out_weight_lap(k):
        whose = lax.rem(y + 4 - k, 4)
        there = out_weight.at[whose, pl.ds((k // 2) * (width // 2), width // 2)]
        return remote(there, there, wide_send.at[k + 3], wide_recv.at[k + 3], y_peer(k))

    for k in range(1, 16):
        box_copy(k).start()
    for load in loads:
        load.wait()
    for k in (1, 3):
        weight_copy(k).start()
    for k in range(1, 16):
        box_in(ahead(c, k)).wait_recv()

    slot_at = lax.broadcasted_iota(jnp.int32, (rows, slots), 1)
    taken = take_slots(kept_row_ref[0:1, :], kept_column_ref[:, 0:1], tokens_ref.shape[0], 1)
    take = jnp.where(slot_at == taken, 1.0, 0.0).astype(jnp.bfloat16)
    full[m] = jnp.dot(take, inbox[...], preferred_element_type=jnp.float32).astype(jnp.bfloat16)

    def row_copy(k, who):
        return remote(
            full.at[who],
            full.at[who],
            row_send.at[k],
            row_recv.at[who],
            (c, lax.rem(z + k, 4) * 2 + core),
        )

    def hop(who):
        return remote(full.at[who], full.at[who], hop_send.at[who], hop_recv.at[who], sibling)

    def z_block(k):
        return lax.rem(z + k, 4) * 2 + core

    def z_sibling(k):
        return lax.rem(z + k, 4) * 2 + 1 - core

    for k in (2, 1, 3):
        row_copy(k, m).start()
    hop(m).start()
    for k in (1, 3, 2):
        row_copy(k, z_block(k)).wait_recv()
        hop(z_block(k)).start()
    for k in (0, 1, 3, 2):
        hop(z_sibling(k)).wait_recv()

    for k in (1, 3):
        weight_copy(k).wait_recv()
        weight_lap(k).start()
    square, route = 0.0, 0.0
    for at in range(8):
        wide = full[at].astype(jnp.float32)
        square += jnp.sum(wide * wide, axis=1, keepdims=True)
        route += jnp.sum(wide * gains_ref[8 + at : 9 + at, :], axis=1, keepdims=True)
    scale = lax.rsqrt(square * (1.0 / (8 * feats)) + EPS)
    score_ref[...] = jnp.broadcast_to(1.0 / (1.0 + jnp.exp(-route)), score_ref.shape)
    for at in range(8):
        wide = full[at].astype(jnp.float32) * scale * gains_ref[at : at + 1, :]
        wide = wide.astype(jnp.bfloat16)
        normed[at] = wide

    def norm_copy(k):
        to = lax.rem(x + 4 - k, 4)
        return remote(
            normed.at[pl.ds(2 * to, 2)],
            blocks.at[:, k],
            norm_send.at[k],
            norm_recv.at[k],
            (to * 4 + y, m),
        )

    for k in (1, 3, 2):
        norm_copy(k).start()
    blocks[0, 0] = normed[2 * x]
    blocks[1, 0] = normed[2 * x + 1]
    half = gate_half_ref.shape[1]
    others = pl.ds(pl.multiple_of((1 - core) * half, 128), half)
    swaps = [
        remote(gate_ref.at[:, others], gate_half_ref, swap_send.at[0], swap_recv.at[0], sibling),
        remote(up_ref.at[:, others], up_half_ref, swap_send.at[1], swap_recv.at[1], sibling),
    ]
    for swap in swaps:
        swap.start()

    def part_copy(k):
        return remote(part.at[rows_of(k)], parts.at[k], part_send.at[k], part_recv.at[k], x_peer(k))

    for k in (1, 3, 2):
        norm_copy(k).wait_recv()
    for k in (1, 3):
        weight_lap(k).wait_recv()
    for k in (1, 3):
        out_weight_copy(k).start()

    @pl.loop(0, cols // 256)
    def _(tile):
        at = pl.ds(pl.multiple_of(tile * 256, 256), 256)
        total = jnp.dot(
            blocks[0].reshape(group, feats),
            weight[pl.ds(0, feats), at],
            preferred_element_type=jnp.float32,
        )
        total += jnp.dot(
            blocks[1].reshape(group, feats),
            weight[pl.ds(feats, feats), at],
            preferred_element_type=jnp.float32,
        )
        part[:, at] = total.astype(jnp.bfloat16)
        share_ref[:, at] = total[0:rows]

    for k in (1, 3, 2):
        part_copy(k).start()
    for k in (1, 3, 2):
        part_copy(k).wait_recv()
        share_ref[:, 0:cols] += parts[k].astype(jnp.float32)

    def turned(at):
        head = share_ref[:, at : at + HEAD_DIM]
        swapped = pltpu.roll(head, HEAD_DIM // 2, 1)
        return (head * cosine_ref[...] + swapped * sine_ref[...]).astype(jnp.bfloat16)

    mine = rows_of(c)
    key_value[mine, 0:HEAD_DIM] = turned(q_cols)
    at = q_cols + kv_cols
    key_value[mine, HEAD_DIM : 2 * HEAD_DIM] = share_ref[:, at : at + HEAD_DIM].astype(jnp.bfloat16)

    def kv_copy(k, who, device):
        return remote(
            key_value.at[rows_of(who)],
            key_value.at[rows_of(who)],
            kv_send.at[k],
            kv_recv.at[who],
            device,
        )

    for k in range(1, 16):
        kv_copy(k, c, (behind(c, k), m)).start()

    queries = jnp.concatenate([turned(h * HEAD_DIM) for h in range(heads)], axis=0)

    for k in range(1, 16):
        kv_copy(k, ahead(c, k), sibling).wait_recv()
    for k in (1, 3):
        out_weight_copy(k).wait_recv()
        out_weight_lap(k).start()

    keys = 16 * rows
    scores = lax.dot_general(
        queries,
        key_value[:, 0:HEAD_DIM],
        (((1,), (1,)), ((), ())),
        preferred_element_type=jnp.float32,
    ) * (HEAD_DIM ** (-0.5))
    query_at = lax.broadcasted_iota(jnp.int32, (heads * rows, keys), 0) % rows * 16 + c
    key_at = lax.broadcasted_iota(jnp.int32, (heads * rows, keys), 1)
    allowed = key_at % rows * 16 + key_at // rows <= query_at
    scores = jnp.where(allowed, scores, -1e30)
    weights = jnp.exp(scores - jnp.max(scores, axis=1, keepdims=True))
    weights = jnp.where(allowed, weights, 0.0)
    total = jnp.sum(weights, axis=1, keepdims=True)
    mixed = (
        jnp.dot(
            weights.astype(jnp.bfloat16),
            key_value[:, HEAD_DIM : 2 * HEAD_DIM],
            preferred_element_type=jnp.float32,
        )
        / total
    ).astype(jnp.bfloat16)
    for h in range(heads):
        attended[0:rows, h * HEAD_DIM : (h + 1) * HEAD_DIM] = mixed[h * rows : (h + 1) * rows]

    def att_copy(k):
        to = lax.rem(x + 4 - k, 4)
        return remote(
            attended.at[0:rows],
            attended.at[rows_of(k)],
            att_send.at[k],
            att_recv.at[k],
            (to * 4 + y, m),
        )

    for k in (1, 3, 2):
        att_copy(k).start()

    def out_copy(k, side):
        return remote(
            delta.at[side, rows_of(k)],
            deltas.at[m],
            out_send.at[2 * k + side],
            out_recv.at[m],
            (lax.rem(x + k, 4) * 4 + y, 2 * x + side),
        )

    def out_in(slot):
        return remote(
            delta.at[0, pl.ds(0, rows)],
            deltas.at[slot],
            out_send.at[slot],
            out_recv.at[slot],
            sibling,
        )

    for k in (1, 3):
        out_weight_lap(k).wait_recv()
    for k in (1, 3, 2):
        att_copy(k).wait_recv()
    for side in range(2):
        for at in range(2):
            delta[side, :, at * width : (at + 1) * width] = jnp.dot(
                attended[...], out_weight[2 * side + at], preferred_element_type=jnp.float32
            ).astype(jnp.bfloat16)
        for k in (2, 1, 3):
            out_copy(k, side).start()

        @pl.when(jnp.logical_not(is_home & (side == core)))
        def _():
            out_copy(0, side).start()

    @pl.when(is_home)
    def _():
        deltas[m] = delta[core, 0:rows, :]

    share_ref[...] = jnp.zeros_like(share_ref)

    @pl.loop(0, 8)
    def _(k):
        slot = lax.rem(k + m, 8)

        @pl.when(jnp.logical_not(is_home & (slot == m)))
        def _():
            out_in(slot).wait_recv()

        share_ref[...] += deltas[slot].astype(jnp.float32)

    mixed = full[m].astype(jnp.float32) + share_ref[...]
    scaled_ref[...] = (mixed * gains_ref[16:17, :]).astype(jnp.bfloat16)

    for k in range(1, 4):
        row_copy(k, m).wait_send()
    for k in range(4):
        hop(z_block(k)).wait_send()

    for swap in swaps:
        swap.wait()

    for k in (1, 3):
        weight_copy(k).wait_send()
        weight_lap(k).wait_send()
        out_weight_copy(k).wait_send()
        out_weight_lap(k).wait_send()
    for side in range(2):
        for k in range(1, 4):
            out_copy(k, side).wait_send()

        @pl.when(jnp.logical_not(is_home & (side == core)))
        def _():
            out_copy(0, side).wait_send()

    for k in range(1, 4):
        norm_copy(k).wait_send()
        part_copy(k).wait_send()
        att_copy(k).wait_send()
    for k in range(1, 16):
        box_copy(k).wait_send()
        kv_copy(k, c, sibling).wait_send()


def attend(
    tokens, destination, kept_row, kept_column, gains, query, key, value, out_weight, gate, up, cosine, sine
):
    count, slots = kept_column.shape[0], 16 * BOX
    feats = tokens.shape[1]
    width = query.shape[0]
    cols = query.shape[1] + key.shape[1] + value.shape[1]
    dma = pltpu.SemaphoreType.DMA
    bf16 = jnp.bfloat16
    vmem, anywhere = pl.BlockSpec(memory_space=pltpu.VMEM), pl.BlockSpec(memory_space=pl.ANY)
    return pl.pallas_call(
        attend_kernel,
        out_shape=(
            jax.ShapeDtypeStruct((count, feats), jnp.float32),
            jax.ShapeDtypeStruct((count, feats), bf16),
            jax.ShapeDtypeStruct((count, 128), jnp.float32),
            jax.ShapeDtypeStruct((gate.shape[0], gate.shape[1] // 2), bf16),
            jax.ShapeDtypeStruct((up.shape[0], up.shape[1] // 2), bf16),
        ),
        in_specs=[vmem] * 5 + [anywhere] * 6 + [vmem] * 2,
        out_specs=(vmem, vmem, vmem, anywhere, anywhere),
        scratch_shapes=[
            pltpu.VMEM((slots, feats), bf16),
            pltpu.VMEM((slots, feats), bf16),
            pltpu.VMEM((8, count, feats), bf16),
            pltpu.VMEM((8, count, feats), bf16),
            pltpu.VMEM((2, 4, count, feats), bf16),
            pltpu.VMEM((4 * width, cols), bf16),
            pltpu.VMEM((4, *out_weight.shape), bf16),
            pltpu.VMEM((4 * count, cols), bf16),
            pltpu.VMEM((4, count, cols), bf16),
            pltpu.VMEM((16 * count, 2 * HEAD_DIM), bf16),
            pltpu.VMEM((4 * count, query.shape[1]), bf16),
            pltpu.VMEM((2, 4 * count, feats), bf16),
            pltpu.VMEM((8, count, feats), bf16),
            dma((4,)),
            dma((2,)),
            dma((2,)),
        ]
        + [dma((16,))] * 18,
        compiler_params=pltpu.CompilerParams(
            collective_id=2, has_side_effects=True, vmem_limit_bytes=VMEM_BYTES
        ),
        name="attend",
    )(
        tokens,
        destination,
        kept_row,
        kept_column,
        gains,
        query,
        key,
        value,
        out_weight,
        gate,
        up,
        cosine,
        sine,
    )


def body(
    tokens,
    norm_gain,
    router_weight,
    query_weight,
    key_weight,
    value_weight,
    out_weight,
    mlp_gain,
    gate_weight,
    up_weight,
    down_weight,
    destination,
    kept_pos,
):
    tok_dev, feature_cols = tokens.shape
    kept_dev = kept_pos.shape[0]
    half_dim = HEAD_DIM // 2
    exponent = jnp.arange(half_dim, dtype=jnp.float32) * (2.0 / HEAD_DIM)
    angles = kept_pos.astype(jnp.float32)[:, None] * (500000.0 ** (-exponent))[None, :]
    cosine, sine = jnp.cos(angles), jnp.sin(angles)
    gains = jnp.concatenate(
        [
            norm_gain.reshape(8, feature_cols),
            router_weight.reshape(8, feature_cols),
            jnp.broadcast_to(mlp_gain, (8, feature_cols)),
        ]
    ).astype(jnp.float32)
    destinations = jnp.broadcast_to(destination, (8, tok_dev))
    kept_row = jnp.broadcast_to(kept_pos, (8, kept_dev))
    kept_column = jnp.broadcast_to(kept_pos[:, None], (kept_dev, 128))
    head_share, scaled, score, gate_half, up_half = attend(
        tokens,
        destinations,
        kept_row,
        kept_column,
        gains,
        query_weight,
        key_weight,
        value_weight,
        out_weight,
        gate_weight,
        up_weight,
        jnp.concatenate([cosine, cosine], axis=1),
        jnp.concatenate([-sine, sine], axis=1),
    )
    arrived = feed_forward(
        scaled,
        head_share,
        score,
        kept_row,
        kept_column,
        destinations,
        gains,
        gate_weight,
        up_weight,
        gate_half,
        up_half,
        down_weight,
    )
    return (tokens.astype(jnp.float32) + arrived.astype(jnp.float32)).astype(jnp.bfloat16)


def solution(mesh):
    in_specs = (
        P("ctx", "mp"),
        P(),
        P(),
        P("ctx", "mp"),
        P("ctx", "mp"),
        P("ctx", "mp"),
        P("mp", "ctx"),
        P("mp"),
        P("mp", "ctx"),
        P("mp", "ctx"),
        P("ctx", "mp"),
        P("ctx"),
        P("ctx"),
    )
    out_specs = P("ctx", "mp")
    return jax.shard_map(body, mesh=mesh, in_specs=in_specs, out_specs=out_specs, check_vma=False)
```

```python
import jax
import jax.numpy as jnp
from jax import lax
from jax.sharding import PartitionSpec as P

from jax.experimental import pallas as pl
from jax.experimental.pallas import tpu as pltpu

HEAD_DIM = 128
BOX = 16
VMEM_BYTES = 60 * 2**20
MESH = pl.DeviceIdType.MESH
OFFSETS = (
    (0, 0), (0, 1), (1, 0), (0, 3), (3, 0), (0, 2), (2, 0), (1, 1),
    (3, 3), (1, 3), (3, 1), (1, 2), (2, 1), (3, 2), (2, 3), (2, 2),
)
EPS = 1e-05


def ahead(c, k):
    dx, dy = OFFSETS[k]
    return lax.rem(c // 4 + dx, 4) * 4 + lax.rem(c % 4 + dy, 4)


def behind(c, k):
    dx, dy = OFFSETS[k]
    return lax.rem(c // 4 + 4 - dx, 4) * 4 + lax.rem(c % 4 + 4 - dy, 4)


def send_slots(destination, kept):
    owner, slot = destination // kept, destination % kept
    going = destination >= 0
    order = jnp.where(going, slot * 16 + owner, 16 * kept)
    first = (jnp.min(order) - owner + 15) // 16
    return jnp.where(going, owner * BOX + slot - first, 16 * BOX)


def take_slots(row, column, shard, axis):
    kept = row.shape[1]
    same = column // shard == row // shard
    at = lax.broadcasted_iota(jnp.int32, (kept, kept), axis)
    first = jnp.min(jnp.where(same, at, kept), axis=axis, keepdims=True)
    mine = row if axis == 0 else column
    return mine // shard * BOX + lax.broadcasted_iota(jnp.int32, mine.shape, 1 - axis) - first


def remote(source, target, sent, landed, device):
    return pltpu.make_async_remote_copy(
        src_ref=source,
        dst_ref=target,
        send_sem=sent,
        recv_sem=landed,
        device_id=device,
        device_id_type=MESH,
    )


def mlp_kernel(
    x_ref,
    share_ref,
    score_ref,
    kept_row_ref,
    kept_column_ref,
    destination_ref,
    gains_ref,
    gate_ref,
    up_ref,
    gate_half_ref,
    up_half_ref,
    down_ref,
    out_ref,
    own_x,
    sib_x,
    own_gain,
    sib_gain,
    weight,
    down,
    part,
    relayed,
    joined,
    sums,
    hidden,
    delta,
    deltas,
    total_ref,
    outbox,
    inbox,
    load_sem,
    swap_send,
    swap_recv,
    x_send,
    x_recv,
    half_send,
    half_recv,
    pass_send,
    pass_recv,
    far_send,
    far_recv,
    sum_send,
    sum_recv,
    join_send,
    join_recv,
    hid_send,
    hid_recv,
    lap_send,
    lap_recv,
    hop_send,
    hop_recv,
    out_send,
    out_recv,
    box_send,
    box_recv,
):
    rows, feats = x_ref.shape
    slots = outbox.shape[0]
    box = slots // 16
    half = gate_ref.shape[1] // 2
    both = 2 * half
    group = 4 * rows
    c, m = lax.axis_index("ctx"), lax.axis_index("mp")
    x, y = c // 4, c % 4
    z, core = m // 2, m % 2
    sibling = (c, z * 2 + 1 - core)

    def z_peer(step):
        return lax.rem(z + step, 4)

    barrier = pltpu.get_barrier_semaphore()

    for k in range(1, 16):
        pl.semaphore_signal(barrier, inc=1, device_id=(ahead(c, k), m), device_id_type=MESH)

    for k in (1, 3):
        pl.semaphore_signal(
            barrier, inc=1, device_id=(c, z_peer(k) * 2 + core), device_id_type=MESH
        )
    pl.semaphore_signal(barrier, inc=1, device_id=sibling, device_id_type=MESH)

    mine = pl.multiple_of(core * half, 128)
    loads = [
        pltpu.make_async_copy(
            gate_ref.at[:, pl.ds(mine, half)],
            weight.at[pl.ds(0, feats), pl.ds(0, half)],
            load_sem.at[0],
        ),
        pltpu.make_async_copy(
            up_ref.at[:, pl.ds(mine, half)],
            weight.at[pl.ds(0, feats), pl.ds(half, half)],
            load_sem.at[1],
        ),
        pltpu.make_async_copy(
            gate_half_ref, weight.at[pl.ds(feats, feats), pl.ds(0, half)], load_sem.at[2]
        ),
        pltpu.make_async_copy(
            up_half_ref, weight.at[pl.ds(feats, feats), pl.ds(half, half)], load_sem.at[3]
        ),
        pltpu.make_async_copy(down_ref, down, load_sem.at[4]),
    ]
    for load in loads:
        load.start()
    own_x[0:rows, :] = x_ref[...]
    own_gain[...] = 1.0 / gains_ref[16:24, :]
    pl.semaphore_wait(barrier, 18)

    def x_copy(k):
        place = pl.ds(k * rows, rows)
        return remote(x_ref, own_x.at[place], x_send.at[k], x_recv.at[k], (behind(c, k), m))

    def x_in(slot):
        place = pl.ds(pl.multiple_of(slot * rows, rows), rows)
        return remote(x_ref, own_x.at[place], x_send.at[slot], x_recv.at[slot], sibling)

    def x_pass(who):
        place = pl.ds(pl.multiple_of(who * rows, rows), rows)
        return remote(
            own_x.at[place], sib_x.at[place], pass_send.at[who], pass_recv.at[who], sibling
        )

    short = rows // 2

    def half_copy(dx, dy, side):
        slot = OFFSETS.index((dx, dy))
        source = OFFSETS.index((0, dy) if side else (dx, 0))
        to = lax.rem(x + 4 - dx, 4) * 4 + y if side else x * 4 + lax.rem(y + 4 - dy, 4)
        return remote(
            own_x.at[pl.ds(source * rows + side * short, short)],
            own_x.at[pl.ds(slot * rows + side * short, short)],
            half_send.at[side * 16 + slot],
            half_recv.at[side * 16 + slot],
            (to, m),
        )

    def half_in(slot, side):
        start = pl.multiple_of(slot * rows + side * short, short)
        return remote(
            own_x.at[pl.ds(0, short)],
            own_x.at[pl.ds(start, short)],
            half_send.at[0],
            half_recv.at[side * 16 + slot],
            sibling,
        )

    def halves(slot):
        dx, dy = OFFSETS[slot]
        if dx:
            return [half_copy(dx, k, 0) for k in range(1, 4)]
        return [half_copy(k, dy, 1) for k in range(1, 4)]

    for k in range(1, 7):
        x_copy(k).start()
    gain_swap = remote(own_gain, sib_gain, swap_send.at[0], swap_recv.at[0], sibling)
    x_pass(0).start()
    gain_swap.start()

    def near(way):
        return z_peer(1 + 2 * way)

    def chip(way):
        return (c, near(way) * 2 + core)

    def piece(turn, to, side):
        return part.at[turn, pl.ds(pl.multiple_of(to * rows + side * short, short), short)]

    def far_copy(turn, way):
        at = turn * 2 + way
        return remote(
            piece(turn, z_peer(2), way),
            relayed.at[turn, way],
            far_send.at[at],
            far_recv.at[at],
            chip(way),
        )

    def sum_copy(turn, way):
        at = turn * 2 + way
        return remote(
            piece(turn, near(way), 1 - way),
            sums.at[turn, way, pl.ds((1 - way) * short, short)],
            sum_send.at[at],
            sum_recv.at[at],
            chip(way),
        )

    def join_copy(turn, way):
        at = turn * 2 + way
        return remote(
            joined.at[turn, way],
            sums.at[turn, way, pl.ds(way * short, short)],
            join_send.at[at],
            join_recv.at[at],
            chip(way),
        )

    def hid_copy(turn, way, slot):
        at = turn * 2 + way
        return remote(
            hidden.at[turn, core, slot],
            hidden.at[turn, core, slot],
            hid_send.at[at],
            hid_recv.at[at],
            chip(way),
        )

    def lap_copy(turn, way, slot):
        at = turn * 2 + way
        there = hidden.at[turn, core, slot, pl.ds(way * short, short)]
        return remote(there, there, lap_send.at[at], lap_recv.at[at], chip(way))

    def hid_pass(turn, at):
        return remote(
            hidden.at[turn, core, at],
            hidden.at[turn, core, at],
            hop_send.at[turn * 4 + at],
            hop_recv.at[turn * 4 + at],
            sibling,
        )

    def hid_passed(turn, at):
        return remote(
            hidden.at[turn, 1 - core, at],
            hidden.at[turn, 1 - core, at],
            hop_send.at[turn * 4 + at],
            hop_recv.at[turn * 4 + at],
            sibling,
        )

    def out_copy(slot, who):
        return remote(
            delta.at[pl.ds(pl.multiple_of(slot * rows, rows), rows)],
            deltas.at[slot],
            out_send.at[slot],
            out_recv.at[slot],
            (who, m),
        )

    def out_in(slot):
        return remote(
            delta.at[pl.ds(0, rows)], deltas.at[slot], out_send.at[slot], out_recv.at[slot], sibling
        )

    def front(turn):
        @pl.loop(0, 4)
        def _(k):
            slot = turn * 4 + k

            @pl.when((slot > 0) & (slot < 7))
            def _():
                x_in(slot).wait_recv()

            @pl.when(slot >= 7)
            def _():
                half_in(slot, 0).wait_recv()
                half_in(slot, 1).wait_recv()

            @pl.when(slot > 0)
            def _():
                x_pass(slot).start()

        for t in range(2):

            @pl.when(turn == t)
            def _():
                for slot in range(3 * t + 1, 3 * t + 4):
                    for copy in halves(slot):
                        copy.start()

        @pl.when(turn == 0)
        def _():
            for load in loads:
                load.wait()
            gain_swap.wait()

        @pl.loop(0, 4)
        def _(k):
            x_pass(turn * 4 + k).wait_recv()

        place = pl.ds(pl.multiple_of(turn * group, group), group)
        mixed = own_x[place, :].astype(jnp.float32) * own_gain[0:1, :]
        square = jnp.sum(mixed * mixed, axis=1, keepdims=True)
        mixed = sib_x[place, :].astype(jnp.float32) * sib_gain[0:1, :]
        square = square + jnp.sum(mixed * mixed, axis=1, keepdims=True)
        square = jnp.broadcast_to(square, (group, 128))
        coarse = square.astype(jnp.bfloat16)
        fine = (square - coarse.astype(jnp.float32)).astype(jnp.bfloat16)
        lane = lax.broadcasted_iota(jnp.int32, (group, 128), 1)
        part[turn, :, pl.ds(both, 128)] = jnp.where(lane < 64, coarse, fine)

        @pl.loop(0, both // 256)
        def _(tile):
            cols = pl.ds(pl.multiple_of(tile * 256, 256), 256)
            total = jnp.dot(
                own_x[place, :], weight[pl.ds(0, feats), cols], preferred_element_type=jnp.float32
            )
            total += jnp.dot(
                sib_x[place, :],
                weight[pl.ds(feats, feats), cols],
                preferred_element_type=jnp.float32,
            )
            part[turn, :, cols] = total.astype(jnp.bfloat16)

        for way in range(2):
            far_copy(turn, way).start()
        for way in range(2):
            sum_copy(turn, way).start()

    def relay(turn):
        for way in range(2):
            far_copy(turn, way).wait_recv()
            joined[turn, way] = (
                piece(turn, near(way), way)[...].astype(jnp.float32)
                + relayed[turn, way].astype(jnp.float32)
            ).astype(jnp.bfloat16)
            join_copy(turn, way).start()

    def middle(turn):
        total = part[turn, pl.ds(pl.multiple_of(z * rows, rows), rows), :].astype(jnp.float32)
        for way in range(2):
            sum_copy(turn, way).wait_recv()
            join_copy(turn, way).wait_recv()
            total += sums[turn, way].astype(jnp.float32)
        square = total[:, both : both + 1] + total[:, both + 64 : both + 65]
        scale = lax.rsqrt(square * (1.0 / (8 * feats)) + EPS)
        gate = total[:, :half] * scale
        up = total[:, half:both] * scale
        hidden[turn, core, z] = (gate / (1.0 + jnp.exp(-gate)) * up).astype(jnp.bfloat16)
        for way in range(2):
            hid_copy(turn, way, z).start()
        hid_pass(turn, z).start()

    def lap(turn):
        for way in range(2):
            slot = near(1 - way)
            hid_copy(turn, way, slot).wait_recv()
            lap_copy(turn, way, slot).start()
            hid_pass(turn, slot).start()

    def back(turn):
        for way in range(2):
            lap_copy(turn, way, z_peer(2)).wait_recv()
        hid_pass(turn, z_peer(2)).start()
        for k in range(4):
            hid_passed(turn, z_peer(k)).wait_recv()
        place = pl.ds(pl.multiple_of(turn * group, group), group)

        @pl.loop(0, feats // 256)
        def _(tile):
            cols = pl.ds(pl.multiple_of(tile * 256, 256), 256)
            total = jnp.dot(
                hidden[turn, 0].reshape(group, half),
                down[pl.ds(0, half), cols],
                preferred_element_type=jnp.float32,
            )
            total += jnp.dot(
                hidden[turn, 1].reshape(group, half),
                down[pl.ds(half, half), cols],
                preferred_element_type=jnp.float32,
            )
            delta[place, cols] = total.astype(jnp.bfloat16)

        for k in range(4):
            dx, dy = 0, 0
            for t in range(4):
                dx = jnp.where(turn == t, OFFSETS[4 * t + k][0], dx)
                dy = jnp.where(turn == t, OFFSETS[4 * t + k][1], dy)
            who = lax.rem(x + dx, 4) * 4 + lax.rem(y + dy, 4)
            if k > 0:
                out_copy(turn * 4 + k, who).start()
            else:

                @pl.when(turn > 0)
                def _():
                    out_copy(turn * 4, who).start()

    @pl.loop(0, 8)
    def _(step):
        for late, stage in enumerate((front, relay, middle, lap, back)):

            @pl.when((step >= late) & (step < late + 4))
            def _():
                stage(step - late)

    total_ref[...] = share_ref[...] + delta[0:rows, :].astype(jnp.float32)

    @pl.loop(1, 16)
    def _(k):
        out_in(k).wait_recv()
        total_ref[...] += deltas[k].astype(jnp.float32)

    update = (score_ref[:, 0:1] * total_ref[...]).astype(jnp.bfloat16)
    slot_at = lax.broadcasted_iota(jnp.int32, (slots, rows), 0)
    shard = destination_ref.shape[1]
    taken = take_slots(kept_row_ref[0:1, :], kept_column_ref[:, 0:1], shard, 0)
    give = jnp.where(slot_at == taken, 1.0, 0.0).astype(jnp.bfloat16)
    outbox[...] = jnp.dot(give, update, preferred_element_type=jnp.float32).astype(jnp.bfloat16)

    def box_of(who):
        return pl.ds(pl.multiple_of(who * box, box), box)

    def box_copy(k):
        who = ahead(c, k)
        return remote(
            outbox.at[box_of(who)], inbox.at[box_of(c)], box_send.at[k], box_recv.at[c], (who, m)
        )

    def box_in(who):
        return remote(
            outbox.at[box_of(who)], inbox.at[box_of(who)], box_send.at[0], box_recv.at[who], sibling
        )

    for k in range(1, 16):
        box_copy(k).start()

    inbox[box_of(c), :] = outbox[box_of(c), :]
    slot_at = lax.broadcasted_iota(jnp.int32, (slots, shard), 0)
    sent = send_slots(destination_ref[0:1, :], rows)
    back_to = jnp.where(slot_at == sent, 1.0, 0.0).T.astype(jnp.bfloat16)

    for k in range(1, 16):
        box_in(ahead(c, k)).wait_recv()

    @pl.loop(0, feats // 256)
    def _(tile):
        cols = pl.ds(pl.multiple_of(tile * 256, 256), 256)
        out_ref[:, cols] = jnp.dot(
            back_to, inbox[:, cols], preferred_element_type=jnp.float32
        ).astype(jnp.bfloat16)

    for k in range(1, 7):
        x_copy(k).wait_send()
        for copy in halves(k):
            copy.wait_send()
    for k in range(1, 16):
        out_in(k).wait_send()
        box_copy(k).wait_send()

    @pl.loop(0, 16)
    def _(who):
        x_pass(who).wait_send()

    @pl.loop(0, 4)
    def _(turn):
        for way in range(2):
            far_copy(turn, way).wait_send()
            sum_copy(turn, way).wait_send()
            join_copy(turn, way).wait_send()
            hid_copy(turn, way, z).wait_send()
            lap_copy(turn, way, near(1 - way)).wait_send()
        for k in range(4):
            hid_pass(turn, z_peer(k)).wait_send()


def feed_forward(
    scaled,
    share,
    score,
    kept_row,
    kept_column,
    destination,
    gains,
    gate_weight,
    up_weight,
    gate_half,
    up_half,
    down_weight,
):
    rows, feats = scaled.shape
    cols = gate_weight.shape[1]
    half = cols // 2
    dma = pltpu.SemaphoreType.DMA
    bf16 = jnp.bfloat16
    vmem, anywhere = pl.BlockSpec(memory_space=pltpu.VMEM), pl.BlockSpec(memory_space=pl.ANY)
    return pl.pallas_call(
        mlp_kernel,
        out_shape=jax.ShapeDtypeStruct((destination.shape[1], feats), bf16),
        in_specs=[vmem] * 7 + [anywhere] * 5,
        out_specs=vmem,
        scratch_shapes=[
            pltpu.VMEM((16 * rows, feats), bf16),
            pltpu.VMEM((16 * rows, feats), bf16),
            pltpu.VMEM((8, feats), jnp.float32),
            pltpu.VMEM((8, feats), jnp.float32),
            pltpu.VMEM((2 * feats, cols), bf16),
            pltpu.VMEM((cols, feats), bf16),
            pltpu.VMEM((4, 4 * rows, cols + 128), bf16),
            pltpu.VMEM((4, 2, rows // 2, cols + 128), bf16),
            pltpu.VMEM((4, 2, rows // 2, cols + 128), bf16),
            pltpu.VMEM((4, 2, rows, cols + 128), bf16),
            pltpu.VMEM((4, 2, 4, rows, half), bf16),
            pltpu.VMEM((16 * rows, feats), bf16),
            pltpu.VMEM((16, rows, feats), bf16),
            pltpu.VMEM((rows, feats), jnp.float32),
            pltpu.VMEM((16 * BOX, feats), bf16),
            pltpu.VMEM((16 * BOX, feats), bf16),
            dma((5,)),
            dma((1,)),
            dma((1,)),
            dma((16,)),
            dma((16,)),
            dma((32,)),
            dma((32,)),
        ]
        + [dma((16,))] * 18,
        compiler_params=pltpu.CompilerParams(
            collective_id=3, has_side_effects=True, vmem_limit_bytes=VMEM_BYTES
        ),
        name="feed_forward",
    )(
        scaled,
        share,
        score,
        kept_row,
        kept_column,
        destination,
        gains,
        gate_weight,
        up_weight,
        gate_half,
        up_half,
        down_weight,
    )


def attend_kernel(
    tokens_ref,
    destination_ref,
    kept_row_ref,
    kept_column_ref,
    gains_ref,
    query_ref,
    key_ref,
    value_ref,
    out_weight_ref,
    gate_ref,
    up_ref,
    cosine_ref,
    sine_ref,
    share_ref,
    scaled_ref,
    score_ref,
    gate_half_ref,
    up_half_ref,
    outbox,
    inbox,
    full,
    normed,
    blocks,
    weight,
    out_weight,
    part,
    parts,
    key_value,
    attended,
    delta,
    deltas,
    load_sem,
    swap_send,
    swap_recv,
    box_send,
    box_recv,
    row_send,
    row_recv,
    hop_send,
    hop_recv,
    norm_send,
    norm_recv,
    wide_send,
    wide_recv,
    part_send,
    part_recv,
    kv_send,
    kv_recv,
    att_send,
    att_recv,
    out_send,
    out_recv,
):
    rows, feats = share_ref.shape
    width = query_ref.shape[0]
    slots = outbox.shape[0]
    box = slots // 16
    group = 4 * rows
    cols = weight.shape[1]
    q_cols, kv_cols = query_ref.shape[1], key_ref.shape[1]
    heads = q_cols // HEAD_DIM
    c, m = lax.axis_index("ctx"), lax.axis_index("mp")
    x, y = c // 4, c % 4
    z, core = m // 2, m % 2
    sibling = (c, z * 2 + 1 - core)

    def rows_of(who, count=1):
        return pl.ds(pl.multiple_of(who * (rows * count), rows), rows * count)

    is_home = x == z
    barrier = pltpu.get_barrier_semaphore()

    def x_peer(k):
        return (lax.rem(x + k, 4) * 4 + y, m)

    def y_peer(k):
        return (x * 4 + lax.rem(y + k, 4), m)

    @pl.loop(0, 8)
    def _(k):
        @pl.when(jnp.logical_not(is_home & (k == m)))
        def _():
            pl.semaphore_signal(barrier, inc=1, device_id=(z * 4 + y, k), device_id_type=MESH)

    for k in range(1, 16):
        pl.semaphore_signal(barrier, inc=1, device_id=(ahead(c, k), m), device_id_type=MESH)
    for k in range(1, 4):
        pl.semaphore_signal(
            barrier,
            inc=1,
            device_id=(c, lax.rem(z + k, 4) * 2 + core),
            device_id_type=MESH,
        )
    pl.semaphore_signal(barrier, inc=1, device_id=sibling, device_id_type=MESH)

    band = pl.ds(pl.multiple_of(y * width, width), width)
    loads = [
        pltpu.make_async_copy(query_ref, weight.at[band, pl.ds(0, q_cols)], load_sem.at[0]),
        pltpu.make_async_copy(key_ref, weight.at[band, pl.ds(q_cols, kv_cols)], load_sem.at[1]),
        pltpu.make_async_copy(
            value_ref, weight.at[band, pl.ds(q_cols + kv_cols, kv_cols)], load_sem.at[2]
        ),
        pltpu.make_async_copy(out_weight_ref, out_weight.at[y], load_sem.at[3]),
    ]
    for load in loads:
        load.start()

    slot_at = lax.broadcasted_iota(jnp.int32, (slots, tokens_ref.shape[0]), 0)
    sent = send_slots(destination_ref[0:1, :], rows)
    pick = jnp.where(slot_at == sent, 1.0, 0.0).astype(jnp.bfloat16)

    @pl.loop(0, feats // 256)
    def _(tile):
        cols = pl.ds(pl.multiple_of(tile * 256, 256), 256)
        outbox[:, cols] = jnp.dot(
            pick, tokens_ref[:, cols], preferred_element_type=jnp.float32
        ).astype(jnp.bfloat16)

    def box_of(who):
        return pl.ds(pl.multiple_of(who * box, box), box)

    inbox[box_of(c), :] = outbox[box_of(c), :]
    pl.semaphore_wait(barrier, jnp.where(is_home, 26, 27))

    def box_copy(k):
        who = ahead(c, k)
        return remote(
            outbox.at[box_of(who)], inbox.at[box_of(c)], box_send.at[k], box_recv.at[c], (who, m)
        )

    def box_in(who):
        return remote(
            outbox.at[box_of(who)], inbox.at[box_of(who)], box_send.at[0], box_recv.at[who], sibling
        )

    def weight_copy(k):
        return remote(
            weight.at[band], weight.at[band], wide_send.at[k], wide_recv.at[k], y_peer(k)
        )

    def out_weight_copy(k):
        return remote(
            out_weight.at[y],
            out_weight.at[y],
            wide_send.at[4 + k],
            wide_recv.at[4 + k],
            y_peer(k),
        )

    def weight_lap(k):
        whose = lax.rem(y + 4 - k, 4)
        start = whose * width + (k // 2) * (width // 2)
        there = weight.at[pl.ds(pl.multiple_of(start, width // 2), width // 2)]
        return remote(there, there, wide_send.at[k - 1], wide_recv.at[k - 1], y_peer(k))

    def out_weight_lap(k):
        whose = lax.rem(y + 4 - k, 4)
        there = out_weight.at[whose, pl.ds((k // 2) * (width // 2), width // 2)]
        return remote(there, there, wide_send.at[k + 3], wide_recv.at[k + 3], y_peer(k))

    for k in range(1, 16):
        box_copy(k).start()
    for load in loads:
        load.wait()
    for k in (1, 3):
        weight_copy(k).start()
    for k in range(1, 16):
        box_in(ahead(c, k)).wait_recv()

    slot_at = lax.broadcasted_iota(jnp.int32, (rows, slots), 1)
    taken = take_slots(kept_row_ref[0:1, :], kept_column_ref[:, 0:1], tokens_ref.shape[0], 1)
    take = jnp.where(slot_at == taken, 1.0, 0.0).astype(jnp.bfloat16)
    full[m] = jnp.dot(take, inbox[...], preferred_element_type=jnp.float32).astype(jnp.bfloat16)

    def row_copy(k, who):
        return remote(
            full.at[who],
            full.at[who],
            row_send.at[k],
            row_recv.at[who],
            (c, lax.rem(z + k, 4) * 2 + core),
        )

    def hop(who):
        return remote(full.at[who], full.at[who], hop_send.at[who], hop_recv.at[who], sibling)

    def z_block(k):
        return lax.rem(z + k, 4) * 2 + core

    def z_sibling(k):
        return lax.rem(z + k, 4) * 2 + 1 - core

    for k in (2, 1, 3):
        row_copy(k, m).start()
    hop(m).start()
    for k in (1, 3, 2):
        row_copy(k, z_block(k)).wait_recv()
        hop(z_block(k)).start()
    for k in (0, 1, 3, 2):
        hop(z_sibling(k)).wait_recv()

    for k in (1, 3):
        weight_copy(k).wait_recv()
        weight_lap(k).start()
    square, route = 0.0, 0.0
    for at in range(8):
        wide = full[at].astype(jnp.float32)
        square += jnp.sum(wide * wide, axis=1, keepdims=True)
        route += jnp.sum(wide * gains_ref[8 + at : 9 + at, :], axis=1, keepdims=True)
    scale = lax.rsqrt(square * (1.0 / (8 * feats)) + EPS)
    score_ref[...] = jnp.broadcast_to(1.0 / (1.0 + jnp.exp(-route)), score_ref.shape)
    for at in range(8):
        wide = full[at].astype(jnp.float32) * scale * gains_ref[at : at + 1, :]
        wide = wide.astype(jnp.bfloat16)
        normed[at] = wide

    def norm_copy(k):
        to = lax.rem(x + 4 - k, 4)
        return remote(
            normed.at[pl.ds(2 * to, 2)],
            blocks.at[:, k],
            norm_send.at[k],
            norm_recv.at[k],
            (to * 4 + y, m),
        )

    for k in (1, 3, 2):
        norm_copy(k).start()
    blocks[0, 0] = normed[2 * x]
    blocks[1, 0] = normed[2 * x + 1]
    half = gate_half_ref.shape[1]
    others = pl.ds(pl.multiple_of((1 - core) * half, 128), half)
    swaps = [
        remote(gate_ref.at[:, others], gate_half_ref, swap_send.at[0], swap_recv.at[0], sibling),
        remote(up_ref.at[:, others], up_half_ref, swap_send.at[1], swap_recv.at[1], sibling),
    ]
    for swap in swaps:
        swap.start()

    def part_copy(k):
        return remote(part.at[rows_of(k)], parts.at[k], part_send.at[k], part_recv.at[k], x_peer(k))

    for k in (1, 3, 2):
        norm_copy(k).wait_recv()
    for k in (1, 3):
        weight_lap(k).wait_recv()
    for k in (1, 3):
        out_weight_copy(k).start()

    @pl.loop(0, cols // 256)
    def _(tile):
        at = pl.ds(pl.multiple_of(tile * 256, 256), 256)
        total = jnp.dot(
            blocks[0].reshape(group, feats),
            weight[pl.ds(0, feats), at],
            preferred_element_type=jnp.float32,
        )
        total += jnp.dot(
            blocks[1].reshape(group, feats),
            weight[pl.ds(feats, feats), at],
            preferred_element_type=jnp.float32,
        )
        part[:, at] = total.astype(jnp.bfloat16)
        share_ref[:, at] = total[0:rows]

    for k in (1, 3, 2):
        part_copy(k).start()
    for k in (1, 3, 2):
        part_copy(k).wait_recv()
        share_ref[:, 0:cols] += parts[k].astype(jnp.float32)

    def turned(at):
        head = share_ref[:, at : at + HEAD_DIM]
        swapped = pltpu.roll(head, HEAD_DIM // 2, 1)
        return (head * cosine_ref[...] + swapped * sine_ref[...]).astype(jnp.bfloat16)

    mine = rows_of(c)
    key_value[mine, 0:HEAD_DIM] = turned(q_cols)
    at = q_cols + kv_cols
    key_value[mine, HEAD_DIM : 2 * HEAD_DIM] = share_ref[:, at : at + HEAD_DIM].astype(jnp.bfloat16)

    def kv_copy(k, who, device):
        return remote(
            key_value.at[rows_of(who)],
            key_value.at[rows_of(who)],
            kv_send.at[k],
            kv_recv.at[who],
            device,
        )

    for k in range(1, 16):
        kv_copy(k, c, (behind(c, k), m)).start()

    queries = jnp.concatenate([turned(h * HEAD_DIM) for h in range(heads)], axis=0)

    for k in range(1, 16):
        kv_copy(k, ahead(c, k), sibling).wait_recv()
    for k in (1, 3):
        out_weight_copy(k).wait_recv()
        out_weight_lap(k).start()

    keys = 16 * rows
    scores = lax.dot_general(
        queries,
        key_value[:, 0:HEAD_DIM],
        (((1,), (1,)), ((), ())),
        preferred_element_type=jnp.float32,
    ) * (HEAD_DIM ** (-0.5))
    query_at = lax.broadcasted_iota(jnp.int32, (heads * rows, keys), 0) % rows * 16 + c
    key_at = lax.broadcasted_iota(jnp.int32, (heads * rows, keys), 1)
    allowed = key_at % rows * 16 + key_at // rows <= query_at
    scores = jnp.where(allowed, scores, -1e30)
    weights = jnp.exp(scores - jnp.max(scores, axis=1, keepdims=True))
    weights = jnp.where(allowed, weights, 0.0)
    total = jnp.sum(weights, axis=1, keepdims=True)
    mixed = (
        jnp.dot(
            weights.astype(jnp.bfloat16),
            key_value[:, HEAD_DIM : 2 * HEAD_DIM],
            preferred_element_type=jnp.float32,
        )
        / total
    ).astype(jnp.bfloat16)
    for h in range(heads):
        attended[0:rows, h * HEAD_DIM : (h + 1) * HEAD_DIM] = mixed[h * rows : (h + 1) * rows]

    def att_copy(k):
        to = lax.rem(x + 4 - k, 4)
        return remote(
            attended.at[0:rows],
            attended.at[rows_of(k)],
            att_send.at[k],
            att_recv.at[k],
            (to * 4 + y, m),
        )

    for k in (1, 3, 2):
        att_copy(k).start()

    def out_copy(k, side):
        return remote(
            delta.at[side, rows_of(k)],
            deltas.at[m],
            out_send.at[2 * k + side],
            out_recv.at[m],
            (lax.rem(x + k, 4) * 4 + y, 2 * x + side),
        )

    def out_in(slot):
        return remote(
            delta.at[0, pl.ds(0, rows)],
            deltas.at[slot],
            out_send.at[slot],
            out_recv.at[slot],
            sibling,
        )

    for k in (1, 3):
        out_weight_lap(k).wait_recv()
    for k in (1, 3, 2):
        att_copy(k).wait_recv()
    for side in range(2):
        for at in range(2):
            delta[side, :, at * width : (at + 1) * width] = jnp.dot(
                attended[...], out_weight[2 * side + at], preferred_element_type=jnp.float32
            ).astype(jnp.bfloat16)
        for k in (2, 1, 3):
            out_copy(k, side).start()

        @pl.when(jnp.logical_not(is_home & (side == core)))
        def _():
            out_copy(0, side).start()

    @pl.when(is_home)
    def _():
        deltas[m] = delta[core, 0:rows, :]

    share_ref[...] = jnp.zeros_like(share_ref)

    @pl.loop(0, 8)
    def _(k):
        slot = lax.rem(k + m, 8)

        @pl.when(jnp.logical_not(is_home & (slot == m)))
        def _():
            out_in(slot).wait_recv()

        share_ref[...] += deltas[slot].astype(jnp.float32)

    mixed = full[m].astype(jnp.float32) + share_ref[...]
    scaled_ref[...] = (mixed * gains_ref[16:17, :]).astype(jnp.bfloat16)

    for k in range(1, 4):
        row_copy(k, m).wait_send()
    for k in range(4):
        hop(z_block(k)).wait_send()

    for swap in swaps:
        swap.wait()

    for k in (1, 3):
        weight_copy(k).wait_send()
        weight_lap(k).wait_send()
        out_weight_copy(k).wait_send()
        out_weight_lap(k).wait_send()
    for side in range(2):
        for k in range(1, 4):
            out_copy(k, side).wait_send()

        @pl.when(jnp.logical_not(is_home & (side == core)))
        def _():
            out_copy(0, side).wait_send()

    for k in range(1, 4):
        norm_copy(k).wait_send()
        part_copy(k).wait_send()
        att_copy(k).wait_send()
    for k in range(1, 16):
        box_copy(k).wait_send()
        kv_copy(k, c, sibling).wait_send()


def attend(
    tokens, destination, kept_row, kept_column, gains, query, key, value, out_weight, gate, up, cosine, sine
):
    count, slots = kept_column.shape[0], 16 * BOX
    feats = tokens.shape[1]
    width = query.shape[0]
    cols = query.shape[1] + key.shape[1] + value.shape[1]
    dma = pltpu.SemaphoreType.DMA
    bf16 = jnp.bfloat16
    vmem, anywhere = pl.BlockSpec(memory_space=pltpu.VMEM), pl.BlockSpec(memory_space=pl.ANY)
    return pl.pallas_call(
        attend_kernel,
        out_shape=(
            jax.ShapeDtypeStruct((count, feats), jnp.float32),
            jax.ShapeDtypeStruct((count, feats), bf16),
            jax.ShapeDtypeStruct((count, 128), jnp.float32),
            jax.ShapeDtypeStruct((gate.shape[0], gate.shape[1] // 2), bf16),
            jax.ShapeDtypeStruct((up.shape[0], up.shape[1] // 2), bf16),
        ),
        in_specs=[vmem] * 5 + [anywhere] * 6 + [vmem] * 2,
        out_specs=(vmem, vmem, vmem, anywhere, anywhere),
        scratch_shapes=[
            pltpu.VMEM((slots, feats), bf16),
            pltpu.VMEM((slots, feats), bf16),
            pltpu.VMEM((8, count, feats), bf16),
            pltpu.VMEM((8, count, feats), bf16),
            pltpu.VMEM((2, 4, count, feats), bf16),
            pltpu.VMEM((4 * width, cols), bf16),
            pltpu.VMEM((4, *out_weight.shape), bf16),
            pltpu.VMEM((4 * count, cols), bf16),
            pltpu.VMEM((4, count, cols), bf16),
            pltpu.VMEM((16 * count, 2 * HEAD_DIM), bf16),
            pltpu.VMEM((4 * count, query.shape[1]), bf16),
            pltpu.VMEM((2, 4 * count, feats), bf16),
            pltpu.VMEM((8, count, feats), bf16),
            dma((4,)),
            dma((2,)),
            dma((2,)),
        ]
        + [dma((16,))] * 18,
        compiler_params=pltpu.CompilerParams(
            collective_id=2, has_side_effects=True, vmem_limit_bytes=VMEM_BYTES
        ),
        name="attend",
    )(
        tokens,
        destination,
        kept_row,
        kept_column,
        gains,
        query,
        key,
        value,
        out_weight,
        gate,
        up,
        cosine,
        sine,
    )


def body(
    tokens,
    norm_gain,
    router_weight,
    query_weight,
    key_weight,
    value_weight,
    out_weight,
    mlp_gain,
    gate_weight,
    up_weight,
    down_weight,
    destination,
    kept_pos,
):
    tok_dev, feature_cols = tokens.shape
    kept_dev = kept_pos.shape[0]
    half_dim = HEAD_DIM // 2
    exponent = jnp.arange(half_dim, dtype=jnp.float32) * (2.0 / HEAD_DIM)
    angles = kept_pos.astype(jnp.float32)[:, None] * (500000.0 ** (-exponent))[None, :]
    cosine, sine = jnp.cos(angles), jnp.sin(angles)
    gains = jnp.concatenate(
        [
            norm_gain.reshape(8, feature_cols),
            router_weight.reshape(8, feature_cols),
            jnp.broadcast_to(mlp_gain, (8, feature_cols)),
        ]
    ).astype(jnp.float32)
    destinations = jnp.broadcast_to(destination, (8, tok_dev))
    kept_row = jnp.broadcast_to(kept_pos, (8, kept_dev))
    kept_column = jnp.broadcast_to(kept_pos[:, None], (kept_dev, 128))
    head_share, scaled, score, gate_half, up_half = attend(
        tokens,
        destinations,
        kept_row,
        kept_column,
        gains,
        query_weight,
        key_weight,
        value_weight,
        out_weight,
        gate_weight,
        up_weight,
        jnp.concatenate([cosine, cosine], axis=1),
        jnp.concatenate([-sine, sine], axis=1),
    )
    arrived = feed_forward(
        scaled,
        head_share,
        score,
        kept_row,
        kept_column,
        destinations,
        gains,
        gate_weight,
        up_weight,
        gate_half,
        up_half,
        down_weight,
    )
    return (tokens.astype(jnp.float32) + arrived.astype(jnp.float32)).astype(jnp.bfloat16)


def solution(mesh):
    in_specs = (
        P("ctx", "mp"),
        P(),
        P(),
        P("ctx", "mp"),
        P("ctx", "mp"),
        P("ctx", "mp"),
        P("mp", "ctx"),
        P("mp"),
        P("mp", "ctx"),
        P("mp", "ctx"),
        P("ctx", "mp"),
        P("ctx"),
        P("ctx"),
    )
    out_specs = P("ctx", "mp")
    return jax.shard_map(body, mesh=mesh, in_specs=in_specs, out_specs=out_specs, check_vma=False)
```

```python
import jax
import jax.numpy as jnp
from jax import lax
from jax.sharding import PartitionSpec as P

from jax.experimental import pallas as pl
from jax.experimental.pallas import tpu as pltpu

HEAD_DIM = 128
BOX = 16
VMEM_BYTES = 60 * 2**20
MESH = pl.DeviceIdType.MESH
OFFSETS = (
    (0, 0), (0, 1), (1, 0), (0, 3), (3, 0), (0, 2), (2, 0), (1, 1),
    (3, 3), (1, 3), (3, 1), (1, 2), (2, 1), (3, 2), (2, 3), (2, 2),
)
EPS = 1e-05


def ahead(c, k):
    dx, dy = OFFSETS[k]
    return lax.rem(c // 4 + dx, 4) * 4 + lax.rem(c % 4 + dy, 4)


def behind(c, k):
    dx, dy = OFFSETS[k]
    return lax.rem(c // 4 + 4 - dx, 4) * 4 + lax.rem(c % 4 + 4 - dy, 4)


def send_slots(destination, kept):
    owner, slot = destination // kept, destination % kept
    going = destination >= 0
    order = jnp.where(going, slot * 16 + owner, 16 * kept)
    first = (jnp.min(order) - owner + 15) // 16
    return jnp.where(going, owner * BOX + slot - first, 16 * BOX)


def take_slots(row, column, shard, axis):
    kept = row.shape[1]
    same = column // shard == row // shard
    at = lax.broadcasted_iota(jnp.int32, (kept, kept), axis)
    first = jnp.min(jnp.where(same, at, kept), axis=axis, keepdims=True)
    mine = row if axis == 0 else column
    return mine // shard * BOX + lax.broadcasted_iota(jnp.int32, mine.shape, 1 - axis) - first


def remote(source, target, sent, landed, device):
    return pltpu.make_async_remote_copy(
        src_ref=source,
        dst_ref=target,
        send_sem=sent,
        recv_sem=landed,
        device_id=device,
        device_id_type=MESH,
    )


def mlp_kernel(
    x_ref,
    share_ref,
    score_ref,
    kept_row_ref,
    kept_column_ref,
    destination_ref,
    gains_ref,
    gate_ref,
    up_ref,
    gate_half_ref,
    up_half_ref,
    down_ref,
    out_ref,
    own_x,
    sib_x,
    own_gain,
    sib_gain,
    weight,
    down,
    part,
    relayed,
    joined,
    sums,
    hidden,
    delta,
    deltas,
    total_ref,
    outbox,
    inbox,
    load_sem,
    swap_send,
    swap_recv,
    x_send,
    x_recv,
    half_send,
    half_recv,
    pass_send,
    pass_recv,
    far_send,
    far_recv,
    sum_send,
    sum_recv,
    join_send,
    join_recv,
    hid_send,
    hid_recv,
    lap_send,
    lap_recv,
    hop_send,
    hop_recv,
    out_send,
    out_recv,
    box_send,
    box_recv,
):
    rows, feats = x_ref.shape
    slots = outbox.shape[0]
    box = slots // 16
    half = gate_ref.shape[1] // 2
    both = 2 * half
    group = 4 * rows
    c, m = lax.axis_index("ctx"), lax.axis_index("mp")
    x, y = c // 4, c % 4
    z, core = m // 2, m % 2
    sibling = (c, z * 2 + 1 - core)

    def z_peer(step):
        return lax.rem(z + step, 4)

    barrier = pltpu.get_barrier_semaphore()

    for k in range(1, 16):
        pl.semaphore_signal(barrier, inc=1, device_id=(ahead(c, k), m), device_id_type=MESH)

    for k in (1, 3):
        pl.semaphore_signal(
            barrier, inc=1, device_id=(c, z_peer(k) * 2 + core), device_id_type=MESH
        )
    pl.semaphore_signal(barrier, inc=1, device_id=sibling, device_id_type=MESH)

    mine = pl.multiple_of(core * half, 128)
    loads = [
        pltpu.make_async_copy(
            gate_ref.at[:, pl.ds(mine, half)],
            weight.at[pl.ds(0, feats), pl.ds(0, half)],
            load_sem.at[0],
        ),
        pltpu.make_async_copy(
            up_ref.at[:, pl.ds(mine, half)],
            weight.at[pl.ds(0, feats), pl.ds(half, half)],
            load_sem.at[1],
        ),
        pltpu.make_async_copy(
            gate_half_ref, weight.at[pl.ds(feats, feats), pl.ds(0, half)], load_sem.at[2]
        ),
        pltpu.make_async_copy(
            up_half_ref, weight.at[pl.ds(feats, feats), pl.ds(half, half)], load_sem.at[3]
        ),
        pltpu.make_async_copy(down_ref, down, load_sem.at[4]),
    ]
    for load in loads:
        load.start()
    own_x[0:rows, :] = x_ref[...]
    own_gain[...] = 1.0 / gains_ref[16:24, :]
    pl.semaphore_wait(barrier, 18)

    def x_copy(k):
        place = pl.ds(k * rows, rows)
        return remote(x_ref, own_x.at[place], x_send.at[k], x_recv.at[k], (behind(c, k), m))

    def x_in(slot):
        place = pl.ds(pl.multiple_of(slot * rows, rows), rows)
        return remote(x_ref, own_x.at[place], x_send.at[slot], x_recv.at[slot], sibling)

    def x_pass(who):
        place = pl.ds(pl.multiple_of(who * rows, rows), rows)
        return remote(
            own_x.at[place], sib_x.at[place], pass_send.at[who], pass_recv.at[who], sibling
        )

    short = rows // 2

    def half_copy(dx, dy, side):
        slot = OFFSETS.index((dx, dy))
        source = OFFSETS.index((0, dy) if side else (dx, 0))
        to = lax.rem(x + 4 - dx, 4) * 4 + y if side else x * 4 + lax.rem(y + 4 - dy, 4)
        return remote(
            own_x.at[pl.ds(source * rows + side * short, short)],
            own_x.at[pl.ds(slot * rows + side * short, short)],
            half_send.at[side * 16 + slot],
            half_recv.at[side * 16 + slot],
            (to, m),
        )

    def half_in(slot, side):
        start = pl.multiple_of(slot * rows + side * short, short)
        return remote(
            own_x.at[pl.ds(0, short)],
            own_x.at[pl.ds(start, short)],
            half_send.at[0],
            half_recv.at[side * 16 + slot],
            sibling,
        )

    def halves(slot):
        dx, dy = OFFSETS[slot]
        if dx:
            return [half_copy(dx, k, 0) for k in range(1, 4)]
        return [half_copy(k, dy, 1) for k in range(1, 4)]

    for k in range(1, 7):
        x_copy(k).start()
    gain_swap = remote(own_gain, sib_gain, swap_send.at[0], swap_recv.at[0], sibling)
    x_pass(0).start()
    gain_swap.start()

    def near(way):
        return z_peer(1 + 2 * way)

    def chip(way):
        return (c, near(way) * 2 + core)

    def piece(turn, to, side):
        return part.at[turn, pl.ds(pl.multiple_of(to * rows + side * short, short), short)]

    def far_copy(turn, way):
        at = turn * 2 + way
        return remote(
            piece(turn, z_peer(2), way),
            relayed.at[turn, way],
            far_send.at[at],
            far_recv.at[at],
            chip(way),
        )

    def sum_copy(turn, way):
        at = turn * 2 + way
        return remote(
            piece(turn, near(way), 1 - way),
            sums.at[turn, way, pl.ds((1 - way) * short, short)],
            sum_send.at[at],
            sum_recv.at[at],
            chip(way),
        )

    def join_copy(turn, way):
        at = turn * 2 + way
        return remote(
            joined.at[turn, way],
            sums.at[turn, way, pl.ds(way * short, short)],
            join_send.at[at],
            join_recv.at[at],
            chip(way),
        )

    def hid_copy(turn, way, slot):
        at = turn * 2 + way
        return remote(
            hidden.at[turn, core, slot],
            hidden.at[turn, core, slot],
            hid_send.at[at],
            hid_recv.at[at],
            chip(way),
        )

    def lap_copy(turn, way, slot):
        at = turn * 2 + way
        there = hidden.at[turn, core, slot, pl.ds(way * short, short)]
        return remote(there, there, lap_send.at[at], lap_recv.at[at], chip(way))

    def hid_pass(turn, at):
        return remote(
            hidden.at[turn, core, at],
            hidden.at[turn, core, at],
            hop_send.at[turn * 4 + at],
            hop_recv.at[turn * 4 + at],
            sibling,
        )

    def hid_passed(turn, at):
        return remote(
            hidden.at[turn, 1 - core, at],
            hidden.at[turn, 1 - core, at],
            hop_send.at[turn * 4 + at],
            hop_recv.at[turn * 4 + at],
            sibling,
        )

    def out_copy(slot, who):
        return remote(
            delta.at[pl.ds(pl.multiple_of(slot * rows, rows), rows)],
            deltas.at[slot],
            out_send.at[slot],
            out_recv.at[slot],
            (who, m),
        )

    def out_in(slot):
        return remote(
            delta.at[pl.ds(0, rows)], deltas.at[slot], out_send.at[slot], out_recv.at[slot], sibling
        )

    def front(turn):
        @pl.loop(0, 4)
        def _(k):
            slot = turn * 4 + k

            @pl.when((slot > 0) & (slot < 7))
            def _():
                x_in(slot).wait_recv()

            @pl.when(slot >= 7)
            def _():
                half_in(slot, 0).wait_recv()
                half_in(slot, 1).wait_recv()

            @pl.when(slot > 0)
            def _():
                x_pass(slot).start()

        for t in range(2):

            @pl.when(turn == t)
            def _():
                for slot in range(3 * t + 1, 3 * t + 4):
                    for copy in halves(slot):
                        copy.start()

        @pl.when(turn == 0)
        def _():
            for load in loads:
                load.wait()
            gain_swap.wait()

        @pl.loop(0, 4)
        def _(k):
            x_pass(turn * 4 + k).wait_recv()

        place = pl.ds(pl.multiple_of(turn * group, group), group)
        mixed = own_x[place, :].astype(jnp.float32) * own_gain[0:1, :]
        square = jnp.sum(mixed * mixed, axis=1, keepdims=True)
        mixed = sib_x[place, :].astype(jnp.float32) * sib_gain[0:1, :]
        square = square + jnp.sum(mixed * mixed, axis=1, keepdims=True)
        square = jnp.broadcast_to(square, (group, 128))
        coarse = square.astype(jnp.bfloat16)
        fine = (square - coarse.astype(jnp.float32)).astype(jnp.bfloat16)
        lane = lax.broadcasted_iota(jnp.int32, (group, 128), 1)
        part[turn, :, pl.ds(both, 128)] = jnp.where(lane < 64, coarse, fine)

        @pl.loop(0, both // 256)
        def _(tile):
            cols = pl.ds(pl.multiple_of(tile * 256, 256), 256)
            total = jnp.dot(
                own_x[place, :], weight[pl.ds(0, feats), cols], preferred_element_type=jnp.float32
            )
            total += jnp.dot(
                sib_x[place, :],
                weight[pl.ds(feats, feats), cols],
                preferred_element_type=jnp.float32,
            )
            part[turn, :, cols] = total.astype(jnp.bfloat16)

        for way in range(2):
            far_copy(turn, way).start()
        for way in range(2):
            sum_copy(turn, way).start()

    def relay(turn):
        for way in range(2):
            far_copy(turn, way).wait_recv()
            joined[turn, way] = (
                piece(turn, near(way), way)[...].astype(jnp.float32)
                + relayed[turn, way].astype(jnp.float32)
            ).astype(jnp.bfloat16)
            join_copy(turn, way).start()

    def middle(turn):
        total = part[turn, pl.ds(pl.multiple_of(z * rows, rows), rows), :].astype(jnp.float32)
        for way in range(2):
            sum_copy(turn, way).wait_recv()
            join_copy(turn, way).wait_recv()
            total += sums[turn, way].astype(jnp.float32)
        square = total[:, both : both + 1] + total[:, both + 64 : both + 65]
        scale = lax.rsqrt(square * (1.0 / (8 * feats)) + EPS)
        gate = total[:, :half] * scale
        up = total[:, half:both] * scale
        hidden[turn, core, z] = (gate / (1.0 + jnp.exp(-gate)) * up).astype(jnp.bfloat16)
        for way in range(2):
            hid_copy(turn, way, z).start()
        hid_pass(turn, z).start()

    def lap(turn):
        for way in range(2):
            slot = near(1 - way)
            hid_copy(turn, way, slot).wait_recv()
            lap_copy(turn, way, slot).start()
            hid_pass(turn, slot).start()

    def back(turn):
        for way in range(2):
            lap_copy(turn, way, z_peer(2)).wait_recv()
        hid_pass(turn, z_peer(2)).start()
        for k in range(4):
            hid_passed(turn, z_peer(k)).wait_recv()
        place = pl.ds(pl.multiple_of(turn * group, group), group)

        @pl.loop(0, feats // 256)
        def _(tile):
            cols = pl.ds(pl.multiple_of(tile * 256, 256), 256)
            total = jnp.dot(
                hidden[turn, 0].reshape(group, half),
                down[pl.ds(0, half), cols],
                preferred_element_type=jnp.float32,
            )
            total += jnp.dot(
                hidden[turn, 1].reshape(group, half),
                down[pl.ds(half, half), cols],
                preferred_element_type=jnp.float32,
            )
            delta[place, cols] = total.astype(jnp.bfloat16)

        for k in range(4):
            dx, dy = 0, 0
            for t in range(4):
                dx = jnp.where(turn == t, OFFSETS[4 * t + k][0], dx)
                dy = jnp.where(turn == t, OFFSETS[4 * t + k][1], dy)
            who = lax.rem(x + dx, 4) * 4 + lax.rem(y + dy, 4)
            if k > 0:
                out_copy(turn * 4 + k, who).start()
            else:

                @pl.when(turn > 0)
                def _():
                    out_copy(turn * 4, who).start()

    @pl.loop(0, 8)
    def _(step):
        for late, stage in enumerate((front, relay, middle, lap, back)):

            @pl.when((step >= late) & (step < late + 4))
            def _():
                stage(step - late)

    total_ref[...] = share_ref[...] + delta[0:rows, :].astype(jnp.float32)

    @pl.loop(1, 16)
    def _(k):
        out_in(k).wait_recv()
        total_ref[...] += deltas[k].astype(jnp.float32)

    update = (score_ref[:, 0:1] * total_ref[...]).astype(jnp.bfloat16)
    slot_at = lax.broadcasted_iota(jnp.int32, (slots, rows), 0)
    shard = destination_ref.shape[1]
    taken = take_slots(kept_row_ref[0:1, :], kept_column_ref[:, 0:1], shard, 0)
    give = jnp.where(slot_at == taken, 1.0, 0.0).astype(jnp.bfloat16)
    outbox[...] = jnp.dot(give, update, preferred_element_type=jnp.float32).astype(jnp.bfloat16)

    def box_of(who):
        return pl.ds(pl.multiple_of(who * box, box), box)

    def box_copy(k):
        who = ahead(c, k)
        return remote(
            outbox.at[box_of(who)], inbox.at[box_of(c)], box_send.at[k], box_recv.at[c], (who, m)
        )

    def box_in(who):
        return remote(
            outbox.at[box_of(who)], inbox.at[box_of(who)], box_send.at[0], box_recv.at[who], sibling
        )

    for k in range(1, 16):
        box_copy(k).start()

    inbox[box_of(c), :] = outbox[box_of(c), :]
    slot_at = lax.broadcasted_iota(jnp.int32, (slots, shard), 0)
    sent = send_slots(destination_ref[0:1, :], rows)
    back_to = jnp.where(slot_at == sent, 1.0, 0.0).T.astype(jnp.bfloat16)

    for k in range(1, 16):
        box_in(ahead(c, k)).wait_recv()

    @pl.loop(0, feats // 256)
    def _(tile):
        cols = pl.ds(pl.multiple_of(tile * 256, 256), 256)
        out_ref[:, cols] = jnp.dot(
            back_to, inbox[:, cols], preferred_element_type=jnp.float32
        ).astype(jnp.bfloat16)

    for k in range(1, 7):
        x_copy(k).wait_send()
        for copy in halves(k):
            copy.wait_send()
    for k in range(1, 16):
        out_in(k).wait_send()
        box_copy(k).wait_send()

    @pl.loop(0, 16)
    def _(who):
        x_pass(who).wait_send()

    @pl.loop(0, 4)
    def _(turn):
        for way in range(2):
            far_copy(turn, way).wait_send()
            sum_copy(turn, way).wait_send()
            join_copy(turn, way).wait_send()
            hid_copy(turn, way, z).wait_send()
            lap_copy(turn, way, near(1 - way)).wait_send()
        for k in range(4):
            hid_pass(turn, z_peer(k)).wait_send()


def feed_forward(
    scaled,
    share,
    score,
    kept_row,
    kept_column,
    destination,
    gains,
    gate_weight,
    up_weight,
    gate_half,
    up_half,
    down_weight,
):
    rows, feats = scaled.shape
    cols = gate_weight.shape[1]
    half = cols // 2
    dma = pltpu.SemaphoreType.DMA
    bf16 = jnp.bfloat16
    vmem, anywhere = pl.BlockSpec(memory_space=pltpu.VMEM), pl.BlockSpec(memory_space=pl.ANY)
    return pl.pallas_call(
        mlp_kernel,
        out_shape=jax.ShapeDtypeStruct((destination.shape[1], feats), bf16),
        in_specs=[vmem] * 7 + [anywhere] * 5,
        out_specs=vmem,
        scratch_shapes=[
            pltpu.VMEM((16 * rows, feats), bf16),
            pltpu.VMEM((16 * rows, feats), bf16),
            pltpu.VMEM((8, feats), jnp.float32),
            pltpu.VMEM((8, feats), jnp.float32),
            pltpu.VMEM((2 * feats, cols), bf16),
            pltpu.VMEM((cols, feats), bf16),
            pltpu.VMEM((4, 4 * rows, cols + 128), bf16),
            pltpu.VMEM((4, 2, rows // 2, cols + 128), bf16),
            pltpu.VMEM((4, 2, rows // 2, cols + 128), bf16),
            pltpu.VMEM((4, 2, rows, cols + 128), bf16),
            pltpu.VMEM((4, 2, 4, rows, half), bf16),
            pltpu.VMEM((16 * rows, feats), bf16),
            pltpu.VMEM((16, rows, feats), bf16),
            pltpu.VMEM((rows, feats), jnp.float32),
            pltpu.VMEM((16 * BOX, feats), bf16),
            pltpu.VMEM((16 * BOX, feats), bf16),
            dma((5,)),
            dma((1,)),
            dma((1,)),
            dma((16,)),
            dma((16,)),
            dma((32,)),
            dma((32,)),
        ]
        + [dma((16,))] * 18,
        compiler_params=pltpu.CompilerParams(
            collective_id=3, has_side_effects=True, vmem_limit_bytes=VMEM_BYTES
        ),
        name="feed_forward",
    )(
        scaled,
        share,
        score,
        kept_row,
        kept_column,
        destination,
        gains,
        gate_weight,
        up_weight,
        gate_half,
        up_half,
        down_weight,
    )


def attend_kernel(
    tokens_ref,
    destination_ref,
    kept_row_ref,
    kept_column_ref,
    gains_ref,
    query_ref,
    key_ref,
    value_ref,
    out_weight_ref,
    gate_ref,
    up_ref,
    cosine_ref,
    sine_ref,
    share_ref,
    scaled_ref,
    score_ref,
    gate_half_ref,
    up_half_ref,
    outbox,
    inbox,
    full,
    normed,
    blocks,
    weight,
    out_weight,
    part,
    parts,
    key_value,
    attended,
    delta,
    deltas,
    load_sem,
    swap_send,
    swap_recv,
    box_send,
    box_recv,
    row_send,
    row_recv,
    hop_send,
    hop_recv,
    norm_send,
    norm_recv,
    wide_send,
    wide_recv,
    part_send,
    part_recv,
    kv_send,
    kv_recv,
    att_send,
    att_recv,
    out_send,
    out_recv,
):
    rows, feats = share_ref.shape
    width = query_ref.shape[0]
    slots = outbox.shape[0]
    box = slots // 16
    group = 4 * rows
    cols = weight.shape[1]
    q_cols, kv_cols = query_ref.shape[1], key_ref.shape[1]
    heads = q_cols // HEAD_DIM
    c, m = lax.axis_index("ctx"), lax.axis_index("mp")
    x, y = c // 4, c % 4
    z, core = m // 2, m % 2
    sibling = (c, z * 2 + 1 - core)

    def rows_of(who, count=1):
        return pl.ds(pl.multiple_of(who * (rows * count), rows), rows * count)

    is_home = x == z
    barrier = pltpu.get_barrier_semaphore()

    def x_peer(k):
        return (lax.rem(x + k, 4) * 4 + y, m)

    def y_peer(k):
        return (x * 4 + lax.rem(y + k, 4), m)

    @pl.loop(0, 8)
    def _(k):
        @pl.when(jnp.logical_not(is_home & (k == m)))
        def _():
            pl.semaphore_signal(barrier, inc=1, device_id=(z * 4 + y, k), device_id_type=MESH)

    for k in range(1, 16):
        pl.semaphore_signal(barrier, inc=1, device_id=(ahead(c, k), m), device_id_type=MESH)
    for k in range(1, 4):
        pl.semaphore_signal(
            barrier,
            inc=1,
            device_id=(c, lax.rem(z + k, 4) * 2 + core),
            device_id_type=MESH,
        )
    pl.semaphore_signal(barrier, inc=1, device_id=sibling, device_id_type=MESH)

    band = pl.ds(pl.multiple_of(y * width, width), width)
    loads = [
        pltpu.make_async_copy(query_ref, weight.at[band, pl.ds(0, q_cols)], load_sem.at[0]),
        pltpu.make_async_copy(key_ref, weight.at[band, pl.ds(q_cols, kv_cols)], load_sem.at[1]),
        pltpu.make_async_copy(
            value_ref, weight.at[band, pl.ds(q_cols + kv_cols, kv_cols)], load_sem.at[2]
        ),
        pltpu.make_async_copy(out_weight_ref, out_weight.at[y], load_sem.at[3]),
    ]
    for load in loads:
        load.start()

    slot_at = lax.broadcasted_iota(jnp.int32, (slots, tokens_ref.shape[0]), 0)
    sent = send_slots(destination_ref[0:1, :], rows)
    pick = jnp.where(slot_at == sent, 1.0, 0.0).astype(jnp.bfloat16)

    @pl.loop(0, feats // 256)
    def _(tile):
        cols = pl.ds(pl.multiple_of(tile * 256, 256), 256)
        outbox[:, cols] = jnp.dot(
            pick, tokens_ref[:, cols], preferred_element_type=jnp.float32
        ).astype(jnp.bfloat16)

    def box_of(who):
        return pl.ds(pl.multiple_of(who * box, box), box)

    inbox[box_of(c), :] = outbox[box_of(c), :]
    pl.semaphore_wait(barrier, jnp.where(is_home, 26, 27))

    def box_copy(k):
        who = ahead(c, k)
        return remote(
            outbox.at[box_of(who)], inbox.at[box_of(c)], box_send.at[k], box_recv.at[c], (who, m)
        )

    def box_in(who):
        return remote(
            outbox.at[box_of(who)], inbox.at[box_of(who)], box_send.at[0], box_recv.at[who], sibling
        )

    def weight_copy(k):
        return remote(
            weight.at[band], weight.at[band], wide_send.at[k], wide_recv.at[k], y_peer(k)
        )

    def out_weight_copy(k):
        return remote(
            out_weight.at[y],
            out_weight.at[y],
            wide_send.at[4 + k],
            wide_recv.at[4 + k],
            y_peer(k),
        )

    def weight_lap(k):
        whose = lax.rem(y + 4 - k, 4)
        start = whose * width + (k // 2) * (width // 2)
        there = weight.at[pl.ds(pl.multiple_of(start, width // 2), width // 2)]
        return remote(there, there, wide_send.at[k - 1], wide_recv.at[k - 1], y_peer(k))

    def out_weight_lap(k):
        whose = lax.rem(y + 4 - k, 4)
        there = out_weight.at[whose, pl.ds((k // 2) * (width // 2), width // 2)]
        return remote(there, there, wide_send.at[k + 3], wide_recv.at[k + 3], y_peer(k))

    for k in range(1, 16):
        box_copy(k).start()
    for load in loads:
        load.wait()
    for k in (1, 3):
        weight_copy(k).start()
    for k in range(1, 16):
        box_in(ahead(c, k)).wait_recv()

    slot_at = lax.broadcasted_iota(jnp.int32, (rows, slots), 1)
    taken = take_slots(kept_row_ref[0:1, :], kept_column_ref[:, 0:1], tokens_ref.shape[0], 1)
    take = jnp.where(slot_at == taken, 1.0, 0.0).astype(jnp.bfloat16)
    full[m] = jnp.dot(take, inbox[...], preferred_element_type=jnp.float32).astype(jnp.bfloat16)

    def row_copy(k, who):
        return remote(
            full.at[who],
            full.at[who],
            row_send.at[k],
            row_recv.at[who],
            (c, lax.rem(z + k, 4) * 2 + core),
        )

    def hop(who):
        return remote(full.at[who], full.at[who], hop_send.at[who], hop_recv.at[who], sibling)

    def z_block(k):
        return lax.rem(z + k, 4) * 2 + core

    def z_sibling(k):
        return lax.rem(z + k, 4) * 2 + 1 - core

    for k in (2, 1, 3):
        row_copy(k, m).start()
    hop(m).start()
    for k in (1, 3, 2):
        row_copy(k, z_block(k)).wait_recv()
        hop(z_block(k)).start()
    for k in (0, 1, 3, 2):
        hop(z_sibling(k)).wait_recv()

    square, route = 0.0, 0.0
    for at in range(8):
        wide = full[at].astype(jnp.float32)
        square += jnp.sum(wide * wide, axis=1, keepdims=True)
        route += jnp.sum(wide * gains_ref[8 + at : 9 + at, :], axis=1, keepdims=True)
    scale = lax.rsqrt(square * (1.0 / (8 * feats)) + EPS)
    score_ref[...] = jnp.broadcast_to(1.0 / (1.0 + jnp.exp(-route)), score_ref.shape)
    for at in range(8):
        wide = full[at].astype(jnp.float32) * scale * gains_ref[at : at + 1, :]
        wide = wide.astype(jnp.bfloat16)
        normed[at] = wide

    def norm_copy(k):
        to = lax.rem(x + 4 - k, 4)
        return remote(
            normed.at[pl.ds(2 * to, 2)],
            blocks.at[:, k],
            norm_send.at[k],
            norm_recv.at[k],
            (to * 4 + y, m),
        )

    for k in (1, 3, 2):
        norm_copy(k).start()
    blocks[0, 0] = normed[2 * x]
    blocks[1, 0] = normed[2 * x + 1]
    for k in (1, 3):
        weight_copy(k).wait_recv()
        weight_lap(k).start()
    half = gate_half_ref.shape[1]
    others = pl.ds(pl.multiple_of((1 - core) * half, 128), half)
    swaps = [
        remote(gate_ref.at[:, others], gate_half_ref, swap_send.at[0], swap_recv.at[0], sibling),
        remote(up_ref.at[:, others], up_half_ref, swap_send.at[1], swap_recv.at[1], sibling),
    ]
    for swap in swaps:
        swap.start()

    def part_copy(k):
        return remote(part.at[rows_of(k)], parts.at[k], part_send.at[k], part_recv.at[k], x_peer(k))

    for k in (1, 3, 2):
        norm_copy(k).wait_recv()
    for k in (1, 3):
        weight_lap(k).wait_recv()
    for k in (1, 3):
        out_weight_copy(k).start()

    @pl.loop(0, cols // 256)
    def _(tile):
        at = pl.ds(pl.multiple_of(tile * 256, 256), 256)
        total = jnp.dot(
            blocks[0].reshape(group, feats),
            weight[pl.ds(0, feats), at],
            preferred_element_type=jnp.float32,
        )
        total += jnp.dot(
            blocks[1].reshape(group, feats),
            weight[pl.ds(feats, feats), at],
            preferred_element_type=jnp.float32,
        )
        part[:, at] = total.astype(jnp.bfloat16)
        share_ref[:, at] = total[0:rows]

    for k in (1, 3, 2):
        part_copy(k).start()
    for k in (1, 3, 2):
        part_copy(k).wait_recv()
        share_ref[:, 0:cols] += parts[k].astype(jnp.float32)

    def turned(at):
        head = share_ref[:, at : at + HEAD_DIM]
        swapped = pltpu.roll(head, HEAD_DIM // 2, 1)
        return (head * cosine_ref[...] + swapped * sine_ref[...]).astype(jnp.bfloat16)

    mine = rows_of(c)
    key_value[mine, 0:HEAD_DIM] = turned(q_cols)
    at = q_cols + kv_cols
    key_value[mine, HEAD_DIM : 2 * HEAD_DIM] = share_ref[:, at : at + HEAD_DIM].astype(jnp.bfloat16)

    def kv_copy(k, who, device):
        return remote(
            key_value.at[rows_of(who)],
            key_value.at[rows_of(who)],
            kv_send.at[k],
            kv_recv.at[who],
            device,
        )

    for k in range(1, 16):
        kv_copy(k, c, (behind(c, k), m)).start()

    queries = jnp.concatenate([turned(h * HEAD_DIM) for h in range(heads)], axis=0)

    for k in range(1, 16):
        kv_copy(k, ahead(c, k), sibling).wait_recv()
    for k in (1, 3):
        out_weight_copy(k).wait_recv()
        out_weight_lap(k).start()

    keys = 16 * rows
    scores = lax.dot_general(
        queries,
        key_value[:, 0:HEAD_DIM],
        (((1,), (1,)), ((), ())),
        preferred_element_type=jnp.float32,
    ) * (HEAD_DIM ** (-0.5))
    query_at = lax.broadcasted_iota(jnp.int32, (heads * rows, 1), 0) % rows * 16 + c
    key_at = lax.broadcasted_iota(jnp.int32, (1, keys), 1)
    allowed = key_at % rows * 16 + key_at // rows <= query_at
    scores = jnp.where(allowed, scores, -1e30)
    weights = jnp.exp(scores - jnp.max(scores, axis=1, keepdims=True))
    weights = jnp.where(allowed, weights, 0.0)
    total = jnp.sum(weights, axis=1, keepdims=True)
    mixed = (
        jnp.dot(
            weights.astype(jnp.bfloat16),
            key_value[:, HEAD_DIM : 2 * HEAD_DIM],
            preferred_element_type=jnp.float32,
        )
        / total
    ).astype(jnp.bfloat16)
    for h in range(heads):
        attended[0:rows, h * HEAD_DIM : (h + 1) * HEAD_DIM] = mixed[h * rows : (h + 1) * rows]

    def att_copy(k):
        to = lax.rem(x + 4 - k, 4)
        return remote(
            attended.at[0:rows],
            attended.at[rows_of(k)],
            att_send.at[k],
            att_recv.at[k],
            (to * 4 + y, m),
        )

    for k in (1, 3, 2):
        att_copy(k).start()

    def out_copy(k, side):
        return remote(
            delta.at[side, rows_of(k)],
            deltas.at[m],
            out_send.at[2 * k + side],
            out_recv.at[m],
            (lax.rem(x + k, 4) * 4 + y, 2 * x + side),
        )

    def out_in(slot):
        return remote(
            delta.at[0, pl.ds(0, rows)],
            deltas.at[slot],
            out_send.at[slot],
            out_recv.at[slot],
            sibling,
        )

    for k in (1, 3):
        out_weight_lap(k).wait_recv()
    for k in (1, 3, 2):
        att_copy(k).wait_recv()
    for side in range(2):
        for at in range(2):
            delta[side, :, at * width : (at + 1) * width] = jnp.dot(
                attended[...], out_weight[2 * side + at], preferred_element_type=jnp.float32
            ).astype(jnp.bfloat16)
        for k in (2, 1, 3):
            out_copy(k, side).start()

        @pl.when(jnp.logical_not(is_home & (side == core)))
        def _():
            out_copy(0, side).start()

    @pl.when(is_home)
    def _():
        deltas[m] = delta[core, 0:rows, :]

    share_ref[...] = jnp.zeros_like(share_ref)

    @pl.loop(0, 8)
    def _(k):
        slot = lax.rem(k + m, 8)

        @pl.when(jnp.logical_not(is_home & (slot == m)))
        def _():
            out_in(slot).wait_recv()

        share_ref[...] += deltas[slot].astype(jnp.float32)

    mixed = full[m].astype(jnp.float32) + share_ref[...]
    scaled_ref[...] = (mixed * gains_ref[16:17, :]).astype(jnp.bfloat16)

    for k in range(1, 4):
        row_copy(k, m).wait_send()
    for k in range(4):
        hop(z_block(k)).wait_send()

    for swap in swaps:
        swap.wait()

    for k in (1, 3):
        weight_copy(k).wait_send()
        weight_lap(k).wait_send()
        out_weight_copy(k).wait_send()
        out_weight_lap(k).wait_send()
    for side in range(2):
        for k in range(1, 4):
            out_copy(k, side).wait_send()

        @pl.when(jnp.logical_not(is_home & (side == core)))
        def _():
            out_copy(0, side).wait_send()

    for k in range(1, 4):
        norm_copy(k).wait_send()
        part_copy(k).wait_send()
        att_copy(k).wait_send()
    for k in range(1, 16):
        box_copy(k).wait_send()
        kv_copy(k, c, sibling).wait_send()


def attend(
    tokens, destination, kept_row, kept_column, gains, query, key, value, out_weight, gate, up, cosine, sine
):
    count, slots = kept_column.shape[0], 16 * BOX
    feats = tokens.shape[1]
    width = query.shape[0]
    cols = query.shape[1] + key.shape[1] + value.shape[1]
    dma = pltpu.SemaphoreType.DMA
    bf16 = jnp.bfloat16
    vmem, anywhere = pl.BlockSpec(memory_space=pltpu.VMEM), pl.BlockSpec(memory_space=pl.ANY)
    return pl.pallas_call(
        attend_kernel,
        out_shape=(
            jax.ShapeDtypeStruct((count, feats), jnp.float32),
            jax.ShapeDtypeStruct((count, feats), bf16),
            jax.ShapeDtypeStruct((count, 128), jnp.float32),
            jax.ShapeDtypeStruct((gate.shape[0], gate.shape[1] // 2), bf16),
            jax.ShapeDtypeStruct((up.shape[0], up.shape[1] // 2), bf16),
        ),
        in_specs=[vmem] * 5 + [anywhere] * 6 + [vmem] * 2,
        out_specs=(vmem, vmem, vmem, anywhere, anywhere),
        scratch_shapes=[
            pltpu.VMEM((slots, feats), bf16),
            pltpu.VMEM((slots, feats), bf16),
            pltpu.VMEM((8, count, feats), bf16),
            pltpu.VMEM((8, count, feats), bf16),
            pltpu.VMEM((2, 4, count, feats), bf16),
            pltpu.VMEM((4 * width, cols), bf16),
            pltpu.VMEM((4, *out_weight.shape), bf16),
            pltpu.VMEM((4 * count, cols), bf16),
            pltpu.VMEM((4, count, cols), bf16),
            pltpu.VMEM((16 * count, 2 * HEAD_DIM), bf16),
            pltpu.VMEM((4 * count, query.shape[1]), bf16),
            pltpu.VMEM((2, 4 * count, feats), bf16),
            pltpu.VMEM((8, count, feats), bf16),
            dma((4,)),
            dma((2,)),
            dma((2,)),
        ]
        + [dma((16,))] * 18,
        compiler_params=pltpu.CompilerParams(
            collective_id=2, has_side_effects=True, vmem_limit_bytes=VMEM_BYTES
        ),
        name="attend",
    )(
        tokens,
        destination,
        kept_row,
        kept_column,
        gains,
        query,
        key,
        value,
        out_weight,
        gate,
        up,
        cosine,
        sine,
    )


def body(
    tokens,
    norm_gain,
    router_weight,
    query_weight,
    key_weight,
    value_weight,
    out_weight,
    mlp_gain,
    gate_weight,
    up_weight,
    down_weight,
    destination,
    kept_pos,
):
    tok_dev, feature_cols = tokens.shape
    kept_dev = kept_pos.shape[0]
    half_dim = HEAD_DIM // 2
    exponent = jnp.arange(half_dim, dtype=jnp.float32) * (2.0 / HEAD_DIM)
    angles = kept_pos.astype(jnp.float32)[:, None] * (500000.0 ** (-exponent))[None, :]
    cosine, sine = jnp.cos(angles), jnp.sin(angles)
    gains = jnp.concatenate(
        [
            norm_gain.reshape(8, feature_cols),
            router_weight.reshape(8, feature_cols),
            jnp.broadcast_to(mlp_gain, (8, feature_cols)),
        ]
    ).astype(jnp.float32)
    destinations = jnp.broadcast_to(destination, (8, tok_dev))
    kept_row = jnp.broadcast_to(kept_pos, (8, kept_dev))
    kept_column = jnp.broadcast_to(kept_pos[:, None], (kept_dev, 128))
    head_share, scaled, score, gate_half, up_half = attend(
        tokens,
        destinations,
        kept_row,
        kept_column,
        gains,
        query_weight,
        key_weight,
        value_weight,
        out_weight,
        gate_weight,
        up_weight,
        jnp.concatenate([cosine, cosine], axis=1),
        jnp.concatenate([-sine, sine], axis=1),
    )
    arrived = feed_forward(
        scaled,
        head_share,
        score,
        kept_row,
        kept_column,
        destinations,
        gains,
        gate_weight,
        up_weight,
        gate_half,
        up_half,
        down_weight,
    )
    return (tokens.astype(jnp.float32) + arrived.astype(jnp.float32)).astype(jnp.bfloat16)


def solution(mesh):
    in_specs = (
        P("ctx", "mp"),
        P(),
        P(),
        P("ctx", "mp"),
        P("ctx", "mp"),
        P("ctx", "mp"),
        P("mp", "ctx"),
        P("mp"),
        P("mp", "ctx"),
        P("mp", "ctx"),
        P("ctx", "mp"),
        P("ctx"),
        P("ctx"),
    )
    out_specs = P("ctx", "mp")
    return jax.shard_map(body, mesh=mesh, in_specs=in_specs, out_specs=out_specs, check_vma=False)
```

```python
import jax
import jax.numpy as jnp
from jax import lax
from jax.sharding import PartitionSpec as P

from jax.experimental import pallas as pl
from jax.experimental.pallas import tpu as pltpu

HEAD_DIM = 128
BOX = 16
VMEM_BYTES = 60 * 2**20
MESH = pl.DeviceIdType.MESH
OFFSETS = (
    (0, 0), (0, 1), (1, 0), (0, 3), (3, 0), (0, 2), (2, 0), (1, 1),
    (3, 3), (1, 3), (3, 1), (1, 2), (2, 1), (3, 2), (2, 3), (2, 2),
)
EPS = 1e-05


def ahead(c, k):
    dx, dy = OFFSETS[k]
    return lax.rem(c // 4 + dx, 4) * 4 + lax.rem(c % 4 + dy, 4)


def behind(c, k):
    dx, dy = OFFSETS[k]
    return lax.rem(c // 4 + 4 - dx, 4) * 4 + lax.rem(c % 4 + 4 - dy, 4)


def send_slots(destination, kept):
    owner, slot = destination // kept, destination % kept
    going = destination >= 0
    order = jnp.where(going, slot * 16 + owner, 16 * kept)
    first = (jnp.min(order) - owner + 15) // 16
    return jnp.where(going, owner * BOX + slot - first, 16 * BOX)


def take_slots(row, column, shard, axis):
    kept = row.shape[1]
    same = column // shard == row // shard
    at = lax.broadcasted_iota(jnp.int32, (kept, kept), axis)
    first = jnp.min(jnp.where(same, at, kept), axis=axis, keepdims=True)
    mine = row if axis == 0 else column
    return mine // shard * BOX + lax.broadcasted_iota(jnp.int32, mine.shape, 1 - axis) - first


def remote(source, target, sent, landed, device):
    return pltpu.make_async_remote_copy(
        src_ref=source,
        dst_ref=target,
        send_sem=sent,
        recv_sem=landed,
        device_id=device,
        device_id_type=MESH,
    )


def mlp_kernel(
    x_ref,
    share_ref,
    score_ref,
    kept_row_ref,
    kept_column_ref,
    destination_ref,
    gains_ref,
    gate_ref,
    up_ref,
    gate_half_ref,
    up_half_ref,
    down_ref,
    out_ref,
    own_x,
    sib_x,
    own_gain,
    sib_gain,
    weight,
    down,
    part,
    relayed,
    joined,
    sums,
    hidden,
    delta,
    deltas,
    total_ref,
    outbox,
    inbox,
    load_sem,
    swap_send,
    swap_recv,
    x_send,
    x_recv,
    half_send,
    half_recv,
    pass_send,
    pass_recv,
    far_send,
    far_recv,
    sum_send,
    sum_recv,
    join_send,
    join_recv,
    hid_send,
    hid_recv,
    lap_send,
    lap_recv,
    hop_send,
    hop_recv,
    out_send,
    out_recv,
    box_send,
    box_recv,
):
    rows, feats = x_ref.shape
    slots = outbox.shape[0]
    box = slots // 16
    half = gate_ref.shape[1] // 2
    both = 2 * half
    group = 4 * rows
    c, m = lax.axis_index("ctx"), lax.axis_index("mp")
    x, y = c // 4, c % 4
    z, core = m // 2, m % 2
    sibling = (c, z * 2 + 1 - core)

    def z_peer(step):
        return lax.rem(z + step, 4)

    barrier = pltpu.get_barrier_semaphore()

    for k in range(1, 16):
        pl.semaphore_signal(barrier, inc=1, device_id=(ahead(c, k), m), device_id_type=MESH)

    for k in (1, 3):
        pl.semaphore_signal(
            barrier, inc=1, device_id=(c, z_peer(k) * 2 + core), device_id_type=MESH
        )
    pl.semaphore_signal(barrier, inc=1, device_id=sibling, device_id_type=MESH)

    mine = pl.multiple_of(core * half, 128)
    loads = [
        pltpu.make_async_copy(
            gate_ref.at[:, pl.ds(mine, half)],
            weight.at[pl.ds(0, feats), pl.ds(0, half)],
            load_sem.at[0],
        ),
        pltpu.make_async_copy(
            up_ref.at[:, pl.ds(mine, half)],
            weight.at[pl.ds(0, feats), pl.ds(half, half)],
            load_sem.at[1],
        ),
        pltpu.make_async_copy(
            gate_half_ref, weight.at[pl.ds(feats, feats), pl.ds(0, half)], load_sem.at[2]
        ),
        pltpu.make_async_copy(
            up_half_ref, weight.at[pl.ds(feats, feats), pl.ds(half, half)], load_sem.at[3]
        ),
        pltpu.make_async_copy(down_ref, down, load_sem.at[4]),
    ]
    for load in loads:
        load.start()
    own_x[0:rows, :] = x_ref[...]
    own_gain[...] = 1.0 / gains_ref[16:24, :]
    pl.semaphore_wait(barrier, 18)

    def x_copy(k):
        place = pl.ds(k * rows, rows)
        return remote(x_ref, own_x.at[place], x_send.at[k], x_recv.at[k], (behind(c, k), m))

    def x_in(slot):
        place = pl.ds(pl.multiple_of(slot * rows, rows), rows)
        return remote(x_ref, own_x.at[place], x_send.at[slot], x_recv.at[slot], sibling)

    def x_pass(who):
        place = pl.ds(pl.multiple_of(who * rows, rows), rows)
        return remote(
            own_x.at[place], sib_x.at[place], pass_send.at[who], pass_recv.at[who], sibling
        )

    short = rows // 2

    def half_copy(dx, dy, side):
        slot = OFFSETS.index((dx, dy))
        source = OFFSETS.index((0, dy) if side else (dx, 0))
        to = lax.rem(x + 4 - dx, 4) * 4 + y if side else x * 4 + lax.rem(y + 4 - dy, 4)
        return remote(
            own_x.at[pl.ds(source * rows + side * short, short)],
            own_x.at[pl.ds(slot * rows + side * short, short)],
            half_send.at[side * 16 + slot],
            half_recv.at[side * 16 + slot],
            (to, m),
        )

    def half_in(slot, side):
        start = pl.multiple_of(slot * rows + side * short, short)
        return remote(
            own_x.at[pl.ds(0, short)],
            own_x.at[pl.ds(start, short)],
            half_send.at[0],
            half_recv.at[side * 16 + slot],
            sibling,
        )

    def halves(slot):
        dx, dy = OFFSETS[slot]
        if dx:
            return [half_copy(dx, k, 0) for k in range(1, 4)]
        return [half_copy(k, dy, 1) for k in range(1, 4)]

    for k in range(1, 7):
        x_copy(k).start()
    gain_swap = remote(own_gain, sib_gain, swap_send.at[0], swap_recv.at[0], sibling)
    x_pass(0).start()
    gain_swap.start()

    def near(way):
        return z_peer(1 + 2 * way)

    def chip(way):
        return (c, near(way) * 2 + core)

    def piece(turn, to, side):
        return part.at[turn, pl.ds(pl.multiple_of(to * rows + side * short, short), short)]

    def far_copy(turn, way):
        at = turn * 2 + way
        return remote(
            piece(turn, z_peer(2), way),
            relayed.at[turn, way],
            far_send.at[at],
            far_recv.at[at],
            chip(way),
        )

    def sum_copy(turn, way):
        at = turn * 2 + way
        return remote(
            piece(turn, near(way), 1 - way),
            sums.at[turn, way, pl.ds((1 - way) * short, short)],
            sum_send.at[at],
            sum_recv.at[at],
            chip(way),
        )

    def join_copy(turn, way):
        at = turn * 2 + way
        return remote(
            joined.at[turn, way],
            sums.at[turn, way, pl.ds(way * short, short)],
            join_send.at[at],
            join_recv.at[at],
            chip(way),
        )

    def hid_copy(turn, way, slot):
        at = turn * 2 + way
        return remote(
            hidden.at[turn, core, slot],
            hidden.at[turn, core, slot],
            hid_send.at[at],
            hid_recv.at[at],
            chip(way),
        )

    def lap_copy(turn, way, slot):
        at = turn * 2 + way
        there = hidden.at[turn, core, slot, pl.ds(way * short, short)]
        return remote(there, there, lap_send.at[at], lap_recv.at[at], chip(way))

    def hid_pass(turn, at):
        return remote(
            hidden.at[turn, core, at],
            hidden.at[turn, core, at],
            hop_send.at[turn * 4 + at],
            hop_recv.at[turn * 4 + at],
            sibling,
        )

    def hid_passed(turn, at):
        return remote(
            hidden.at[turn, 1 - core, at],
            hidden.at[turn, 1 - core, at],
            hop_send.at[turn * 4 + at],
            hop_recv.at[turn * 4 + at],
            sibling,
        )

    def out_copy(slot, who):
        return remote(
            delta.at[pl.ds(pl.multiple_of(slot * rows, rows), rows)],
            deltas.at[slot],
            out_send.at[slot],
            out_recv.at[slot],
            (who, m),
        )

    def out_in(slot):
        return remote(
            delta.at[pl.ds(0, rows)], deltas.at[slot], out_send.at[slot], out_recv.at[slot], sibling
        )

    def front(turn):
        @pl.loop(0, 4)
        def _(k):
            slot = turn * 4 + k

            @pl.when((slot > 0) & (slot < 7))
            def _():
                x_in(slot).wait_recv()

            @pl.when(slot >= 7)
            def _():
                half_in(slot, 0).wait_recv()
                half_in(slot, 1).wait_recv()

            @pl.when(slot > 0)
            def _():
                x_pass(slot).start()

        for t in range(2):

            @pl.when(turn == t)
            def _():
                for slot in range(3 * t + 1, 3 * t + 4):
                    for copy in halves(slot):
                        copy.start()

        @pl.when(turn == 0)
        def _():
            for load in loads:
                load.wait()
            gain_swap.wait()

        @pl.loop(0, 4)
        def _(k):
            x_pass(turn * 4 + k).wait_recv()

        place = pl.ds(pl.multiple_of(turn * group, group), group)
        mixed = own_x[place, :].astype(jnp.float32) * own_gain[0:1, :]
        square = jnp.sum(mixed * mixed, axis=1, keepdims=True)
        mixed = sib_x[place, :].astype(jnp.float32) * sib_gain[0:1, :]
        square = square + jnp.sum(mixed * mixed, axis=1, keepdims=True)
        square = jnp.broadcast_to(square, (group, 128))
        coarse = square.astype(jnp.bfloat16)
        fine = (square - coarse.astype(jnp.float32)).astype(jnp.bfloat16)
        lane = lax.broadcasted_iota(jnp.int32, (group, 128), 1)
        part[turn, :, pl.ds(both, 128)] = jnp.where(lane < 64, coarse, fine)

        @pl.loop(0, both // 256)
        def _(tile):
            cols = pl.ds(pl.multiple_of(tile * 256, 256), 256)
            total = jnp.dot(
                own_x[place, :], weight[pl.ds(0, feats), cols], preferred_element_type=jnp.float32
            )
            total += jnp.dot(
                sib_x[place, :],
                weight[pl.ds(feats, feats), cols],
                preferred_element_type=jnp.float32,
            )
            part[turn, :, cols] = total.astype(jnp.bfloat16)

        for way in range(2):
            far_copy(turn, way).start()
        for way in range(2):
            sum_copy(turn, way).start()

    def relay(turn):
        for way in range(2):
            far_copy(turn, way).wait_recv()
            joined[turn, way] = (
                piece(turn, near(way), way)[...].astype(jnp.float32)
                + relayed[turn, way].astype(jnp.float32)
            ).astype(jnp.bfloat16)
            join_copy(turn, way).start()

    def middle(turn):
        total = part[turn, pl.ds(pl.multiple_of(z * rows, rows), rows), :].astype(jnp.float32)
        for way in range(2):
            sum_copy(turn, way).wait_recv()
            join_copy(turn, way).wait_recv()
            total += sums[turn, way].astype(jnp.float32)
        square = total[:, both : both + 1] + total[:, both + 64 : both + 65]
        scale = lax.rsqrt(square * (1.0 / (8 * feats)) + EPS)
        gate = total[:, :half] * scale
        up = total[:, half:both] * scale
        hidden[turn, core, z] = (gate / (1.0 + jnp.exp(-gate)) * up).astype(jnp.bfloat16)
        for way in range(2):
            hid_copy(turn, way, z).start()
        hid_pass(turn, z).start()

    def lap(turn):
        for way in range(2):
            slot = near(1 - way)
            hid_copy(turn, way, slot).wait_recv()
            lap_copy(turn, way, slot).start()
            hid_pass(turn, slot).start()

    def back(turn):
        for way in range(2):
            lap_copy(turn, way, z_peer(2)).wait_recv()
        hid_pass(turn, z_peer(2)).start()
        for k in range(4):
            hid_passed(turn, z_peer(k)).wait_recv()
        place = pl.ds(pl.multiple_of(turn * group, group), group)

        @pl.loop(0, feats // 256)
        def _(tile):
            cols = pl.ds(pl.multiple_of(tile * 256, 256), 256)
            total = jnp.dot(
                hidden[turn, 0].reshape(group, half),
                down[pl.ds(0, half), cols],
                preferred_element_type=jnp.float32,
            )
            total += jnp.dot(
                hidden[turn, 1].reshape(group, half),
                down[pl.ds(half, half), cols],
                preferred_element_type=jnp.float32,
            )
            delta[place, cols] = total.astype(jnp.bfloat16)

        for k in range(4):
            dx, dy = 0, 0
            for t in range(4):
                dx = jnp.where(turn == t, OFFSETS[4 * t + k][0], dx)
                dy = jnp.where(turn == t, OFFSETS[4 * t + k][1], dy)
            who = lax.rem(x + dx, 4) * 4 + lax.rem(y + dy, 4)
            if k > 0:
                out_copy(turn * 4 + k, who).start()
            else:

                @pl.when(turn > 0)
                def _():
                    out_copy(turn * 4, who).start()

    @pl.loop(0, 8)
    def _(step):
        for late, stage in enumerate((front, relay, middle, lap, back)):

            @pl.when((step >= late) & (step < late + 4))
            def _():
                stage(step - late)

    total_ref[...] = share_ref[...] + delta[0:rows, :].astype(jnp.float32)

    @pl.loop(1, 16)
    def _(k):
        out_in(k).wait_recv()
        total_ref[...] += deltas[k].astype(jnp.float32)

    update = (score_ref[:, 0:1] * total_ref[...]).astype(jnp.bfloat16)
    slot_at = lax.broadcasted_iota(jnp.int32, (slots, rows), 0)
    shard = destination_ref.shape[1]
    taken = take_slots(kept_row_ref[0:1, :], kept_column_ref[:, 0:1], shard, 0)
    give = jnp.where(slot_at == taken, 1.0, 0.0).astype(jnp.bfloat16)
    outbox[...] = jnp.dot(give, update, preferred_element_type=jnp.float32).astype(jnp.bfloat16)

    def box_of(who):
        return pl.ds(pl.multiple_of(who * box, box), box)

    def box_copy(k):
        who = ahead(c, k)
        return remote(
            outbox.at[box_of(who)], inbox.at[box_of(c)], box_send.at[k], box_recv.at[c], (who, m)
        )

    def box_in(who):
        return remote(
            outbox.at[box_of(who)], inbox.at[box_of(who)], box_send.at[0], box_recv.at[who], sibling
        )

    for k in range(1, 16):
        box_copy(k).start()

    inbox[box_of(c), :] = outbox[box_of(c), :]
    slot_at = lax.broadcasted_iota(jnp.int32, (slots, shard), 0)
    sent = send_slots(destination_ref[0:1, :], rows)
    back_to = jnp.where(slot_at == sent, 1.0, 0.0).T.astype(jnp.bfloat16)

    for k in range(1, 16):
        box_in(ahead(c, k)).wait_recv()

    @pl.loop(0, feats // 256)
    def _(tile):
        cols = pl.ds(pl.multiple_of(tile * 256, 256), 256)
        out_ref[:, cols] = jnp.dot(
            back_to, inbox[:, cols], preferred_element_type=jnp.float32
        ).astype(jnp.bfloat16)

    for k in range(1, 7):
        x_copy(k).wait_send()
        for copy in halves(k):
            copy.wait_send()
    for k in range(1, 16):
        out_in(k).wait_send()
        box_copy(k).wait_send()

    @pl.loop(0, 16)
    def _(who):
        x_pass(who).wait_send()

    @pl.loop(0, 4)
    def _(turn):
        for way in range(2):
            far_copy(turn, way).wait_send()
            sum_copy(turn, way).wait_send()
            join_copy(turn, way).wait_send()
            hid_copy(turn, way, z).wait_send()
            lap_copy(turn, way, near(1 - way)).wait_send()
        for k in range(4):
            hid_pass(turn, z_peer(k)).wait_send()


def feed_forward(
    scaled,
    share,
    score,
    kept_row,
    kept_column,
    destination,
    gains,
    gate_weight,
    up_weight,
    gate_half,
    up_half,
    down_weight,
):
    rows, feats = scaled.shape
    cols = gate_weight.shape[1]
    half = cols // 2
    dma = pltpu.SemaphoreType.DMA
    bf16 = jnp.bfloat16
    vmem, anywhere = pl.BlockSpec(memory_space=pltpu.VMEM), pl.BlockSpec(memory_space=pl.ANY)
    return pl.pallas_call(
        mlp_kernel,
        out_shape=jax.ShapeDtypeStruct((destination.shape[1], feats), bf16),
        in_specs=[vmem] * 7 + [anywhere] * 5,
        out_specs=vmem,
        scratch_shapes=[
            pltpu.VMEM((16 * rows, feats), bf16),
            pltpu.VMEM((16 * rows, feats), bf16),
            pltpu.VMEM((8, feats), jnp.float32),
            pltpu.VMEM((8, feats), jnp.float32),
            pltpu.VMEM((2 * feats, cols), bf16),
            pltpu.VMEM((cols, feats), bf16),
            pltpu.VMEM((4, 4 * rows, cols + 128), bf16),
            pltpu.VMEM((4, 2, rows // 2, cols + 128), bf16),
            pltpu.VMEM((4, 2, rows // 2, cols + 128), bf16),
            pltpu.VMEM((4, 2, rows, cols + 128), bf16),
            pltpu.VMEM((4, 2, 4, rows, half), bf16),
            pltpu.VMEM((16 * rows, feats), bf16),
            pltpu.VMEM((16, rows, feats), bf16),
            pltpu.VMEM((rows, feats), jnp.float32),
            pltpu.VMEM((16 * BOX, feats), bf16),
            pltpu.VMEM((16 * BOX, feats), bf16),
            dma((5,)),
            dma((1,)),
            dma((1,)),
            dma((16,)),
            dma((16,)),
            dma((32,)),
            dma((32,)),
        ]
        + [dma((16,))] * 18,
        compiler_params=pltpu.CompilerParams(
            collective_id=3, has_side_effects=True, vmem_limit_bytes=VMEM_BYTES
        ),
        name="feed_forward",
    )(
        scaled,
        share,
        score,
        kept_row,
        kept_column,
        destination,
        gains,
        gate_weight,
        up_weight,
        gate_half,
        up_half,
        down_weight,
    )


def attend_kernel(
    tokens_ref,
    destination_ref,
    kept_row_ref,
    kept_column_ref,
    gains_ref,
    query_ref,
    key_ref,
    value_ref,
    out_weight_ref,
    gate_ref,
    up_ref,
    cosine_ref,
    sine_ref,
    share_ref,
    scaled_ref,
    score_ref,
    gate_half_ref,
    up_half_ref,
    outbox,
    inbox,
    full,
    normed,
    blocks,
    weight,
    out_weight,
    part,
    parts,
    key_value,
    attended,
    delta,
    deltas,
    load_sem,
    swap_send,
    swap_recv,
    box_send,
    box_recv,
    row_send,
    row_recv,
    hop_send,
    hop_recv,
    norm_send,
    norm_recv,
    wide_send,
    wide_recv,
    part_send,
    part_recv,
    kv_send,
    kv_recv,
    att_send,
    att_recv,
    out_send,
    out_recv,
):
    rows, feats = share_ref.shape
    width = query_ref.shape[0]
    slots = outbox.shape[0]
    box = slots // 16
    group = 4 * rows
    cols = weight.shape[1]
    q_cols, kv_cols = query_ref.shape[1], key_ref.shape[1]
    heads = q_cols // HEAD_DIM
    c, m = lax.axis_index("ctx"), lax.axis_index("mp")
    x, y = c // 4, c % 4
    z, core = m // 2, m % 2
    sibling = (c, z * 2 + 1 - core)

    def rows_of(who, count=1):
        return pl.ds(pl.multiple_of(who * (rows * count), rows), rows * count)

    is_home = x == z
    barrier = pltpu.get_barrier_semaphore()

    def x_peer(k):
        return (lax.rem(x + k, 4) * 4 + y, m)

    def y_peer(k):
        return (x * 4 + lax.rem(y + k, 4), m)

    @pl.loop(0, 8)
    def _(k):
        @pl.when(jnp.logical_not(is_home & (k == m)))
        def _():
            pl.semaphore_signal(barrier, inc=1, device_id=(z * 4 + y, k), device_id_type=MESH)

    for k in range(1, 16):
        pl.semaphore_signal(barrier, inc=1, device_id=(ahead(c, k), m), device_id_type=MESH)
    for k in range(1, 4):
        pl.semaphore_signal(
            barrier,
            inc=1,
            device_id=(c, lax.rem(z + k, 4) * 2 + core),
            device_id_type=MESH,
        )
    pl.semaphore_signal(barrier, inc=1, device_id=sibling, device_id_type=MESH)

    band = pl.ds(pl.multiple_of(y * width, width), width)
    loads = [
        pltpu.make_async_copy(query_ref, weight.at[band, pl.ds(0, q_cols)], load_sem.at[0]),
        pltpu.make_async_copy(key_ref, weight.at[band, pl.ds(q_cols, kv_cols)], load_sem.at[1]),
        pltpu.make_async_copy(
            value_ref, weight.at[band, pl.ds(q_cols + kv_cols, kv_cols)], load_sem.at[2]
        ),
        pltpu.make_async_copy(out_weight_ref, out_weight.at[y], load_sem.at[3]),
    ]
    for load in loads:
        load.start()

    slot_at = lax.broadcasted_iota(jnp.int32, (slots, tokens_ref.shape[0]), 0)
    sent = send_slots(destination_ref[0:1, :], rows)
    pick = jnp.where(slot_at == sent, 1.0, 0.0).astype(jnp.bfloat16)

    @pl.loop(0, feats // 256)
    def _(tile):
        cols = pl.ds(pl.multiple_of(tile * 256, 256), 256)
        outbox[:, cols] = jnp.dot(
            pick, tokens_ref[:, cols], preferred_element_type=jnp.float32
        ).astype(jnp.bfloat16)

    def box_of(who):
        return pl.ds(pl.multiple_of(who * box, box), box)

    inbox[box_of(c), :] = outbox[box_of(c), :]
    pl.semaphore_wait(barrier, jnp.where(is_home, 26, 27))

    def box_copy(k):
        who = ahead(c, k)
        return remote(
            outbox.at[box_of(who)], inbox.at[box_of(c)], box_send.at[k], box_recv.at[c], (who, m)
        )

    def box_in(who):
        return remote(
            outbox.at[box_of(who)], inbox.at[box_of(who)], box_send.at[0], box_recv.at[who], sibling
        )

    def weight_copy(k):
        return remote(
            weight.at[band], weight.at[band], wide_send.at[k], wide_recv.at[k], y_peer(k)
        )

    def out_weight_copy(k):
        return remote(
            out_weight.at[y],
            out_weight.at[y],
            wide_send.at[4 + k],
            wide_recv.at[4 + k],
            y_peer(k),
        )

    def weight_lap(k):
        whose = lax.rem(y + 4 - k, 4)
        start = whose * width + (k // 2) * (width // 2)
        there = weight.at[pl.ds(pl.multiple_of(start, width // 2), width // 2)]
        return remote(there, there, wide_send.at[k - 1], wide_recv.at[k - 1], y_peer(k))

    def out_weight_lap(k):
        whose = lax.rem(y + 4 - k, 4)
        there = out_weight.at[whose, pl.ds((k // 2) * (width // 2), width // 2)]
        return remote(there, there, wide_send.at[k + 3], wide_recv.at[k + 3], y_peer(k))

    for k in range(1, 16):
        box_copy(k).start()
    for load in loads:
        load.wait()
    for k in (1, 3):
        weight_copy(k).start()
    for k in range(1, 16):
        box_in(ahead(c, k)).wait_recv()

    slot_at = lax.broadcasted_iota(jnp.int32, (rows, slots), 1)
    taken = take_slots(kept_row_ref[0:1, :], kept_column_ref[:, 0:1], tokens_ref.shape[0], 1)
    take = jnp.where(slot_at == taken, 1.0, 0.0).astype(jnp.bfloat16)
    full[m] = jnp.dot(take, inbox[...], preferred_element_type=jnp.float32).astype(jnp.bfloat16)

    def row_copy(k, who):
        return remote(
            full.at[who],
            full.at[who],
            row_send.at[k],
            row_recv.at[who],
            (c, lax.rem(z + k, 4) * 2 + core),
        )

    def hop(who):
        return remote(full.at[who], full.at[who], hop_send.at[who], hop_recv.at[who], sibling)

    def z_block(k):
        return lax.rem(z + k, 4) * 2 + core

    def z_sibling(k):
        return lax.rem(z + k, 4) * 2 + 1 - core

    for k in (2, 1, 3):
        row_copy(k, m).start()
    hop(m).start()
    for k in (1, 3, 2):
        row_copy(k, z_block(k)).wait_recv()
        hop(z_block(k)).start()
    for k in (0, 1, 3, 2):
        hop(z_sibling(k)).wait_recv()

    square, route = 0.0, 0.0
    for at in range(8):
        wide = full[at].astype(jnp.float32)
        square += jnp.sum(wide * wide, axis=1, keepdims=True)
        route += jnp.sum(wide * gains_ref[8 + at : 9 + at, :], axis=1, keepdims=True)
    scale = lax.rsqrt(square * (1.0 / (8 * feats)) + EPS)
    score_ref[...] = jnp.broadcast_to(1.0 / (1.0 + jnp.exp(-route)), score_ref.shape)
    for at in range(8):
        wide = full[at].astype(jnp.float32) * scale * gains_ref[at : at + 1, :]
        wide = wide.astype(jnp.bfloat16)
        normed[at] = wide

    def norm_copy(k):
        to = lax.rem(x + 4 - k, 4)
        return remote(
            normed.at[pl.ds(2 * to, 2)],
            blocks.at[:, k],
            norm_send.at[k],
            norm_recv.at[k],
            (to * 4 + y, m),
        )

    for k in (1, 3, 2):
        norm_copy(k).start()
    blocks[0, 0] = normed[2 * x]
    blocks[1, 0] = normed[2 * x + 1]
    for k in (1, 3):
        weight_copy(k).wait_recv()
        weight_lap(k).start()
    for k in (1, 3):
        out_weight_copy(k).start()
    half = gate_half_ref.shape[1]
    others = pl.ds(pl.multiple_of((1 - core) * half, 128), half)
    swaps = [
        remote(gate_ref.at[:, others], gate_half_ref, swap_send.at[0], swap_recv.at[0], sibling),
        remote(up_ref.at[:, others], up_half_ref, swap_send.at[1], swap_recv.at[1], sibling),
    ]
    for swap in swaps:
        swap.start()

    def part_copy(k):
        return remote(part.at[rows_of(k)], parts.at[k], part_send.at[k], part_recv.at[k], x_peer(k))

    for k in (1, 3, 2):
        norm_copy(k).wait_recv()
    for k in (1, 3):
        weight_lap(k).wait_recv()

    @pl.loop(0, cols // 256)
    def _(tile):
        at = pl.ds(pl.multiple_of(tile * 256, 256), 256)
        total = jnp.dot(
            blocks[0].reshape(group, feats),
            weight[pl.ds(0, feats), at],
            preferred_element_type=jnp.float32,
        )
        total += jnp.dot(
            blocks[1].reshape(group, feats),
            weight[pl.ds(feats, feats), at],
            preferred_element_type=jnp.float32,
        )
        part[:, at] = total.astype(jnp.bfloat16)
        share_ref[:, at] = total[0:rows]

    for k in (1, 3, 2):
        part_copy(k).start()
    for k in (1, 3, 2):
        part_copy(k).wait_recv()
        share_ref[:, 0:cols] += parts[k].astype(jnp.float32)

    def turned(at):
        head = share_ref[:, at : at + HEAD_DIM]
        swapped = pltpu.roll(head, HEAD_DIM // 2, 1)
        return (head * cosine_ref[...] + swapped * sine_ref[...]).astype(jnp.bfloat16)

    mine = rows_of(c)
    key_value[mine, 0:HEAD_DIM] = turned(q_cols)
    at = q_cols + kv_cols
    key_value[mine, HEAD_DIM : 2 * HEAD_DIM] = share_ref[:, at : at + HEAD_DIM].astype(jnp.bfloat16)

    def kv_copy(k, who, device):
        return remote(
            key_value.at[rows_of(who)],
            key_value.at[rows_of(who)],
            kv_send.at[k],
            kv_recv.at[who],
            device,
        )

    for k in range(1, 16):
        kv_copy(k, c, (behind(c, k), m)).start()

    queries = jnp.concatenate([turned(h * HEAD_DIM) for h in range(heads)], axis=0)

    for k in range(1, 16):
        kv_copy(k, ahead(c, k), sibling).wait_recv()
    for k in (1, 3):
        out_weight_copy(k).wait_recv()
        out_weight_lap(k).start()

    keys = 16 * rows
    scores = lax.dot_general(
        queries,
        key_value[:, 0:HEAD_DIM],
        (((1,), (1,)), ((), ())),
        preferred_element_type=jnp.float32,
    ) * (HEAD_DIM ** (-0.5))
    query_at = lax.broadcasted_iota(jnp.int32, (heads * rows, 1), 0) % rows * 16 + c
    key_at = lax.broadcasted_iota(jnp.int32, (1, keys), 1)
    allowed = key_at % rows * 16 + key_at // rows <= query_at
    scores = jnp.where(allowed, scores, -1e30)
    weights = jnp.exp(scores - jnp.max(scores, axis=1, keepdims=True))
    weights = jnp.where(allowed, weights, 0.0)
    total = jnp.sum(weights, axis=1, keepdims=True)
    mixed = (
        jnp.dot(
            weights.astype(jnp.bfloat16),
            key_value[:, HEAD_DIM : 2 * HEAD_DIM],
            preferred_element_type=jnp.float32,
        )
        / total
    ).astype(jnp.bfloat16)
    for h in range(heads):
        attended[0:rows, h * HEAD_DIM : (h + 1) * HEAD_DIM] = mixed[h * rows : (h + 1) * rows]

    def att_copy(k):
        to = lax.rem(x + 4 - k, 4)
        return remote(
            attended.at[0:rows],
            attended.at[rows_of(k)],
            att_send.at[k],
            att_recv.at[k],
            (to * 4 + y, m),
        )

    for k in (1, 3, 2):
        att_copy(k).start()

    def out_copy(k, side):
        return remote(
            delta.at[side, rows_of(k)],
            deltas.at[m],
            out_send.at[2 * k + side],
            out_recv.at[m],
            (lax.rem(x + k, 4) * 4 + y, 2 * x + side),
        )

    def out_in(slot):
        return remote(
            delta.at[0, pl.ds(0, rows)],
            deltas.at[slot],
            out_send.at[slot],
            out_recv.at[slot],
            sibling,
        )

    for k in (1, 3):
        out_weight_lap(k).wait_recv()
    for k in (1, 3, 2):
        att_copy(k).wait_recv()
    for side in range(2):
        for at in range(2):
            delta[side, :, at * width : (at + 1) * width] = jnp.dot(
                attended[...], out_weight[2 * side + at], preferred_element_type=jnp.float32
            ).astype(jnp.bfloat16)
        for k in (2, 1, 3):
            out_copy(k, side).start()

        @pl.when(jnp.logical_not(is_home & (side == core)))
        def _():
            out_copy(0, side).start()

    @pl.when(is_home)
    def _():
        deltas[m] = delta[core, 0:rows, :]

    share_ref[...] = jnp.zeros_like(share_ref)

    @pl.loop(0, 8)
    def _(k):
        slot = lax.rem(k + m, 8)

        @pl.when(jnp.logical_not(is_home & (slot == m)))
        def _():
            out_in(slot).wait_recv()

        share_ref[...] += deltas[slot].astype(jnp.float32)

    mixed = full[m].astype(jnp.float32) + share_ref[...]
    scaled_ref[...] = (mixed * gains_ref[16:17, :]).astype(jnp.bfloat16)

    for k in range(1, 4):
        row_copy(k, m).wait_send()
    for k in range(4):
        hop(z_block(k)).wait_send()

    for swap in swaps:
        swap.wait()

    for k in (1, 3):
        weight_copy(k).wait_send()
        weight_lap(k).wait_send()
        out_weight_copy(k).wait_send()
        out_weight_lap(k).wait_send()
    for side in range(2):
        for k in range(1, 4):
            out_copy(k, side).wait_send()

        @pl.when(jnp.logical_not(is_home & (side == core)))
        def _():
            out_copy(0, side).wait_send()

    for k in range(1, 4):
        norm_copy(k).wait_send()
        part_copy(k).wait_send()
        att_copy(k).wait_send()
    for k in range(1, 16):
        box_copy(k).wait_send()
        kv_copy(k, c, sibling).wait_send()


def attend(
    tokens, destination, kept_row, kept_column, gains, query, key, value, out_weight, gate, up, cosine, sine
):
    count, slots = kept_column.shape[0], 16 * BOX
    feats = tokens.shape[1]
    width = query.shape[0]
    cols = query.shape[1] + key.shape[1] + value.shape[1]
    dma = pltpu.SemaphoreType.DMA
    bf16 = jnp.bfloat16
    vmem, anywhere = pl.BlockSpec(memory_space=pltpu.VMEM), pl.BlockSpec(memory_space=pl.ANY)
    return pl.pallas_call(
        attend_kernel,
        out_shape=(
            jax.ShapeDtypeStruct((count, feats), jnp.float32),
            jax.ShapeDtypeStruct((count, feats), bf16),
            jax.ShapeDtypeStruct((count, 128), jnp.float32),
            jax.ShapeDtypeStruct((gate.shape[0], gate.shape[1] // 2), bf16),
            jax.ShapeDtypeStruct((up.shape[0], up.shape[1] // 2), bf16),
        ),
        in_specs=[vmem] * 5 + [anywhere] * 6 + [vmem] * 2,
        out_specs=(vmem, vmem, vmem, anywhere, anywhere),
        scratch_shapes=[
            pltpu.VMEM((slots, feats), bf16),
            pltpu.VMEM((slots, feats), bf16),
            pltpu.VMEM((8, count, feats), bf16),
            pltpu.VMEM((8, count, feats), bf16),
            pltpu.VMEM((2, 4, count, feats), bf16),
            pltpu.VMEM((4 * width, cols), bf16),
            pltpu.VMEM((4, *out_weight.shape), bf16),
            pltpu.VMEM((4 * count, cols), bf16),
            pltpu.VMEM((4, count, cols), bf16),
            pltpu.VMEM((16 * count, 2 * HEAD_DIM), bf16),
            pltpu.VMEM((4 * count, query.shape[1]), bf16),
            pltpu.VMEM((2, 4 * count, feats), bf16),
            pltpu.VMEM((8, count, feats), bf16),
            dma((4,)),
            dma((2,)),
            dma((2,)),
        ]
        + [dma((16,))] * 18,
        compiler_params=pltpu.CompilerParams(
            collective_id=2, has_side_effects=True, vmem_limit_bytes=VMEM_BYTES
        ),
        name="attend",
    )(
        tokens,
        destination,
        kept_row,
        kept_column,
        gains,
        query,
        key,
        value,
        out_weight,
        gate,
        up,
        cosine,
        sine,
    )


def body(
    tokens,
    norm_gain,
    router_weight,
    query_weight,
    key_weight,
    value_weight,
    out_weight,
    mlp_gain,
    gate_weight,
    up_weight,
    down_weight,
    destination,
    kept_pos,
):
    tok_dev, feature_cols = tokens.shape
    kept_dev = kept_pos.shape[0]
    half_dim = HEAD_DIM // 2
    exponent = jnp.arange(half_dim, dtype=jnp.float32) * (2.0 / HEAD_DIM)
    angles = kept_pos.astype(jnp.float32)[:, None] * (500000.0 ** (-exponent))[None, :]
    cosine, sine = jnp.cos(angles), jnp.sin(angles)
    gains = jnp.concatenate(
        [
            norm_gain.reshape(8, feature_cols),
            router_weight.reshape(8, feature_cols),
            jnp.broadcast_to(mlp_gain, (8, feature_cols)),
        ]
    ).astype(jnp.float32)
    destinations = jnp.broadcast_to(destination, (8, tok_dev))
    kept_row = jnp.broadcast_to(kept_pos, (8, kept_dev))
    kept_column = jnp.broadcast_to(kept_pos[:, None], (kept_dev, 128))
    head_share, scaled, score, gate_half, up_half = attend(
        tokens,
        destinations,
        kept_row,
        kept_column,
        gains,
        query_weight,
        key_weight,
        value_weight,
        out_weight,
        gate_weight,
        up_weight,
        jnp.concatenate([cosine, cosine], axis=1),
        jnp.concatenate([-sine, sine], axis=1),
    )
    arrived = feed_forward(
        scaled,
        head_share,
        score,
        kept_row,
        kept_column,
        destinations,
        gains,
        gate_weight,
        up_weight,
        gate_half,
        up_half,
        down_weight,
    )
    return (tokens.astype(jnp.float32) + arrived.astype(jnp.float32)).astype(jnp.bfloat16)


def solution(mesh):
    in_specs = (
        P("ctx", "mp"),
        P(),
        P(),
        P("ctx", "mp"),
        P("ctx", "mp"),
        P("ctx", "mp"),
        P("mp", "ctx"),
        P("mp"),
        P("mp", "ctx"),
        P("mp", "ctx"),
        P("ctx", "mp"),
        P("ctx"),
        P("ctx"),
    )
    out_specs = P("ctx", "mp")
    return jax.shard_map(body, mesh=mesh, in_specs=in_specs, out_specs=out_specs, check_vma=False)
```
